32 devices in a mesh: seq: 4 (over y, x), ret: 8 (over z, core).
Axes of the slice: x: 2, y: 2, z: 4, core: 2. Of those that a mesh axis runs over, the one named last changes fastest.
Arguments:
- queries: bfloat16 [3072, 4096], P('seq', 'ret'), may hold values from -4 to 4
- grad_ctx: bfloat16 [3072, 4096], P('seq', 'ret'), may hold values from -6 to 6
- neighbours: bfloat16 [64, 128, 896], P(('seq', 'ret')), may hold values from -6 to 6
- up_weight: bfloat16 [896, 3584], replicated, may hold values from -0.1875 to 0.1875
- down_weight: bfloat16 [3584, 896], replicated, may hold values from -0.09375 to 0.09375
- key_weight: bfloat16 [896, 4096], P(None, 'ret'), may hold values from -0.1875 to 0.1875
- value_weight: bfloat16 [896, 4096], P(None, 'ret'), may hold values from -0.1875 to 0.1875
- group_ids: int32 [48, 2], P('seq'), may hold values from 0 to 3, all different within a row; in each aligned block of 12 rows (0 to 11, 12 to 23, ...) at most 8 rows name the same one
- slot_ids: int32 [48, 2], P('seq'), may hold values from 0 to 15
Outputs:
- context: bfloat16 [3072, 4096], P('seq', 'ret')
- grad_queries: bfloat16 [3072, 4096], P('seq', 'ret')
- grad_encoded: bfloat16 [64, 128, 896], P(('seq', 'ret'))
- grad_key_weight: float32 [896, 4096], P('seq', 'ret')
- grad_value_weight: float32 [896, 4096], P('seq', 'ret')
The draws below stay inside these ranges and needn't reach their ends.
Inputs may be any that keep to these rules, and one draw needn't show every extreme that they name: `group_ids`: the two neighbours of a span lie on different indices of seq. Among the spans of one index of seq no index of seq is named more than 8 times, and in every draw some index of seq is named exactly 8 times by the spans of some index of seq.
All inputs are finite; a program needn't handle non-finite values.
Results may differ from the reference program's by a relative error of at most 0.018.
Values may be sent and summed in bfloat16 or wider, within the bound.
No kernel may reach another device: no remote copies, remote signals or barrier semaphores. Data moves between devices by JAX's collectives and lax.ppermute only.
A program may use at most 192 MiB of HBM per device.

```python
import math
import jax
import jax.numpy as jnp
import numpy as np
from jax import lax

HEADS = 32
HD = 128
DE = 896
FFE = 3584
SPAN = 64
RLEN = 128
TOK_SEQ = 768
NB_DEV = 2
TOKENS = 3072
CH_G = 12
SPANS = 48
CAP = 8
NB_SEQ = 16
NEIGH = 64
HB = 4
N_SEQ = 4
N_RET = 8


def set_ends(values, key, smallest, high):
    longest = values.shape.index(max(values.shape))
    spots = []
    for shift in (0, 1):
        where = [jax.random.randint(jax.random.fold_in(key, axis), (), 0, length) for axis, length in enumerate(values.shape)]
        where[longest] = (where[longest] + shift) % values.shape[longest]
        spots.append(tuple(where))
    return values.at[spots[0]].set(smallest).at[spots[1]].set(high)


def block_scale(own_key, extent, pieces, least, largest):
    def one(dim, shards_of):
        steps = jax.random.uniform(jax.random.fold_in(jax.random.fold_in(own_key, 6), dim), (shards_of,), jnp.float32, least / len(pieces), largest / len(pieces))
        return jnp.repeat(jnp.exp(steps), extent[dim] // shards_of).reshape((-1,) + (1,) * (len(extent) - dim - 1))

    gain = one(*pieces[0])
    for cut in pieces[1:]:
        gain = gain * one(*cut)
    return gain


def shared_out(key, own, number, rows, count, top, limit, skew):
    sequence = jax.random.permutation(key, count)
    heavy_load, ordinary = load_shares(count, rows * top, limit, skew, True), load_shares(count, rows * top, limit, skew, False)
    places = jnp.arange(count)

    def named(lengths, rotation):
        used = int((lengths > 0).sum())
        fixed = max(1, used // 4)
        passed = fixed + (places - fixed + rotation * (used - fixed)) % max(1, count - fixed)
        return jnp.zeros((count,), jnp.int32).at[sequence[jnp.where(places < fixed, places, passed)]].set(jnp.asarray(lengths, jnp.int32))

    lengths = jnp.where(number % 4 == 0, named(heavy_load, number // 4), named(ordinary, number - number // 4 - 1))
    mixed = jax.random.permutation(jax.random.fold_in(own, 3), count)
    giver, receiver = mixed[0:count // 2 * 2:2], mixed[1:count // 2 * 2:2]
    slack = jnp.minimum(lengths[giver] - 1, limit - lengths[receiver]) // 2
    slack = jnp.where((giver == sequence[0]) | (receiver == sequence[0]) | (lengths[receiver] == 0), 0, jnp.maximum(slack, 0))
    passed = jax.random.randint(jax.random.fold_in(own, 4), (count // 2,), 0, 1 << 20) % (slack + 1)
    lengths = lengths.at[giver].add(-passed).at[receiver].add(passed)
    members = jnp.searchsorted(jnp.cumsum(lengths), jnp.arange(rows * top), side="right").astype(jnp.int32)
    table = members.reshape(top, rows).T
    table = table[jax.random.permutation(jax.random.fold_in(own, 1), rows)]
    rotation = jax.random.randint(jax.random.fold_in(own, 2), (rows, 1), 0, top)
    return jnp.take_along_axis(table, (jnp.arange(top)[None, :] + rotation) % top, axis=1)


def load_shares(count, total, reach, slope, full):
    weights = [(1 << 20) // math.isqrt(grade ** slope) + 1 for grade in range(1, count + 1)]
    largest = reach if full else min(reach, max(-(-total // count), total * weights[0] // sum(weights)))
    least = 1 if total - largest >= count - 1 else 0
    given, spare = [largest] + [least] * (count - 1), total - largest - least * (count - 1)
    while spare > 0:
        movable = [i for i in range(1, count) if given[i] < largest] or [i for i in range(1, count) if given[i] < reach]
        pool, budget = sum([weights[i] for i in movable]), spare
        for i in movable:
            addition = min(reach - given[i], max(1, budget * weights[i] // pool), spare)
            given[i] = given[i] + addition
            spare = spare - addition
    return np.array(given)


def normal_values(key, shape, width, reach, pieces=(), held_as=jnp.bfloat16):
    factor_of = block_scale(key, shape, pieces, -0.22, 0.18) if pieces else 1.0
    drawn = jax.random.normal(key, shape, jnp.float32) * width * factor_of
    return jnp.minimum(jnp.maximum(drawn, -reach), reach).astype(held_as)


def setup_inputs(seed: int = 0) -> dict:
    seeds = jax.random.split(jax.random.key(seed), 10)
    queries = normal_values(seeds[0], (TOKENS, HEADS * HD), 1.0, 4.0, ((0, 4), (1, 8)))
    grad_ctx = normal_values(seeds[1], (TOKENS, HEADS * HD), 1.0, 6.0, ((0, 4), (1, 8)))
    neighbours = normal_values(seeds[2], (NEIGH, RLEN, DE), 1.0, 6.0, ((0, 32),))
    up_weight = normal_values(seeds[3], (DE, FFE), DE ** -0.5, 0.1875)
    down_weight = normal_values(seeds[4], (FFE, DE), FFE ** -0.5, 0.09375)
    key_weight = normal_values(seeds[5], (DE, HEADS * HD), DE ** -0.5, 0.1875, ((1, 8),))
    value_weight = normal_values(seeds[6], (DE, HEADS * HD), DE ** -0.5, 0.1875, ((1, 8),))
    group_ids_keys = jax.random.split(jax.random.fold_in(seeds[7], 1), SPANS // CH_G)
    group_ids_turns = jax.random.permutation(jax.random.fold_in(seeds[7], 3), SPANS // CH_G)
    group_ids = jax.vmap(lambda own, number: shared_out(jax.random.fold_in(seeds[7], 2), own, number, CH_G, N_SEQ, 2, CAP, 2))(group_ids_keys, group_ids_turns).reshape((SPANS, 2))
    slot_ids = set_ends(jax.random.randint(seeds[8], (SPANS, 2), 0, NB_SEQ), jax.random.fold_in(seeds[8], 1), 0, NB_SEQ - 1).astype(jnp.int32)
    return dict(queries=queries, grad_ctx=grad_ctx, neighbours=neighbours, up_weight=up_weight, down_weight=down_weight, key_weight=key_weight, value_weight=value_weight, group_ids=group_ids, slot_ids=slot_ids)


def encode(raw_block, up_weight, down_weight):
    amount, row_len, feat_width = raw_block.shape
    inputs = raw_block.reshape(-1, feat_width).astype(jnp.float32)
    normed = (inputs * lax.rsqrt(lax.optimization_barrier(jnp.mean(inputs * inputs, axis=-1, keepdims=True)) + 1e-06)).astype(jnp.bfloat16)
    hidden = jax.nn.gelu(jnp.dot(normed, up_weight, preferred_element_type=jnp.float32)).astype(jnp.bfloat16)
    output = inputs + jnp.dot(hidden, down_weight, preferred_element_type=jnp.float32)
    return output.astype(jnp.bfloat16).reshape(amount, row_len, feat_width)

def attend(queries, key_req, value_req, grad_out):
    score_scale = 1.0 / math.sqrt(queries.shape[-1])
    query_f = queries.astype(jnp.float32)
    key_f = key_req.astype(jnp.float32)
    value_f = value_req.astype(jnp.float32)
    grad_f = grad_out.astype(jnp.float32)
    scores = jnp.einsum('cqhd,ckhd->chqk', query_f, key_f) * score_scale
    weights = jnp.exp(scores)
    weights = weights / lax.optimization_barrier(jnp.sum(weights, axis=-1, keepdims=True))
    probs = weights.astype(jnp.bfloat16)
    probs_f = probs.astype(jnp.float32)
    context = jnp.einsum('chqk,ckhd->cqhd', probs_f, value_f).astype(jnp.bfloat16)
    grad_probs = jnp.einsum('cqhd,ckhd->chqk', grad_f, value_f)
    mixed = (weights * (grad_probs - lax.optimization_barrier(jnp.sum(weights * grad_probs, axis=-1, keepdims=True))) * score_scale).astype(jnp.bfloat16)
    mixed_f = mixed.astype(jnp.float32)
    grad_queries = jnp.einsum('chqk,ckhd->cqhd', mixed_f, key_f).astype(jnp.bfloat16)
    grad_keys = jnp.einsum('chqk,cqhd->ckhd', mixed_f, query_f).astype(jnp.bfloat16)
    grad_values = jnp.einsum('chqk,cqhd->ckhd', probs_f, grad_f).astype(jnp.bfloat16)
    return (context, grad_queries, grad_keys, grad_values)

def reference(queries, grad_ctx, neighbours, up_weight, down_weight, key_weight, value_weight, group_ids, slot_ids):
    encoded = lax.map(lambda raw_block: encode(raw_block, up_weight, down_weight), neighbours.reshape(N_SEQ * N_RET, NB_DEV, RLEN, DE)).reshape(NEIGH, RLEN, DE)
    request_rows = (group_ids * NB_SEQ + slot_ids).astype(jnp.int32).reshape(-1)
    head_width = HB * HD
    requests = 2 * CH_G
    shape_q = (CH_G, SPAN, HB, HD)
    shape_kv = (CH_G, 2 * RLEN, HB, HD)
    grad_total = jnp.zeros((NEIGH, RLEN, DE), jnp.float32)
    contexts = []
    grad_qs = []
    key_grads = []
    value_grads = []
    for block_idx in range(N_RET):
        columns = slice(block_idx * head_width, (block_idx + 1) * head_width)
        key_block = key_weight[:, columns]
        value_block = value_weight[:, columns]
        query_block = queries[:, columns]
        grad_block = grad_ctx[:, columns]

        def one_group(carry, group_idx):
            grad_table, key_acc, value_acc = carry
            row_start = (group_idx * TOK_SEQ).astype(jnp.int32)
            query_rows = lax.dynamic_slice_in_dim(query_block, row_start, TOK_SEQ, 0)
            grad_rows = lax.dynamic_slice_in_dim(grad_block, row_start, TOK_SEQ, 0)
            wanted = lax.dynamic_slice_in_dim(request_rows, (group_idx * requests).astype(jnp.int32), requests, 0)
            picked = jnp.take(encoded, wanted, axis=0).reshape(-1, DE)
            key_flat = jnp.dot(picked, key_block, preferred_element_type=jnp.float32).astype(jnp.bfloat16)
            value_flat = jnp.dot(picked, value_block, preferred_element_type=jnp.float32).astype(jnp.bfloat16)
            context, grad_query, grad_keys, grad_values = attend(query_rows.reshape(shape_q), key_flat.reshape(shape_kv), value_flat.reshape(shape_kv), grad_rows.reshape(shape_q))
            grad_keys = grad_keys.reshape(-1, head_width)
            grad_values = grad_values.reshape(-1, head_width)
            key_acc = key_acc + jnp.dot(picked.astype(jnp.float32).T, grad_keys.astype(jnp.float32))
            value_acc = value_acc + jnp.dot(picked.astype(jnp.float32).T, grad_values.astype(jnp.float32))
            grad_part = (jnp.dot(grad_keys, key_block.T, preferred_element_type=jnp.float32) + jnp.dot(grad_values, value_block.T, preferred_element_type=jnp.float32)).astype(jnp.bfloat16)
            grad_table = grad_table.at[wanted].add(grad_part.reshape(requests, RLEN, DE).astype(jnp.float32))
            return ((grad_table, key_acc, value_acc), (context.reshape(TOK_SEQ, head_width), grad_query.reshape(TOK_SEQ, head_width)))
        start = (grad_total, jnp.zeros((DE, head_width), jnp.float32), jnp.zeros((DE, head_width), jnp.float32))
        (grad_total, key_acc, value_acc), (context, grad_query) = lax.scan(one_group, start, jnp.arange(N_SEQ, dtype=jnp.int32))
        contexts.append(context)
        grad_qs.append(grad_query)
        key_grads.append(key_acc)
        value_grads.append(value_acc)
    context_all = jnp.stack(contexts, axis=2).reshape(TOKENS, HEADS * HD)
    grad_q_all = jnp.stack(grad_qs, axis=2).reshape(TOKENS, HEADS * HD)
    return (context_all, grad_q_all, grad_total.astype(jnp.bfloat16), jnp.concatenate(key_grads, axis=1), jnp.concatenate(value_grads, axis=1))
```

```python
import functools
import math

import jax
import jax.numpy as jnp
from jax import lax
from jax.experimental import pallas as pl
from jax.experimental.pallas import tpu as pltpu
from jax.sharding import PartitionSpec as P

HD = 128
VMEM_BYTES = 48 * 1024 * 1024
NT = (((1,), (1,)), ((), ()))
NN = (((1,), (0,)), ((), ()))


def params():
    return pltpu.CompilerParams(vmem_limit_bytes=VMEM_BYTES)


def vmem():
    return pl.BlockSpec(memory_space=pltpu.VMEM)


def smem():
    return pl.BlockSpec(memory_space=pltpu.SMEM)


def mm(a, b, dims):
    return lax.dot_general(a, b, dims, preferred_element_type=jnp.float32)


def encode(raw_block, up_weight, down_weight):
    amount, row_len, feat_width = raw_block.shape
    inputs = raw_block.reshape(-1, feat_width).astype(jnp.float32)
    normed = (inputs * lax.rsqrt(jnp.mean(inputs * inputs, axis=-1, keepdims=True) + 1e-06)).astype(
        jnp.bfloat16
    )
    hidden = jax.nn.gelu(jnp.dot(normed, up_weight, preferred_element_type=jnp.float32)).astype(
        jnp.bfloat16
    )
    output = inputs + jnp.dot(hidden, down_weight, preferred_element_type=jnp.float32)
    return output.astype(jnp.bfloat16).reshape(amount, row_len, feat_width)


def ranks_of(targets):
    count = targets.shape[-1]
    same = targets[..., :, None] == targets[..., None, :]
    earlier = jnp.arange(count)[:, None] > jnp.arange(count)[None, :]
    return jnp.sum((same & earlier).astype(jnp.int32), axis=-1)


def dispatch_kernel(span_of, q_ref, g_ref, out_ref):
    slots, _, span_len, _ = out_ref.shape

    def step(j, carry):
        row = pl.multiple_of(span_of[j] * span_len, span_len)
        out_ref[j, 0] = q_ref[pl.ds(row, span_len), :]
        out_ref[j, 1] = g_ref[pl.ds(row, span_len), :]
        return carry

    lax.fori_loop(0, slots, step, 0)


def dispatch(span_of, queries, grad_ctx, span_len):
    slots = span_of.shape[0]
    width = queries.shape[1]
    return pl.pallas_call(
        dispatch_kernel,
        out_shape=jax.ShapeDtypeStruct((slots, 2, span_len, width), jnp.bfloat16),
        in_specs=[smem(), vmem(), vmem()],
        out_specs=vmem(),
        compiler_params=params(),
        cost_estimate=pl.CostEstimate(
            flops=0, bytes_accessed=slots * span_len * width * 6, transcendentals=0
        ),
        name="dispatch",
    )(span_of, queries, grad_ctx)


def combine_kernel(position, back_ref, ctx_ref, gq_ref):
    span_len = back_ref.shape[2]
    spans = ctx_ref.shape[0] // span_len

    def step(c, carry):
        first, second = position[2 * c], position[2 * c + 1]
        rows = pl.ds(pl.multiple_of(c * span_len, span_len), span_len)
        for which, out in ((0, ctx_ref), (1, gq_ref)):
            total = back_ref[first, which].astype(jnp.float32) + back_ref[second, which].astype(
                jnp.float32
            )
            out[rows, :] = total.astype(out.dtype)
        return carry

    lax.fori_loop(0, spans, step, 0)


def combine(position, back, rows):
    width = back.shape[3]
    return pl.pallas_call(
        combine_kernel,
        out_shape=[jax.ShapeDtypeStruct((rows, width), jnp.bfloat16)] * 2,
        in_specs=[smem(), vmem()],
        out_specs=[vmem(), vmem()],
        compiler_params=params(),
        cost_estimate=pl.CostEstimate(
            flops=rows * width * 2, bytes_accessed=back.size * 2 + rows * width * 4, transcendentals=0
        ),
        name="combine",
    )(position, back)


def fill_diagonal(dst, block, heads, span_len):
    for h in range(heads):
        dst[h * span_len : (h + 1) * span_len, h * HD : (h + 1) * HD] = block[:, h * HD : (h + 1) * HD]


def slot_scores(kv_ref, nbr, q_diag, g_diag, row_len, width, scale):
    rows = pl.ds(pl.multiple_of(nbr * row_len, row_len), row_len)
    keys = kv_ref[rows, :width]
    values = kv_ref[rows, width:]
    expo = jnp.exp(mm(keys, q_diag[...], NT) * scale)
    grad_probs = mm(values, g_diag[...], NT)
    return rows, keys, values, expo, grad_probs


def stats_kernel(row_len, scale, nbrs, valid, qg_ref, kv_ref, stats_ref, *diag):
    slots, _, span_len, width = qg_ref.shape
    heads = width // HD
    for ref in diag:
        ref[...] = jnp.zeros_like(ref)

    def step(pair, carry):
        @pl.when(valid[2 * pair] + valid[2 * pair + 1] > 0)
        def _():
            for u in range(2):
                j = 2 * pair + u
                fill_diagonal(diag[2 * u], qg_ref[j, 0], heads, span_len)
                fill_diagonal(diag[2 * u + 1], qg_ref[j, 1], heads, span_len)
                _, _, _, expo, grad_probs = slot_scores(
                    kv_ref, nbrs[j], diag[2 * u], diag[2 * u + 1], row_len, width, scale
                )
                total = jnp.sum(expo, axis=0, keepdims=True)
                probs = expo / jnp.where(total > 0.0, total, 1.0)
                stats_ref[j, 0:1, :] = total
                stats_ref[j, 1:2, :] = jnp.sum(probs * grad_probs, axis=0, keepdims=True)

        return carry

    lax.fori_loop(0, slots // 2, step, 0)


def slot_stats(nbrs, valid, qg, kv, row_len, scale):
    slots, _, span_len, width = qg.shape
    lanes = span_len * (width // HD)
    return pl.pallas_call(
        functools.partial(stats_kernel, row_len, scale),
        out_shape=jax.ShapeDtypeStruct((slots, 2, lanes), jnp.float32),
        in_specs=[smem(), smem(), vmem(), vmem()],
        out_specs=vmem(),
        scratch_shapes=[pltpu.VMEM((lanes, width), jnp.bfloat16)] * 4,
        compiler_params=params(),
        cost_estimate=pl.CostEstimate(
            flops=slots * 4 * row_len * lanes * width,
            bytes_accessed=qg.size * 2 + kv.size * 2,
            transcendentals=slots * row_len * lanes,
        ),
        name="slot_stats",
    )(nbrs, valid, qg, kv)


def attend_kernel(
    row_len, scale, nbrs, valid, partner, qg_ref, kv_ref, own_ref, all_ref, back_ref, dkv_ref, acc, *diag
):
    slots, _, span_len, width = qg_ref.shape
    heads = width // HD
    for ref in diag:
        ref[...] = jnp.zeros_like(ref)
    acc[...] = jnp.zeros_like(acc)

    def step(pair, carry):
        @pl.when(valid[2 * pair] + valid[2 * pair + 1] > 0)
        def _():
            for u in range(2):
                j = 2 * pair + u
                q_diag, g_diag = diag[2 * u], diag[2 * u + 1]
                fill_diagonal(q_diag, qg_ref[j, 0], heads, span_len)
                fill_diagonal(g_diag, qg_ref[j, 1], heads, span_len)
                rows, keys, values, expo, grad_probs = slot_scores(
                    kv_ref, nbrs[j], q_diag, g_diag, row_len, width, scale
                )
                own = own_ref[j]
                other = all_ref[partner[j]]
                total = own[0:1] + other[0:1]
                total = jnp.where(total > 0.0, total, 1.0)
                shift = (own[0:1] / total) * own[1:2] + (other[0:1] / total) * other[1:2]
                live = valid[j] > 0
                weights = expo / total
                mixed = weights * (grad_probs - shift) * scale
                weights = jnp.where(live, weights, 0.0)
                mixed = jnp.where(live, mixed, 0.0)
                probs_n = weights.T.astype(jnp.bfloat16)
                mixed_n = mixed.T.astype(jnp.bfloat16)
                for h in range(heads):
                    part = slice(h * span_len, (h + 1) * span_len)
                    cols = slice(h * HD, (h + 1) * HD)
                    back_ref[j, 0, :, cols] = mm(probs_n[part], values[:, cols], NN).astype(jnp.bfloat16)
                    back_ref[j, 1, :, cols] = mm(mixed_n[part], keys[:, cols], NN).astype(jnp.bfloat16)
                acc[rows, :width] += mm(mixed.astype(jnp.bfloat16), q_diag[...], NN)
                acc[rows, width:] += mm(weights.astype(jnp.bfloat16), g_diag[...], NN)

        return carry

    lax.fori_loop(0, slots // 2, step, 0)
    dkv_ref[...] = acc[...].astype(jnp.bfloat16)


def attend(nbrs, valid, partner, qg, kv, own, everyone, row_len, scale):
    slots, _, span_len, width = qg.shape
    lanes = span_len * (width // HD)
    return pl.pallas_call(
        functools.partial(attend_kernel, row_len, scale),
        out_shape=[
            jax.ShapeDtypeStruct(qg.shape, jnp.bfloat16),
            jax.ShapeDtypeStruct(kv.shape, jnp.bfloat16),
        ],
        in_specs=[smem()] * 3 + [vmem()] * 4,
        out_specs=[vmem(), vmem()],
        scratch_shapes=[pltpu.VMEM(kv.shape, jnp.float32)]
        + [pltpu.VMEM((lanes, width), jnp.bfloat16)] * 4,
        compiler_params=params(),
        cost_estimate=pl.CostEstimate(
            flops=slots * 12 * row_len * lanes * width,
            bytes_accessed=qg.size * 4 + kv.size * 4,
            transcendentals=slots * row_len * lanes,
        ),
        name="attend",
    )(nbrs, valid, partner, qg, kv, own, everyone)


def body(
    queries,
    grad_ctx,
    neighbours,
    up_weight,
    down_weight,
    key_weight,
    value_weight,
    group_ids,
    slot_ids,
):
    groups = lax.axis_size("seq")
    me = lax.axis_index("seq")
    span_count = group_ids.shape[0]
    capacity = 2 * span_count // groups + 2
    slot_total = groups * capacity
    width = queries.shape[1]
    span_len = queries.shape[0] // span_count
    own_count, row_len, feat = neighbours.shape
    table_len = own_count * lax.axis_size("ret")
    scale = 1.0 / math.sqrt(HD)

    targets = group_ids.reshape(-1)
    position = targets * capacity + ranks_of(targets)
    request_ids = jnp.arange(2 * span_count, dtype=jnp.int32)
    taken = position[None, :] == jnp.arange(slot_total, dtype=jnp.int32)[:, None]
    span_of = jnp.sum(jnp.where(taken, request_ids[None, :] // 2, 0), axis=1)
    outgoing = dispatch(span_of, queries, grad_ctx, span_len)
    arrived = lax.all_to_all(
        outgoing.reshape(groups, capacity, 2, span_len, width),
        "seq",
        split_axis=0,
        concat_axis=0,
        tiled=True,
    ).reshape(slot_total, 2, span_len, width)

    codes = lax.all_gather(
        group_ids.reshape(-1) * table_len + slot_ids.reshape(-1), "seq", axis=0, tiled=False
    )
    all_targets, all_slots = codes // table_len, codes % table_len
    all_ranks = ranks_of(all_targets)
    sources = jnp.arange(groups, dtype=jnp.int32)[:, None]
    places = all_targets * slot_total + sources * capacity + all_ranks
    partners = jnp.flip(places.reshape(groups, span_count, 2), axis=2).reshape(groups, -1)
    holds = (all_targets == me)[:, None, :] & (
        all_ranks[:, None, :] == jnp.arange(capacity, dtype=jnp.int32)[None, :, None]
    )
    valid = jnp.sum(holds.astype(jnp.int32), axis=2).reshape(-1)
    nbrs = jnp.sum(jnp.where(holds, all_slots[:, None, :], 0), axis=2).reshape(-1)
    partner = jnp.sum(jnp.where(holds, partners[:, None, :], 0), axis=2).reshape(-1)

    encoded_own = encode(neighbours, up_weight, down_weight)
    table = lax.all_gather(encoded_own, "ret", axis=0, tiled=True).reshape(-1, feat)
    kv_weight = jnp.concatenate([key_weight, value_weight], axis=1)
    kv = jnp.dot(table, kv_weight, preferred_element_type=jnp.float32).astype(jnp.bfloat16)

    own_stats = slot_stats(nbrs, valid, arrived, kv, row_len, scale)
    all_stats = lax.all_gather(own_stats, "seq", axis=0, tiled=True)
    outgoing_back, grad_kv = attend(
        nbrs, valid, partner, arrived, kv, own_stats, all_stats, row_len, scale
    )
    back = lax.all_to_all(
        outgoing_back.reshape(groups, capacity, 2, span_len, width),
        "seq",
        split_axis=0,
        concat_axis=0,
        tiled=True,
    ).reshape(slot_total, 2, span_len, width)

    grad_table = mm(grad_kv, kv_weight, NT).astype(jnp.bfloat16)
    grad_encoded = lax.psum_scatter(
        grad_table.reshape(table_len, row_len, feat), "ret", scatter_dimension=0, tiled=True
    )
    grad_weight = mm(table, grad_kv, (((0,), (0,)), ((), ()))).astype(jnp.bfloat16)
    grad_weight = lax.psum_scatter(grad_weight, "seq", scatter_dimension=0, tiled=True)
    context, grad_query = combine(position, back, queries.shape[0])
    return (
        context,
        grad_query,
        grad_encoded,
        grad_weight[:, :width].astype(jnp.float32),
        grad_weight[:, width:].astype(jnp.float32),
    )


def solution(mesh):
    return jax.shard_map(
        body,
        mesh=mesh,
        in_specs=(
            P("seq", "ret"),
            P("seq", "ret"),
            P(("seq", "ret"), None, None),
            P(),
            P(),
            P(None, "ret"),
            P(None, "ret"),
            P("seq", None),
            P("seq", None),
        ),
        out_specs=(
            P("seq", "ret"),
            P("seq", "ret"),
            P(("seq", "ret"), None, None),
            P("seq", "ret"),
            P("seq", "ret"),
        ),
        check_vma=False,
    )
```

```python
import functools
import math

import jax
import jax.numpy as jnp
from jax import lax
from jax.experimental import pallas as pl
from jax.experimental.pallas import tpu as pltpu
from jax.sharding import PartitionSpec as P

HD = 128
NT = (((1,), (1,)), ((), ()))
NN = (((1,), (0,)), ((), ()))
TN = (((0,), (0,)), ((), ()))
BF16 = jnp.bfloat16
F32 = jnp.float32


def params(mib):
    return pltpu.CompilerParams(vmem_limit_bytes=mib * 1024 * 1024)


def vmem():
    return pl.BlockSpec(memory_space=pltpu.VMEM)


def anyspace():
    return pl.BlockSpec(memory_space=pl.ANY)


def smem():
    return pl.BlockSpec(memory_space=pltpu.SMEM)


def cost(flops, nbytes, trans=0):
    return pl.CostEstimate(flops=flops, bytes_accessed=nbytes, transcendentals=trans)


def mm(a, b, dims):
    return lax.dot_general(a, b, dims, preferred_element_type=F32)


def fetch(pairs, sems):
    copies = [pltpu.make_async_copy(src, dst, sems.at[i]) for i, (src, dst) in enumerate(pairs)]
    for copy in copies:
        copy.start()
    return copies


def encode_kernel(x_ref, up_ref, down_ref, out_ref, up, down, normed, acc, usem, dsem):
    steps, _, block = up.shape

    def copies(i):
        cols = pl.ds(pl.multiple_of(i * block, block), block)
        return (
            pltpu.make_async_copy(up_ref.at[:, cols], up.at[i], usem.at[i]),
            pltpu.make_async_copy(down_ref.at[cols, :], down.at[i], dsem.at[i]),
        )

    for i in range(steps):
        for copy in copies(i):
            copy.start()
    x = x_ref[...].astype(F32)
    normed[...] = (x * lax.rsqrt(jnp.mean(x * x, axis=-1, keepdims=True) + 1e-06)).astype(BF16)
    acc[...] = x

    def step(i, carry):
        up_in, down_in = copies(i)
        up_in.wait()
        h = mm(normed[...], up[i], NN)
        inner = math.sqrt(2.0 / math.pi) * (h + 0.044715 * (h * h * h))
        hidden = (0.5 * h * (1.0 + jnp.tanh(inner))).astype(BF16)
        down_in.wait()
        acc[...] += mm(hidden, down[i], NN)
        return carry

    lax.fori_loop(0, steps, step, 0)
    out_ref[...] = acc[...].astype(BF16)


def encode(neighbours, up_weight, down_weight):
    feat, hidden = up_weight.shape
    rows = neighbours.reshape(-1, feat)
    block = 512 if hidden % 512 == 0 else hidden
    steps = hidden // block
    return pl.pallas_call(
        encode_kernel,
        out_shape=jax.ShapeDtypeStruct(rows.shape, BF16),
        in_specs=[vmem(), anyspace(), anyspace()],
        out_specs=vmem(),
        scratch_shapes=[
            pltpu.VMEM((steps, feat, block), BF16),
            pltpu.VMEM((steps, block, feat), BF16),
            pltpu.VMEM(rows.shape, BF16),
            pltpu.VMEM(rows.shape, F32),
            pltpu.SemaphoreType.DMA((steps,)),
            pltpu.SemaphoreType.DMA((steps,)),
        ],
        compiler_params=params(56),
        cost_estimate=cost(4 * rows.shape[0] * feat * hidden, 4 * feat * hidden, rows.shape[0] * hidden),
        name="encode",
    )(rows, up_weight, down_weight).reshape(neighbours.shape)


def project_kernel(table_ref, kw_ref, vw_ref, kv_ref):
    width = kw_ref.shape[1]
    kv_ref[:, :width] = mm(table_ref[...], kw_ref[...], NN).astype(BF16)
    kv_ref[:, width:] = mm(table_ref[...], vw_ref[...], NN).astype(BF16)


def project(table, key_weight, value_weight):
    rows, feat = table.shape
    width = key_weight.shape[1]
    block = 512 if rows % 512 == 0 else rows
    return pl.pallas_call(
        project_kernel,
        grid=(rows // block,),
        out_shape=jax.ShapeDtypeStruct((rows, 2 * width), BF16),
        in_specs=[
            pl.BlockSpec((block, feat), lambda i: (i, 0)),
            pl.BlockSpec((feat, width), lambda i: (0, 0)),
            pl.BlockSpec((feat, width), lambda i: (0, 0)),
        ],
        out_specs=pl.BlockSpec((block, 2 * width), lambda i: (i, 0)),
        compiler_params=params(59),
        cost_estimate=cost(40 * rows * feat * width, rows * (feat + 2 * width) * 2),
        name="project",
    )(table, key_weight, value_weight)


def exchange(pieces, axis):
    size = len(pieces)
    return [pieces[0]] + [
        lax.ppermute(pieces[d], axis, [(s, s ^ d) for s in range(size)]) for d in range(1, size)
    ]


def signs_of(*arrays):
    return [lax.slice(a, (0,) * a.ndim, (1,) * (a.ndim - 1) + (8,)) for a in arrays]


def dispatch_kernel(waits, me, group_ids, q_ref, g_ref, *refs):
    out_refs, refs = refs[waits:-5], refs[-5:]
    position, place, taken, held, sems = refs
    groups, capacity, _, span_len, _ = held.shape
    for d in range(groups):
        taken[d] = 0

    def step(i, carry):
        span = i // 2
        offset = jnp.bitwise_xor(group_ids[span, i % 2], me[0])
        rank = taken[offset]
        taken[offset] = rank + 1
        position[i] = offset * capacity + rank
        place[i] = offset * groups * capacity + offset * capacity + rank
        rows = pl.ds(pl.multiple_of(span * span_len, span_len), span_len)
        held[offset, rank, 0] = q_ref[rows, :]
        held[offset, rank, 1] = g_ref[rows, :]
        return carry

    lax.fori_loop(0, position.shape[0], step, 0)
    for copy in fetch([(held.at[d], ref) for d, ref in enumerate(out_refs)], sems):
        copy.wait()


def dispatch(me, group_ids, queries, grad_ctx, groups, capacity, span_len, waits):
    width = queries.shape[1]
    requests = group_ids.size
    piece = (capacity, 2, span_len, width)
    outs = pl.pallas_call(
        functools.partial(dispatch_kernel, len(waits)),
        out_shape=[jax.ShapeDtypeStruct(piece, BF16)] * groups
        + [jax.ShapeDtypeStruct((requests,), jnp.int32)] * 2,
        in_specs=[smem(), smem(), vmem(), vmem()] + [anyspace()] * len(waits),
        out_specs=[anyspace()] * groups + [smem()] * 2,
        scratch_shapes=[
            pltpu.SMEM((groups,), jnp.int32),
            pltpu.VMEM((groups, *piece), BF16),
            pltpu.SemaphoreType.DMA((groups,)),
        ],
        compiler_params=params(56),
        cost_estimate=cost(0, groups * capacity * span_len * width * 6),
        name="dispatch",
    )(me, group_ids, queries, grad_ctx, *waits)
    return outs[:groups], outs[groups], outs[groups + 1]


def slots_kernel(groups, waits, capacity, table_len, me, *refs):
    codes, (counts, nbrs, partner, taken) = refs[:groups], refs[groups + waits :]
    slots = groups * capacity

    def clear(j, carry):
        nbrs[j] = 0
        partner[j] = 0
        return carry

    lax.fori_loop(0, slots, clear, 0)
    for d in range(groups):
        source = jnp.bitwise_xor(me[0], d)
        for h in range(groups):
            taken[h] = 0

        def step(span, carry, d=d, source=source):
            both = []
            for i in range(2):
                code = codes[d][0, 2 * span + i]
                target = code // table_len
                rank = taken[target]
                taken[target] = rank + 1
                there = jnp.bitwise_xor(target, source) * capacity + rank
                both.append((target, rank, code % table_len, there))
            for i in range(2):
                target, rank, nbr, _ = both[i]
                other, _, _, there = both[1 - i]

                @pl.when(target == me[0])
                def _():
                    nbrs[d * capacity + rank] = nbr
                    partner[d * capacity + rank] = jnp.bitwise_xor(other, me[0]) * slots + there

            return carry

        lax.fori_loop(0, codes[d].shape[1] // 2, step, 0)
        counts[d] = taken[me[0]]


def slot_lists(me, codes, capacity, table_len, waits):
    groups = len(codes)
    slots = groups * capacity
    return pl.pallas_call(
        functools.partial(slots_kernel, groups, len(waits), capacity, table_len),
        out_shape=[
            jax.ShapeDtypeStruct((groups,), jnp.int32),
            jax.ShapeDtypeStruct((slots,), jnp.int32),
            jax.ShapeDtypeStruct((slots,), jnp.int32),
        ],
        in_specs=[smem()] * (1 + groups) + [anyspace()] * len(waits),
        out_specs=[smem()] * 3,
        scratch_shapes=[pltpu.SMEM((groups,), jnp.int32)],
        compiler_params=params(56),
        cost_estimate=cost(0, slots * 16),
        name="slot_lists",
    )(me, *codes, *waits)


def gather_groups(refs, held):
    size = refs[0].shape[0]
    for d, ref in enumerate(refs):
        held[d * size : (d + 1) * size] = ref[...]


def combine_grad_kernel(groups, position, *refs):
    pieces, (out, held) = refs[:groups], refs[-2:]
    span_len = held.shape[1]
    gather_groups(pieces, held)

    def step(c, carry):
        rows = pl.ds(pl.multiple_of(c * span_len, span_len), span_len)
        first, second = held[position[2 * c]], held[position[2 * c + 1]]
        out[rows, :] = (first.astype(F32) + second.astype(F32)).astype(BF16)
        return carry

    lax.fori_loop(0, out.shape[0] // span_len, step, 0)


def combine_grad(position, pieces, rows, waits):
    groups = len(pieces)
    capacity, span_len, width = pieces[0].shape
    return pl.pallas_call(
        functools.partial(combine_grad_kernel, groups),
        out_shape=jax.ShapeDtypeStruct((rows, width), BF16),
        in_specs=[smem()] + [vmem()] * groups + [anyspace()] * len(waits),
        out_specs=vmem(),
        scratch_shapes=[pltpu.VMEM((groups * capacity, span_len, width), BF16)],
        compiler_params=params(16),
        cost_estimate=cost(rows * width * 250000, groups * pieces[0].size * 2 + rows * width * 2),
        name="combine_grad_queries",
    )(position, *pieces, *waits)


def combine_context_kernel(groups, position, place, *refs):
    pieces, stats = refs[:groups], refs[groups : 2 * groups]
    out, held, held_stats, shares = refs[2 * groups :]
    span_len, width = held.shape[1:]
    spans = out.shape[0] // span_len
    gather_groups(pieces, held)
    gather_groups(stats, held_stats)
    shares[...] = jnp.zeros_like(shares)
    for c in range(spans):
        first = held_stats[place[2 * c]][0:1]
        second = held_stats[place[2 * c + 1]][0:1]
        total = first + second
        shares[2 * c : 2 * c + 1, :] = first / total
        shares[2 * c + 1 : 2 * c + 2, :] = second / total
    columns = shares[...].T
    for c in range(spans):
        pair = [held[position[2 * c + i]] for i in range(2)]
        for h in range(width // HD):
            cols = slice(h * HD, (h + 1) * HD)
            part = columns[h * span_len : (h + 1) * span_len]
            total = sum(
                pair[i][:, cols].astype(F32) * part[:, 2 * c + i : 2 * c + i + 1] for i in range(2)
            )
            out[c * span_len : (c + 1) * span_len, cols] = total.astype(BF16)


def combine_context(position, place, pieces, stats, rows):
    groups = len(pieces)
    capacity, span_len, width = pieces[0].shape
    slots, two, lanes = stats[0].shape
    padded = -(-2 * (rows // span_len) // 128) * 128
    return pl.pallas_call(
        functools.partial(combine_context_kernel, groups),
        out_shape=jax.ShapeDtypeStruct((rows, width), BF16),
        in_specs=[smem()] * 2 + [vmem()] * (2 * groups),
        out_specs=vmem(),
        scratch_shapes=[
            pltpu.VMEM((groups * capacity, span_len, width), BF16),
            pltpu.VMEM((groups * slots, two, lanes), F32),
            pltpu.VMEM((padded, lanes), F32),
        ],
        compiler_params=params(24),
        cost_estimate=cost(rows * width * 4, groups * pieces[0].size * 2 + rows * width * 2),
        name="combine_context",
    )(position, place, *pieces, *stats)


def fill_diagonal(dst, block, heads, span_len):
    for h in range(heads):
        side = (h % 2) * HD
        dst[h * span_len : (h + 1) * span_len, side : side + HD] = block[:, h * HD : (h + 1) * HD]


def store_pair(dst, k, p, both, span_len):
    for s in range(2):
        cols = slice((2 * p + s) * HD, (2 * p + s + 1) * HD)
        rows = slice(s * span_len, (s + 1) * span_len)
        dst[k, :, cols] = both[rows, s * HD : (s + 1) * HD].astype(BF16)


def rows_of(nbr, row_len):
    return pl.ds(pl.multiple_of(nbr * row_len, row_len), row_len)


def columns_of(p, width, span_len):
    first = 2 * p * HD
    return (
        slice(first, first + 2 * HD),
        slice(width + first, width + first + 2 * HD),
        slice(2 * p * span_len, 2 * (p + 1) * span_len),
    )


def arrival(held, d, sems):
    return pltpu.make_async_copy(held.at[d], held.at[d], sems.at[d])


def local_kernel(groups, row_len, scale, counts, nbrs, *refs):
    qg_refs, (kv_ref, stats_ref), refs = refs[:groups], refs[groups : groups + 2], refs[groups + 2 :]
    ctx_refs, refs = refs[:groups], refs[groups:]
    kv, qg, ctx, ksem, isem, osem = refs[:6]
    diag = refs[6:]
    capacity, _, span_len, width = qg_refs[0].shape
    heads = width // HD
    kv_in = fetch([(kv_ref, kv)], ksem)
    fetch([(ref, qg.at[d]) for d, ref in enumerate(qg_refs)], isem)
    ctx_out = [pltpu.make_async_copy(ctx.at[d], ref, osem.at[d]) for d, ref in enumerate(ctx_refs)]
    for ref in diag:
        ref[...] = jnp.zeros_like(ref)
    kv_in[0].wait()

    def one_group(d, carry):
        arrival(qg, d, isem).wait()

        def step(i, carry):
            for u in range(2):
                k = jnp.minimum(2 * i + u, counts[d] - 1)
                j = d * capacity + k
                q_diag, g_diag = diag[2 * u], diag[2 * u + 1]
                fill_diagonal(q_diag, qg[d, k, 0], heads, span_len)
                fill_diagonal(g_diag, qg[d, k, 1], heads, span_len)
                rows = rows_of(nbrs[j], row_len)
                for p in range(heads // 2):
                    cols, vcols, lanes = columns_of(p, width, span_len)
                    values = kv[rows, vcols]
                    expo = jnp.exp(mm(kv[rows, cols], q_diag[lanes, :], NT) * scale)
                    grad_probs = mm(values, g_diag[lanes, :], NT)
                    total = jnp.sum(expo, axis=0, keepdims=True)
                    probs = expo / jnp.where(total > 0.0, total, 1.0)
                    stats_ref[j, 0:1, lanes] = total
                    stats_ref[j, 1:2, lanes] = jnp.sum(probs * grad_probs, axis=0, keepdims=True)
                    store_pair(ctx.at[d], k, p, mm(probs.astype(BF16).T, values, NN), span_len)
            return carry

        lax.fori_loop(0, (counts[d] + 1) // 2, step, 0)
        for e in range(groups):

            @pl.when(d == e)
            def _():
                ctx_out[e].start()

        return carry

    lax.fori_loop(0, groups, one_group, 0)
    for copy in ctx_out:
        copy.wait()


def attend_local(counts, nbrs, qg, kv, row_len, scale):
    groups = len(qg)
    capacity, _, span_len, width = qg[0].shape
    slots = groups * capacity
    lanes = span_len * (width // HD)
    outs = pl.pallas_call(
        functools.partial(local_kernel, groups, row_len, scale),
        out_shape=[jax.ShapeDtypeStruct((slots, 2, lanes), F32)]
        + [jax.ShapeDtypeStruct((capacity, span_len, width), BF16)] * groups,
        in_specs=[smem()] * 2 + [anyspace()] * (groups + 1),
        out_specs=[vmem()] + [anyspace()] * groups,
        scratch_shapes=[
            pltpu.VMEM(kv.shape, BF16),
            pltpu.VMEM((groups, *qg[0].shape), BF16),
            pltpu.VMEM((groups, capacity, span_len, width), BF16),
            pltpu.SemaphoreType.DMA((1,)),
            pltpu.SemaphoreType.DMA((groups,)),
            pltpu.SemaphoreType.DMA((groups,)),
        ]
        + [pltpu.VMEM((lanes, 2 * HD), BF16)] * 4,
        compiler_params=params(56),
        cost_estimate=cost(
            slots * 48 * row_len * lanes * HD,
            kv.size * 2 + slots * span_len * width * 6,
            slots * row_len * lanes,
        ),
        name="attend_local",
    )(counts, nbrs, *qg, kv)
    return outs[0], outs[1:]


def grads_kernel(groups, row_len, scale, counts, nbrs, partner, *refs):
    qg_refs, stat_refs, refs = refs[:groups], refs[groups : 2 * groups], refs[2 * groups :]
    (kv_ref, kw_ref, vw_ref), refs = refs[:3], refs[3:]
    gq_refs, (dkv_ref, part_ref), refs = refs[:groups], refs[groups : groups + 2], refs[groups + 2 :]
    kv, qg, stats, kw, vw, gq, acc, dkv, part, ksem, qsem, ssem, osem, psem = refs[:14]
    diag = refs[14:]
    capacity, _, span_len, width = qg_refs[0].shape
    slots = groups * capacity
    heads = width // HD
    stats_in = fetch(
        [(ref, stats.at[pl.ds(d * slots, slots)]) for d, ref in enumerate(stat_refs)], ssem
    )
    kv_in, kw_in, vw_in = fetch([(kv_ref, kv), (kw_ref, kw), (vw_ref, vw)], ksem)
    fetch([(ref, qg.at[d]) for d, ref in enumerate(qg_refs)], qsem)
    gq_out = [pltpu.make_async_copy(gq.at[d], ref, osem.at[d]) for d, ref in enumerate(gq_refs)]
    for ref in diag:
        ref[...] = jnp.zeros_like(ref)
    block = 256 if kv.shape[0] % 256 == 0 else kv.shape[0]
    blocks = kv.shape[0] // block

    def rows_at(i):
        return pl.ds(pl.multiple_of(i * block, block), block)

    def clear(i, carry):
        acc[rows_at(i), :] = jnp.zeros((block, 2 * width), F32)
        return carry

    lax.fori_loop(0, blocks, clear, 0)
    for copy in [*stats_in, kv_in]:
        copy.wait()

    def one_group(d, carry):
        arrival(qg, d, qsem).wait()

        def step(i, carry):
            for u in range(2):
                place = 2 * i + u
                live = place < counts[d]
                k = jnp.minimum(place, counts[d] - 1)
                j = d * capacity + k
                q_diag, g_diag = diag[2 * u], diag[2 * u + 1]
                fill_diagonal(q_diag, qg[d, k, 0], heads, span_len)
                fill_diagonal(g_diag, qg[d, k, 1], heads, span_len)
                rows = rows_of(nbrs[j], row_len)
                own, other = stats[j], stats[partner[j]]
                total = own[0:1] + other[0:1]
                total = jnp.where(total > 0.0, total, 1.0)
                shift = (own[0:1] / total) * own[1:2] + (other[0:1] / total) * other[1:2]
                for p in range(heads // 2):
                    cols, vcols, lanes = columns_of(p, width, span_len)
                    keys = kv[rows, cols]
                    expo = jnp.exp(mm(keys, q_diag[lanes, :], NT) * scale)
                    grad_probs = mm(kv[rows, vcols], g_diag[lanes, :], NT)
                    weights = expo / total[:, lanes]
                    mixed = weights * (grad_probs - shift[:, lanes]) * scale
                    store_pair(gq.at[d], k, p, mm(mixed.astype(BF16).T, keys, NN), span_len)
                    weights = jnp.where(live, weights, 0.0).astype(BF16)
                    mixed = jnp.where(live, mixed, 0.0).astype(BF16)
                    acc[rows, cols] += mm(mixed, q_diag[lanes, :], NN)
                    acc[rows, vcols] += mm(weights, g_diag[lanes, :], NN)
            return carry

        lax.fori_loop(0, (counts[d] + 1) // 2, step, 0)
        for e in range(groups):

            @pl.when(d == e)
            def _():
                gq_out[e].start()

        return carry

    lax.fori_loop(0, groups, one_group, 0)
    kw_in.wait()
    vw_in.wait()

    def results(i):
        b = rows_at(i)
        return (
            pltpu.make_async_copy(part.at[b], part_ref.at[b], psem.at[i, 0]),
            pltpu.make_async_copy(dkv.at[b], dkv_ref.at[b], psem.at[i, 1]),
        )

    def finish(i, carry):
        b = rows_at(i)
        dkv[b, :] = acc[b, :].astype(BF16)
        part[b, :] = (mm(dkv[b, :width], kw[...], NT) + mm(dkv[b, width:], vw[...], NT)).astype(BF16)
        for copy in results(i):
            copy.start()
        return carry

    def drain(i, carry):
        for copy in results(i):
            copy.wait()
        return carry

    lax.fori_loop(0, blocks, finish, 0)
    lax.fori_loop(0, blocks, drain, 0)
    for copy in gq_out:
        copy.wait()


def row_blocks(total, size):
    size = size if total % size == 0 else total
    return [pl.ds(i * size, size) for i in range(total // size)]


def attend_grads(counts, nbrs, partner, qg, stats, kv, key_weight, value_weight, row_len, scale):
    groups = len(qg)
    capacity, _, span_len, width = qg[0].shape
    slots = groups * capacity
    lanes = span_len * (width // HD)
    rows = kv.shape[0]
    feat = key_weight.shape[0]
    outs = pl.pallas_call(
        functools.partial(grads_kernel, groups, row_len, scale),
        out_shape=[jax.ShapeDtypeStruct((capacity, span_len, width), BF16)] * groups
        + [
            jax.ShapeDtypeStruct((rows, 2 * width), BF16),
            jax.ShapeDtypeStruct((rows, feat), BF16),
        ],
        in_specs=[smem()] * 3 + [anyspace()] * (2 * groups + 3),
        out_specs=[anyspace()] * (groups + 2),
        scratch_shapes=[
            pltpu.VMEM(kv.shape, BF16),
            pltpu.VMEM((groups, *qg[0].shape), BF16),
            pltpu.VMEM((groups * slots, 2, lanes), F32),
            pltpu.VMEM((feat, width), BF16),
            pltpu.VMEM((feat, width), BF16),
            pltpu.VMEM((groups, capacity, span_len, width), BF16),
            pltpu.VMEM((rows, 2 * width), F32),
            pltpu.VMEM((rows, 2 * width), BF16),
            pltpu.VMEM((rows, feat), BF16),
            pltpu.SemaphoreType.DMA((3,)),
            pltpu.SemaphoreType.DMA((groups,)),
            pltpu.SemaphoreType.DMA((groups,)),
            pltpu.SemaphoreType.DMA((groups,)),
            pltpu.SemaphoreType.DMA((max(1, rows // 256), 2)),
        ]
        + [pltpu.VMEM((lanes, 2 * HD), BF16)] * 4,
        compiler_params=params(56),
        cost_estimate=cost(
            4 * rows * feat * width + slots * 72 * row_len * lanes * HD,
            rows * feat * 2 + rows * width * 8 + slots * span_len * width * 6,
            slots * row_len * lanes,
        ),
        name="attend_grads",
    )(counts, nbrs, partner, *qg, *stats, kv, key_weight, value_weight)
    return outs[:groups], outs[groups], outs[groups + 1]


def weight_kernel(groups, waits, me, table, dkv, *refs):
    piece_refs, total = refs[waits : waits + groups], refs[-1]
    share = total.shape[1]
    for cols in row_blocks(total.shape[2], 256):
        product = mm(table[...], dkv[:, cols], TN).astype(BF16)
        for e in range(groups):
            total[e, :, cols] = product[e * share : (e + 1) * share]
    for d, piece in enumerate(piece_refs):
        piece[...] = total[jnp.bitwise_xor(me[0], d)]


def grad_weights(me, table, grad_kv, groups, waits):
    feat, columns = table.shape[1], grad_kv.shape[1]
    return pl.pallas_call(
        functools.partial(weight_kernel, groups, len(waits)),
        out_shape=[jax.ShapeDtypeStruct((feat // groups, columns), BF16)] * groups,
        in_specs=[smem(), vmem(), vmem()] + [anyspace()] * len(waits),
        out_specs=[vmem()] * groups,
        scratch_shapes=[pltpu.VMEM((groups, feat // groups, columns), BF16)],
        compiler_params=params(56),
        cost_estimate=cost(table.size * columns * 2, table.size * 2 + grad_kv.size * 2),
        name="grad_weights",
    )(me, table, grad_kv, *waits)


def body(
    queries,
    grad_ctx,
    neighbours,
    up_weight,
    down_weight,
    key_weight,
    value_weight,
    group_ids,
    slot_ids,
):
    groups = lax.axis_size("seq")
    if groups & (groups - 1):
        raise ValueError("seq size")
    me = lax.axis_index("seq").reshape(1)
    span_count = group_ids.shape[0]
    capacity = 2 * span_count // groups + 2
    width = queries.shape[1]
    span_len = queries.shape[0] // span_count
    own_count, row_len, feat = neighbours.shape
    table_len = own_count * lax.axis_size("ret")
    scale = 1.0 / math.sqrt(HD)

    encoded_own = encode(neighbours, up_weight, down_weight)
    table = lax.all_gather(encoded_own, "ret", axis=0, tiled=True).reshape(-1, feat)
    outgoing, position, place = dispatch(
        me, group_ids, queries, grad_ctx, groups, capacity, span_len, signs_of(encoded_own)
    )
    arrived = exchange(outgoing, "seq")
    kv = project(table, key_weight, value_weight)

    codes = (group_ids * table_len + slot_ids).reshape(1, -1)
    codes = exchange([codes] * groups, "seq")
    counts, nbrs, partner = slot_lists(me, codes, capacity, table_len, signs_of(kv))
    own_stats, local_ctx = attend_local(counts, nbrs, arrived, kv, row_len, scale)
    stats = exchange([own_stats] * groups, "seq")
    ctx_back = exchange(local_ctx, "seq")
    local_gq, grad_kv, grad_table = attend_grads(
        counts, nbrs, partner, arrived, stats, kv, key_weight, value_weight, row_len, scale
    )
    grad_encoded = lax.psum_scatter(
        grad_table.reshape(table_len, row_len, feat), "ret", scatter_dimension=0, tiled=True
    )
    gq_back = exchange(local_gq, "seq")
    pieces = exchange(
        grad_weights(me, table, grad_kv, groups, signs_of(*ctx_back[1:])), "seq"
    )
    grad_weight = sum(piece.astype(F32) for piece in pieces)
    context = combine_context(position, place, ctx_back, stats, queries.shape[0])
    grad_query = combine_grad(position, gq_back, queries.shape[0], [])
    return (context, grad_query, grad_encoded, grad_weight[:, :width], grad_weight[:, width:])


def solution(mesh):
    return jax.shard_map(
        body,
        mesh=mesh,
        in_specs=(
            P("seq", "ret"),
            P("seq", "ret"),
            P(("seq", "ret"), None, None),
            P(),
            P(),
            P(None, "ret"),
            P(None, "ret"),
            P("seq", None),
            P("seq", None),
        ),
        out_specs=(
            P("seq", "ret"),
            P("seq", "ret"),
            P(("seq", "ret"), None, None),
            P("seq", "ret"),
            P("seq", "ret"),
        ),
        check_vma=False,
    )
```

```python
import functools
import math

import jax
import jax.numpy as jnp
from jax import lax
from jax.experimental import pallas as pl
from jax.experimental.pallas import tpu as pltpu
from jax.sharding import PartitionSpec as P

HD = 128
UNROLL = 4
TAIL_FLOPS = 32000000000
WEIGHT_FLOPS = 70000000000
NT = (((1,), (1,)), ((), ()))
NN = (((1,), (0,)), ((), ()))
TN = (((0,), (0,)), ((), ()))
BF16 = jnp.bfloat16
F32 = jnp.float32


def params(mib):
    return pltpu.CompilerParams(vmem_limit_bytes=mib * 1024 * 1024)


def vmem():
    return pl.BlockSpec(memory_space=pltpu.VMEM)


def anyspace():
    return pl.BlockSpec(memory_space=pl.ANY)


def smem():
    return pl.BlockSpec(memory_space=pltpu.SMEM)


def cost(flops, nbytes, trans=0):
    return pl.CostEstimate(flops=flops, bytes_accessed=nbytes, transcendentals=trans)


def mm(a, b, dims):
    return lax.dot_general(a, b, dims, preferred_element_type=F32)


def fetch(pairs, sems):
    copies = [pltpu.make_async_copy(src, dst, sems.at[i]) for i, (src, dst) in enumerate(pairs)]
    for copy in copies:
        copy.start()
    return copies


def encode_kernel(x_ref, up_ref, down_ref, out_ref, up, down, normed, acc, usem, dsem):
    steps, _, block = up.shape

    def copies(i):
        cols = pl.ds(pl.multiple_of(i * block, block), block)
        return (
            pltpu.make_async_copy(up_ref.at[:, cols], up.at[i], usem.at[i]),
            pltpu.make_async_copy(down_ref.at[cols, :], down.at[i], dsem.at[i]),
        )

    for i in range(steps):
        for copy in copies(i):
            copy.start()
    x = x_ref[...].astype(F32)
    normed[...] = (x * lax.rsqrt(jnp.mean(x * x, axis=-1, keepdims=True) + 1e-06)).astype(BF16)
    acc[...] = x

    def step(i, carry):
        up_in, down_in = copies(i)
        up_in.wait()
        h = mm(normed[...], up[i], NN)
        inner = math.sqrt(2.0 / math.pi) * (h + 0.044715 * (h * h * h))
        hidden = (0.5 * h * (1.0 + jnp.tanh(inner))).astype(BF16)
        down_in.wait()
        acc[...] += mm(hidden, down[i], NN)
        return carry

    lax.fori_loop(0, steps, step, 0)
    out_ref[...] = acc[...].astype(BF16)


def encode(neighbours, up_weight, down_weight):
    feat, hidden = up_weight.shape
    rows = neighbours.reshape(-1, feat)
    block = 512 if hidden % 512 == 0 else hidden
    steps = hidden // block
    return pl.pallas_call(
        encode_kernel,
        out_shape=jax.ShapeDtypeStruct(rows.shape, BF16),
        in_specs=[vmem(), anyspace(), anyspace()],
        out_specs=vmem(),
        scratch_shapes=[
            pltpu.VMEM((steps, feat, block), BF16),
            pltpu.VMEM((steps, block, feat), BF16),
            pltpu.VMEM(rows.shape, BF16),
            pltpu.VMEM(rows.shape, F32),
            pltpu.SemaphoreType.DMA((steps,)),
            pltpu.SemaphoreType.DMA((steps,)),
        ],
        compiler_params=params(56),
        cost_estimate=cost(4 * rows.shape[0] * feat * hidden, 4 * feat * hidden, rows.shape[0] * hidden),
        name="encode",
    )(rows, up_weight, down_weight).reshape(neighbours.shape)


def project_kernel(table_ref, kw_ref, vw_ref, kv_ref):
    width = kw_ref.shape[1]
    kv_ref[:, :width] = mm(table_ref[...], kw_ref[...], NN).astype(BF16)
    kv_ref[:, width:] = mm(table_ref[...], vw_ref[...], NN).astype(BF16)


def project(table, key_weight, value_weight):
    rows, feat = table.shape
    width = key_weight.shape[1]
    block = 512 if rows % 512 == 0 else rows
    return pl.pallas_call(
        project_kernel,
        grid=(rows // block,),
        out_shape=jax.ShapeDtypeStruct((rows, 2 * width), BF16),
        in_specs=[
            pl.BlockSpec((block, feat), lambda i: (i, 0)),
            pl.BlockSpec((feat, width), lambda i: (0, 0)),
            pl.BlockSpec((feat, width), lambda i: (0, 0)),
        ],
        out_specs=pl.BlockSpec((block, 2 * width), lambda i: (i, 0)),
        compiler_params=params(59),
        cost_estimate=cost(8 * rows * feat * width, rows * (feat + 2 * width) * 2),
        name="project",
    )(table, key_weight, value_weight)


def exchange(pieces, axis):
    size = len(pieces)
    return [pieces[0]] + [
        lax.ppermute(pieces[d], axis, [(s, s ^ d) for s in range(size)]) for d in range(1, size)
    ]


def signs_of(*arrays):
    return [lax.slice(a, (0,) * a.ndim, (1,) * (a.ndim - 1) + (8,)) for a in arrays]


def dispatch_kernel(waits, me, group_ids, q_ref, g_ref, *refs):
    out_refs, refs = refs[waits:-5], refs[-5:]
    position, place, taken, held, sems = refs
    groups, capacity, _, span_len, _ = held.shape
    for d in range(groups):
        taken[d] = 0

    def step(i, carry):
        span = i // 2
        offset = jnp.bitwise_xor(group_ids[i % 2, span], me[0])
        rank = taken[offset]
        taken[offset] = rank + 1
        position[i] = offset * capacity + rank
        place[i] = offset * groups * capacity + offset * capacity + rank
        rows = pl.ds(pl.multiple_of(span * span_len, span_len), span_len)
        held[offset, rank, 0] = q_ref[rows, :]
        held[offset, rank, 1] = g_ref[rows, :]
        return carry

    lax.fori_loop(0, position.shape[0], step, 0)
    for copy in fetch([(held.at[d], ref) for d, ref in enumerate(out_refs)], sems):
        copy.wait()


def dispatch(me, group_ids, queries, grad_ctx, groups, capacity, span_len, waits):
    width = queries.shape[1]
    requests = group_ids.size
    piece = (capacity, 2, span_len, width)
    outs = pl.pallas_call(
        functools.partial(dispatch_kernel, len(waits)),
        out_shape=[jax.ShapeDtypeStruct(piece, BF16)] * groups
        + [jax.ShapeDtypeStruct((requests,), jnp.int32)] * 2,
        in_specs=[smem(), smem(), vmem(), vmem()] + [anyspace()] * len(waits),
        out_specs=[anyspace()] * groups + [smem()] * 2,
        scratch_shapes=[
            pltpu.SMEM((groups,), jnp.int32),
            pltpu.VMEM((groups, *piece), BF16),
            pltpu.SemaphoreType.DMA((groups,)),
        ],
        compiler_params=params(56),
        cost_estimate=cost(0, groups * capacity * span_len * width * 6),
        name="dispatch",
    )(me, group_ids, queries, grad_ctx, *waits)
    return outs[:groups], outs[groups], outs[groups + 1]


def slots_kernel(groups, waits, capacity, slot_bits, me, *refs):
    codes, (counts, nbrs, partner, taken) = refs[:groups], refs[groups + waits :]
    slots = groups * capacity
    for d in range(groups):
        source = jnp.bitwise_xor(me[0], d)
        for h in range(groups):
            taken[h] = 0

        def step(span, carry, d=d, source=source):
            both = []
            for i in range(2):
                code = codes[d][0, 2 * span + i]
                target = jnp.right_shift(code, slot_bits)
                rank = taken[target]
                taken[target] = rank + 1
                there = jnp.bitwise_xor(target, source) * capacity + rank
                both.append((target, rank, jnp.bitwise_and(code, (1 << slot_bits) - 1), there))
            for i in range(2):
                target, rank, nbr, _ = both[i]
                other, _, _, there = both[1 - i]

                @pl.when(target == me[0])
                def _():
                    nbrs[d * capacity + rank] = nbr
                    partner[d * capacity + rank] = jnp.bitwise_xor(other, me[0]) * slots + there

            return carry

        lax.fori_loop(0, codes[d].shape[1] // 2, step, 0)
        counts[d] = taken[me[0]]


def slot_lists(me, codes, capacity, slot_bits, waits):
    groups = len(codes)
    slots = groups * capacity
    return pl.pallas_call(
        functools.partial(slots_kernel, groups, len(waits), capacity, slot_bits),
        out_shape=[
            jax.ShapeDtypeStruct((groups,), jnp.int32),
            jax.ShapeDtypeStruct((slots,), jnp.int32),
            jax.ShapeDtypeStruct((slots,), jnp.int32),
        ],
        in_specs=[smem()] * (1 + groups) + [anyspace()] * len(waits),
        out_specs=[smem()] * 3,
        scratch_shapes=[pltpu.SMEM((groups,), jnp.int32)],
        compiler_params=params(56),
        cost_estimate=cost(0, slots * 16),
        name="slot_lists",
    )(me, *codes, *waits)


def gather_groups(refs, held):
    size = refs[0].shape[0]
    for d, ref in enumerate(refs):
        held[d * size : (d + 1) * size] = ref[...]


def combine_grad_kernel(groups, position, *refs):
    pieces, (out, held) = refs[:groups], refs[-2:]
    span_len = held.shape[1]
    gather_groups(pieces, held)

    def step(c, carry):
        rows = pl.ds(pl.multiple_of(c * span_len, span_len), span_len)
        first, second = held[position[2 * c]], held[position[2 * c + 1]]
        out[rows, :] = (first.astype(F32) + second.astype(F32)).astype(BF16)
        return carry

    lax.fori_loop(0, out.shape[0] // span_len, step, 0)


def combine_grad(position, pieces, rows, waits):
    groups = len(pieces)
    capacity, span_len, width = pieces[0].shape
    return pl.pallas_call(
        functools.partial(combine_grad_kernel, groups),
        out_shape=jax.ShapeDtypeStruct((rows, width), BF16),
        in_specs=[smem()] + [vmem()] * groups + [anyspace()] * len(waits),
        out_specs=vmem(),
        scratch_shapes=[pltpu.VMEM((groups * capacity, span_len, width), BF16)],
        compiler_params=params(16),
        cost_estimate=cost(TAIL_FLOPS, groups * pieces[0].size * 2 + rows * width * 2),
        name="combine_grad_queries",
    )(position, *pieces, *waits)


def combine_context_kernel(groups, position, place, *refs):
    pieces, stats = refs[:groups], refs[groups : 2 * groups]
    out, held, held_stats, shares = refs[2 * groups :]
    span_len, width = held.shape[1:]
    spans = out.shape[0] // span_len
    gather_groups(pieces, held)
    gather_groups(stats, held_stats)
    shares[...] = jnp.zeros_like(shares)
    for c in range(spans):
        first = held_stats[place[2 * c]][0:1]
        second = held_stats[place[2 * c + 1]][0:1]
        total = first + second
        shares[2 * c : 2 * c + 1, :] = first / total
        shares[2 * c + 1 : 2 * c + 2, :] = second / total
    columns = shares[...].T
    for c in range(spans):
        pair = [held[position[2 * c + i]] for i in range(2)]
        for h in range(width // HD):
            cols = slice(h * HD, (h + 1) * HD)
            part = columns[h * span_len : (h + 1) * span_len]
            total = sum(
                pair[i][:, cols].astype(F32) * part[:, 2 * c + i : 2 * c + i + 1] for i in range(2)
            )
            out[c * span_len : (c + 1) * span_len, cols] = total.astype(BF16)


def combine_context(position, place, pieces, stats, rows):
    groups = len(pieces)
    capacity, span_len, width = pieces[0].shape
    slots, two, lanes = stats[0].shape
    padded = -(-2 * (rows // span_len) // 128) * 128
    return pl.pallas_call(
        functools.partial(combine_context_kernel, groups),
        out_shape=jax.ShapeDtypeStruct((rows, width), BF16),
        in_specs=[smem()] * 2 + [vmem()] * (2 * groups),
        out_specs=vmem(),
        scratch_shapes=[
            pltpu.VMEM((groups * capacity, span_len, width), BF16),
            pltpu.VMEM((groups * slots, two, lanes), F32),
            pltpu.VMEM((padded, lanes), F32),
        ],
        compiler_params=params(24),
        cost_estimate=cost(rows * width * 4, groups * pieces[0].size * 2 + rows * width * 2),
        name="combine_context",
    )(position, place, *pieces, *stats)


def fill_diagonal(dst, block, heads, span_len):
    for h in range(heads):
        side = (h % 2) * HD
        dst[h * span_len : (h + 1) * span_len, side : side + HD] = block[:, h * HD : (h + 1) * HD]


def store_pair(dst, k, p, both, span_len):
    for s in range(2):
        cols = slice((2 * p + s) * HD, (2 * p + s + 1) * HD)
        rows = slice(s * span_len, (s + 1) * span_len)
        dst[k, :, cols] = both[rows, s * HD : (s + 1) * HD].astype(BF16)


def rows_of(nbr, row_len):
    return pl.ds(pl.multiple_of(nbr * row_len, row_len), row_len)


def columns_of(p, width, span_len):
    first = 2 * p * HD
    return (
        slice(first, first + 2 * HD),
        slice(width + first, width + first + 2 * HD),
        slice(2 * p * span_len, 2 * (p + 1) * span_len),
    )


def arrival(held, d, sems):
    return pltpu.make_async_copy(held.at[d], held.at[d], sems.at[d])


def local_kernel(groups, row_len, scale, counts, nbrs, *refs):
    qg_refs, (kv_ref, stats_ref), refs = refs[:groups], refs[groups : groups + 2], refs[groups + 2 :]
    ctx_refs, refs = refs[:groups], refs[groups:]
    kv, qg, ctx, ksem, isem, osem = refs[:6]
    diag = refs[6:]
    capacity, _, span_len, width = qg_refs[0].shape
    heads = width // HD
    kv_in = fetch([(kv_ref, kv)], ksem)
    fetch([(ref, qg.at[d]) for d, ref in enumerate(qg_refs)], isem)
    ctx_out = [pltpu.make_async_copy(ctx.at[d], ref, osem.at[d]) for d, ref in enumerate(ctx_refs)]
    for ref in diag:
        ref[...] = jnp.zeros_like(ref)
    kv_in[0].wait()

    def one_group(d, carry):
        arrival(qg, d, isem).wait()

        def step(i, carry):
            for u in range(UNROLL):
                k = jnp.minimum(UNROLL * i + u, counts[d] - 1)
                j = d * capacity + k
                q_diag, g_diag = diag[2 * u], diag[2 * u + 1]
                fill_diagonal(q_diag, qg[d, k, 0], heads, span_len)
                fill_diagonal(g_diag, qg[d, k, 1], heads, span_len)
                rows = rows_of(nbrs[j], row_len)
                for p in range(heads // 2):
                    cols, vcols, lanes = columns_of(p, width, span_len)
                    values = kv[rows, vcols]
                    expo = jnp.exp(mm(kv[rows, cols], q_diag[lanes, :], NT) * scale)
                    grad_probs = mm(values, g_diag[lanes, :], NT)
                    total = jnp.sum(expo, axis=0, keepdims=True)
                    probs = expo / jnp.where(total > 0.0, total, 1.0)
                    stats_ref[j, 0:1, lanes] = total
                    stats_ref[j, 1:2, lanes] = jnp.sum(probs * grad_probs, axis=0, keepdims=True)
                    store_pair(ctx.at[d], k, p, mm(probs.astype(BF16).T, values, NN), span_len)
            return carry

        lax.fori_loop(0, (counts[d] + UNROLL - 1) // UNROLL, step, 0)
        for e in range(groups):

            @pl.when(d == e)
            def _():
                ctx_out[e].start()

        return carry

    lax.fori_loop(0, groups, one_group, 0)
    for copy in ctx_out:
        copy.wait()


def attend_local(counts, nbrs, qg, kv, row_len, scale):
    groups = len(qg)
    capacity, _, span_len, width = qg[0].shape
    slots = groups * capacity
    lanes = span_len * (width // HD)
    outs = pl.pallas_call(
        functools.partial(local_kernel, groups, row_len, scale),
        out_shape=[jax.ShapeDtypeStruct((slots, 2, lanes), F32)]
        + [jax.ShapeDtypeStruct((capacity, span_len, width), BF16)] * groups,
        in_specs=[smem()] * 2 + [anyspace()] * (groups + 1),
        out_specs=[vmem()] + [anyspace()] * groups,
        scratch_shapes=[
            pltpu.VMEM(kv.shape, BF16),
            pltpu.VMEM((groups, *qg[0].shape), BF16),
            pltpu.VMEM((groups, capacity, span_len, width), BF16),
            pltpu.SemaphoreType.DMA((1,)),
            pltpu.SemaphoreType.DMA((groups,)),
            pltpu.SemaphoreType.DMA((groups,)),
        ]
        + [pltpu.VMEM((lanes, 2 * HD), BF16)] * (2 * UNROLL),
        compiler_params=params(56),
        cost_estimate=cost(
            slots * 48 * row_len * lanes * HD,
            kv.size * 2 + slots * span_len * width * 6,
            slots * row_len * lanes,
        ),
        name="attend_local",
    )(counts, nbrs, *qg, kv)
    return outs[0], outs[1:]


def grads_kernel(groups, row_len, scale, counts, nbrs, partner, *refs):
    qg_refs, stat_refs, refs = refs[:groups], refs[groups : 2 * groups], refs[2 * groups :]
    (kv_ref, kw_ref, vw_ref), refs = refs[:3], refs[3:]
    gq_refs, (dkv_ref, part_ref), refs = refs[:groups], refs[groups : groups + 2], refs[groups + 2 :]
    kv, qg, stats, kw, vw, gq, acc, dkv, part, ksem, qsem, ssem, osem, psem = refs[:14]
    diag = refs[14:]
    capacity, _, span_len, width = qg_refs[0].shape
    slots = groups * capacity
    heads = width // HD
    stats_in = fetch(
        [(ref, stats.at[pl.ds(d * slots, slots)]) for d, ref in enumerate(stat_refs)], ssem
    )
    kv_in, kw_in, vw_in = fetch([(kv_ref, kv), (kw_ref, kw), (vw_ref, vw)], ksem)
    fetch([(ref, qg.at[d]) for d, ref in enumerate(qg_refs)], qsem)
    gq_out = [pltpu.make_async_copy(gq.at[d], ref, osem.at[d]) for d, ref in enumerate(gq_refs)]
    for ref in diag:
        ref[...] = jnp.zeros_like(ref)
    block = 256 if kv.shape[0] % 256 == 0 else kv.shape[0]
    blocks = kv.shape[0] // block

    def rows_at(i):
        return pl.ds(pl.multiple_of(i * block, block), block)

    def clear(i, carry):
        acc[rows_at(i), :] = jnp.zeros((block, 2 * width), F32)
        return carry

    lax.fori_loop(0, blocks, clear, 0)
    for copy in [*stats_in, kv_in]:
        copy.wait()

    def one_group(d, carry):
        arrival(qg, d, qsem).wait()

        def step(i, carry):
            for u in range(UNROLL):
                place = UNROLL * i + u
                live = place < counts[d]
                k = jnp.minimum(place, counts[d] - 1)
                j = d * capacity + k
                q_diag, g_diag = diag[2 * u], diag[2 * u + 1]
                fill_diagonal(q_diag, qg[d, k, 0], heads, span_len)
                fill_diagonal(g_diag, qg[d, k, 1], heads, span_len)
                rows = rows_of(nbrs[j], row_len)
                own, other = stats[j], stats[partner[j]]
                total = own[0:1] + other[0:1]
                total = jnp.where(total > 0.0, total, 1.0)
                shift = (own[0:1] / total) * own[1:2] + (other[0:1] / total) * other[1:2]
                for p in range(heads // 2):
                    cols, vcols, lanes = columns_of(p, width, span_len)
                    keys = kv[rows, cols]
                    expo = jnp.exp(mm(keys, q_diag[lanes, :], NT) * scale)
                    grad_probs = mm(kv[rows, vcols], g_diag[lanes, :], NT)
                    weights = expo / total[:, lanes]
                    mixed = weights * (grad_probs - shift[:, lanes]) * scale
                    store_pair(gq.at[d], k, p, mm(mixed.astype(BF16).T, keys, NN), span_len)
                    weights = jnp.where(live, weights, 0.0).astype(BF16)
                    mixed = jnp.where(live, mixed, 0.0).astype(BF16)
                    acc[rows, cols] += mm(mixed, q_diag[lanes, :], NN)
                    acc[rows, vcols] += mm(weights, g_diag[lanes, :], NN)
            return carry

        lax.fori_loop(0, (counts[d] + UNROLL - 1) // UNROLL, step, 0)
        for e in range(groups):

            @pl.when(d == e)
            def _():
                gq_out[e].start()

        return carry

    lax.fori_loop(0, groups, one_group, 0)
    kw_in.wait()
    vw_in.wait()

    def results(i):
        b = rows_at(i)
        return (
            pltpu.make_async_copy(part.at[b], part_ref.at[b], psem.at[i, 0]),
            pltpu.make_async_copy(dkv.at[b], dkv_ref.at[b], psem.at[i, 1]),
        )

    def finish(i, carry):
        b = rows_at(i)
        dkv[b, :] = acc[b, :].astype(BF16)
        part[b, :] = (mm(dkv[b, :width], kw[...], NT) + mm(dkv[b, width:], vw[...], NT)).astype(BF16)
        for copy in results(i):
            copy.start()
        return carry

    def drain(i, carry):
        for copy in results(i):
            copy.wait()
        return carry

    lax.fori_loop(0, blocks, finish, 0)
    lax.fori_loop(0, blocks, drain, 0)
    for copy in gq_out:
        copy.wait()


def row_blocks(total, size):
    size = size if total % size == 0 else total
    return [pl.ds(i * size, size) for i in range(total // size)]


def attend_grads(counts, nbrs, partner, qg, stats, kv, key_weight, value_weight, row_len, scale):
    groups = len(qg)
    capacity, _, span_len, width = qg[0].shape
    slots = groups * capacity
    lanes = span_len * (width // HD)
    rows = kv.shape[0]
    feat = key_weight.shape[0]
    outs = pl.pallas_call(
        functools.partial(grads_kernel, groups, row_len, scale),
        out_shape=[jax.ShapeDtypeStruct((capacity, span_len, width), BF16)] * groups
        + [
            jax.ShapeDtypeStruct((rows, 2 * width), BF16),
            jax.ShapeDtypeStruct((rows, feat), BF16),
        ],
        in_specs=[smem()] * 3 + [anyspace()] * (2 * groups + 3),
        out_specs=[anyspace()] * (groups + 2),
        scratch_shapes=[
            pltpu.VMEM(kv.shape, BF16),
            pltpu.VMEM((groups, *qg[0].shape), BF16),
            pltpu.VMEM((groups * slots, 2, lanes), F32),
            pltpu.VMEM((feat, width), BF16),
            pltpu.VMEM((feat, width), BF16),
            pltpu.VMEM((groups, capacity, span_len, width), BF16),
            pltpu.VMEM((rows, 2 * width), F32),
            pltpu.VMEM((rows, 2 * width), BF16),
            pltpu.VMEM((rows, feat), BF16),
            pltpu.SemaphoreType.DMA((3,)),
            pltpu.SemaphoreType.DMA((groups,)),
            pltpu.SemaphoreType.DMA((groups,)),
            pltpu.SemaphoreType.DMA((groups,)),
            pltpu.SemaphoreType.DMA((max(1, rows // 256), 2)),
        ]
        + [pltpu.VMEM((lanes, 2 * HD), BF16)] * (2 * UNROLL),
        compiler_params=params(56),
        cost_estimate=cost(
            4 * rows * feat * width + slots * 72 * row_len * lanes * HD,
            rows * feat * 2 + rows * width * 8 + slots * span_len * width * 6,
            slots * row_len * lanes,
        ),
        name="attend_grads",
    )(counts, nbrs, partner, *qg, *stats, kv, key_weight, value_weight)
    return outs[:groups], outs[groups], outs[groups + 1]


def weight_kernel(groups, waits, me, table, dkv, *refs):
    piece_refs, total = refs[waits : waits + groups], refs[-1]
    share = total.shape[1]
    for cols in row_blocks(total.shape[2], 256):
        product = mm(table[...], dkv[:, cols], TN).astype(BF16)
        for e in range(groups):
            total[e, :, cols] = product[e * share : (e + 1) * share]
    for d, piece in enumerate(piece_refs):
        piece[...] = total[jnp.bitwise_xor(me[0], d)]


def grad_weights(me, table, grad_kv, groups, waits):
    feat, columns = table.shape[1], grad_kv.shape[1]
    return pl.pallas_call(
        functools.partial(weight_kernel, groups, len(waits)),
        out_shape=[jax.ShapeDtypeStruct((feat // groups, columns), BF16)] * groups,
        in_specs=[smem(), vmem(), vmem()] + [anyspace()] * len(waits),
        out_specs=[vmem()] * groups,
        scratch_shapes=[pltpu.VMEM((groups, feat // groups, columns), BF16)],
        compiler_params=params(56),
        cost_estimate=cost(WEIGHT_FLOPS, table.size * 2 + grad_kv.size * 2),
        name="grad_weights",
    )(me, table, grad_kv, *waits)


def body(
    queries,
    grad_ctx,
    neighbours,
    up_weight,
    down_weight,
    key_weight,
    value_weight,
    group_ids,
    slot_ids,
):
    groups = lax.axis_size("seq")
    if groups & (groups - 1):
        raise ValueError("seq size")
    me = lax.axis_index("seq").reshape(1)
    span_count = group_ids.shape[0]
    capacity = 2 * span_count // groups + 2
    width = queries.shape[1]
    span_len = queries.shape[0] // span_count
    own_count, row_len, feat = neighbours.shape
    table_len = own_count * lax.axis_size("ret")
    scale = 1.0 / math.sqrt(HD)

    encoded_own = encode(neighbours, up_weight, down_weight)
    table = lax.all_gather(encoded_own, "ret", axis=0, tiled=True).reshape(-1, feat)
    outgoing, position, place = dispatch(
        me, group_ids.T, queries, grad_ctx, groups, capacity, span_len, [encoded_own]
    )
    arrived = exchange(outgoing, "seq")
    kv = project(table, key_weight, value_weight)

    slot_bits = (table_len - 1).bit_length()
    codes = (group_ids * (1 << slot_bits) + slot_ids).reshape(1, -1)
    codes = exchange([codes] * groups, "seq")
    counts, nbrs, partner = slot_lists(me, codes, capacity, slot_bits, [kv])
    own_stats, local_ctx = attend_local(counts, nbrs, arrived, kv, row_len, scale)
    stats = exchange([own_stats] * groups, "seq")
    ctx_back = exchange(local_ctx, "seq")
    local_gq, grad_kv, grad_table = attend_grads(
        counts, nbrs, partner, arrived, stats, kv, key_weight, value_weight, row_len, scale
    )
    grad_encoded = lax.psum_scatter(
        grad_table.reshape(table_len, row_len, feat), "ret", scatter_dimension=0, tiled=True
    )
    gq_back = exchange(local_gq, "seq")
    pieces = exchange(
        grad_weights(me, table, grad_kv, groups, signs_of(*ctx_back[1:])), "seq"
    )
    grad_weight = sum(piece.astype(F32) for piece in pieces)
    context = combine_context(position, place, ctx_back, stats, queries.shape[0])
    grad_query = combine_grad(position, gq_back, queries.shape[0], [])
    return (context, grad_query, grad_encoded, grad_weight[:, :width], grad_weight[:, width:])


def solution(mesh):
    return jax.shard_map(
        body,
        mesh=mesh,
        in_specs=(
            P("seq", "ret"),
            P("seq", "ret"),
            P(("seq", "ret"), None, None),
            P(),
            P(),
            P(None, "ret"),
            P(None, "ret"),
            P("seq", None),
            P("seq", None),
        ),
        out_specs=(
            P("seq", "ret"),
            P("seq", "ret"),
            P(("seq", "ret"), None, None),
            P("seq", "ret"),
            P("seq", "ret"),
        ),
        check_vma=False,
    )
```

```python
import functools
import math

import jax
import jax.numpy as jnp
from jax import lax
from jax.experimental import pallas as pl
from jax.experimental.pallas import tpu as pltpu
from jax.sharding import PartitionSpec as P

HD = 128
HEADER = 16
UNROLL = 4
TAIL_FLOPS = 32000000000
WEIGHT_FLOPS = 70000000000
NT = (((1,), (1,)), ((), ()))
NN = (((1,), (0,)), ((), ()))
TN = (((0,), (0,)), ((), ()))
BF16 = jnp.bfloat16
F32 = jnp.float32


def params(mib):
    return pltpu.CompilerParams(vmem_limit_bytes=mib * 1024 * 1024)


def vmem():
    return pl.BlockSpec(memory_space=pltpu.VMEM)


def anyspace():
    return pl.BlockSpec(memory_space=pl.ANY)


def smem():
    return pl.BlockSpec(memory_space=pltpu.SMEM)


def cost(flops, nbytes, trans=0):
    return pl.CostEstimate(flops=flops, bytes_accessed=nbytes, transcendentals=trans)


def mm(a, b, dims):
    return lax.dot_general(a, b, dims, preferred_element_type=F32)


def fetch(pairs, sems):
    copies = [pltpu.make_async_copy(src, dst, sems.at[i]) for i, (src, dst) in enumerate(pairs)]
    for copy in copies:
        copy.start()
    return copies


def encode_kernel(x_ref, up_ref, down_ref, out_ref, up, down, normed, acc, usem, dsem):
    steps, _, block = up.shape

    def copies(i):
        cols = pl.ds(pl.multiple_of(i * block, block), block)
        return (
            pltpu.make_async_copy(up_ref.at[:, cols], up.at[i], usem.at[i]),
            pltpu.make_async_copy(down_ref.at[cols, :], down.at[i], dsem.at[i]),
        )

    for i in range(steps):
        for copy in copies(i):
            copy.start()
    x = x_ref[...].astype(F32)
    normed[...] = (x * lax.rsqrt(jnp.mean(x * x, axis=-1, keepdims=True) + 1e-06)).astype(BF16)
    acc[...] = x

    def step(i, carry):
        up_in, down_in = copies(i)
        up_in.wait()
        h = mm(normed[...], up[i], NN)
        inner = math.sqrt(2.0 / math.pi) * (h + 0.044715 * (h * h * h))
        hidden = (0.5 * h * (1.0 + jnp.tanh(inner))).astype(BF16)
        down_in.wait()
        acc[...] += mm(hidden, down[i], NN)
        return carry

    lax.fori_loop(0, steps, step, 0)
    out_ref[...] = acc[...].astype(BF16)


def encode(neighbours, up_weight, down_weight):
    feat, hidden = up_weight.shape
    rows = neighbours.reshape(-1, feat)
    block = 512 if hidden % 512 == 0 else hidden
    steps = hidden // block
    return pl.pallas_call(
        encode_kernel,
        out_shape=jax.ShapeDtypeStruct(rows.shape, BF16),
        in_specs=[vmem(), anyspace(), anyspace()],
        out_specs=vmem(),
        scratch_shapes=[
            pltpu.VMEM((steps, feat, block), BF16),
            pltpu.VMEM((steps, block, feat), BF16),
            pltpu.VMEM(rows.shape, BF16),
            pltpu.VMEM(rows.shape, F32),
            pltpu.SemaphoreType.DMA((steps,)),
            pltpu.SemaphoreType.DMA((steps,)),
        ],
        compiler_params=params(56),
        cost_estimate=cost(4 * rows.shape[0] * feat * hidden, 4 * feat * hidden, rows.shape[0] * hidden),
        name="encode",
    )(rows, up_weight, down_weight).reshape(neighbours.shape)


def project_kernel(row_len, table_ref, kw_ref, vw_ref, kv_ref):
    pairs = kw_ref.shape[1] // (2 * HD)
    for first, weight in ((0, kw_ref), (pairs, vw_ref)):
        product = mm(table_ref[...], weight[...], NN).astype(BF16)
        for n in range(table_ref.shape[0] // row_len):
            for p in range(pairs):
                kv_ref[n, first + p] = product[
                    n * row_len : (n + 1) * row_len, p * 2 * HD : (p + 1) * 2 * HD
                ]


def project(table, key_weight, value_weight, row_len):
    rows, feat = table.shape
    width = key_weight.shape[1]
    block = 512 if rows % 512 == 0 else rows
    blocks = 2 * width // (2 * HD)
    return pl.pallas_call(
        functools.partial(project_kernel, row_len),
        grid=(rows // block,),
        out_shape=jax.ShapeDtypeStruct((rows // row_len, blocks, row_len, 2 * HD), BF16),
        in_specs=[
            pl.BlockSpec((block, feat), lambda i: (i, 0)),
            pl.BlockSpec((feat, width), lambda i: (0, 0)),
            pl.BlockSpec((feat, width), lambda i: (0, 0)),
        ],
        out_specs=pl.BlockSpec((block // row_len, blocks, row_len, 2 * HD), lambda i: (i, 0, 0, 0)),
        compiler_params=params(59),
        cost_estimate=cost(8 * rows * feat * width, rows * (feat + 2 * width) * 2),
        name="project",
    )(table, key_weight, value_weight)


def exchange(pieces, axis):
    size = len(pieces)
    return [pieces[0]] + [
        lax.ppermute(pieces[d], axis, [(s, s ^ d) for s in range(size)]) for d in range(1, size)
    ]


def signs_of(*arrays):
    return [lax.slice(a, (0,) * a.ndim, (1,) * (a.ndim - 1) + (8,)) for a in arrays]


def dispatch_kernel(waits, me, group_ids, slot_ids, q_ref, g_ref, *refs):
    out_refs, refs = refs[waits:-6], refs[-6:]
    position, place, taken, held, info, sems = refs
    groups, rows, _ = held.shape
    requests = position.shape[0]
    span_len = q_ref.shape[0] // (requests // 2)
    capacity = (rows - HEADER) // (2 * span_len)
    slots = groups * capacity
    for d in range(groups):
        taken[d] = 0
    info[...] = jnp.zeros_like(info)

    def step(i, carry):
        span = i // 2
        offset = jnp.bitwise_xor(group_ids[i % 2, span], me[0])
        rank = taken[offset]
        taken[offset] = rank + 1
        position[i] = offset * capacity + rank
        place[i] = offset * slots + offset * capacity + rank
        source = pl.ds(pl.multiple_of(span * span_len, span_len), span_len)
        first = pl.multiple_of(rank * (2 * span_len), span_len)
        held[offset, pl.ds(first, span_len), :] = q_ref[source, :]
        held[offset, pl.ds(first + span_len, span_len), :] = g_ref[source, :]
        return carry

    lax.fori_loop(0, requests, step, 0)
    kind = lax.broadcasted_iota(jnp.int32, info.shape[1:], 0)
    lane = lax.broadcasted_iota(jnp.int32, info.shape[1:], 1)

    def note(i, carry):
        span, side = i // 2, i % 2
        target, other = group_ids[side, span], group_ids[1 - side, span]
        offset = jnp.bitwise_xor(target, me[0])
        rank = position[i] - offset * capacity
        there = position[2 * span + 1 - side]
        facts = jnp.where(
            kind == 0,
            slot_ids[side, span],
            jnp.where(kind == 1, jnp.bitwise_xor(target, other), jnp.where(kind == 2, there, 0)),
        )
        info[offset] = jnp.where((lane == rank) & (kind < 3), facts, info[offset])
        return carry

    lax.fori_loop(0, requests, note, 0)
    for d in range(groups):
        facts = jnp.where(kind == 3, taken[d], info[d]).astype(F32)
        held[d, rows - HEADER :, :] = jnp.zeros((HEADER, held.shape[2]), BF16)
        held[d, rows - HEADER :, :128] = facts.astype(BF16)
    for copy in fetch([(held.at[d], ref) for d, ref in enumerate(out_refs)], sems):
        copy.wait()


def dispatch(me, group_ids, slot_ids, queries, grad_ctx, groups, capacity, span_len, waits):
    width = queries.shape[1]
    requests = group_ids.size
    piece = (capacity * 2 * span_len + HEADER, width)
    outs = pl.pallas_call(
        functools.partial(dispatch_kernel, len(waits)),
        out_shape=[jax.ShapeDtypeStruct(piece, BF16)] * groups
        + [jax.ShapeDtypeStruct((requests,), jnp.int32)] * 2,
        in_specs=[smem()] * 3 + [vmem(), vmem()] + [anyspace()] * len(waits),
        out_specs=[anyspace()] * groups + [smem()] * 2,
        scratch_shapes=[
            pltpu.SMEM((groups,), jnp.int32),
            pltpu.VMEM((groups, *piece), BF16),
            pltpu.VMEM((groups, HEADER, 128), jnp.int32),
            pltpu.SemaphoreType.DMA((groups,)),
        ],
        compiler_params=params(56),
        cost_estimate=cost(0, groups * capacity * span_len * width * 6),
        name="dispatch",
    )(me, group_ids, slot_ids, queries, grad_ctx, *waits)
    return outs[:groups], outs[groups], outs[groups + 1]


def gather_groups(refs, held):
    size = refs[0].shape[0]
    for d, ref in enumerate(refs):
        held[d * size : (d + 1) * size] = ref[...]


def combine_grad_kernel(groups, position, *refs):
    pieces, (out, held) = refs[:groups], refs[-2:]
    span_len = held.shape[1]
    gather_groups(pieces, held)

    def step(c, carry):
        rows = pl.ds(pl.multiple_of(c * span_len, span_len), span_len)
        first, second = held[position[2 * c]], held[position[2 * c + 1]]
        out[rows, :] = (first.astype(F32) + second.astype(F32)).astype(BF16)
        return carry

    lax.fori_loop(0, out.shape[0] // span_len, step, 0)


def combine_grad(position, pieces, rows, waits):
    groups = len(pieces)
    capacity, span_len, width = pieces[0].shape
    return pl.pallas_call(
        functools.partial(combine_grad_kernel, groups),
        out_shape=jax.ShapeDtypeStruct((rows, width), BF16),
        in_specs=[smem()] + [vmem()] * groups + [anyspace()] * len(waits),
        out_specs=vmem(),
        scratch_shapes=[pltpu.VMEM((groups * capacity, span_len, width), BF16)],
        compiler_params=params(16),
        cost_estimate=cost(TAIL_FLOPS, groups * pieces[0].size * 2 + rows * width * 2),
        name="combine_grad_queries",
    )(position, *pieces, *waits)


def combine_context_kernel(groups, position, place, *refs):
    pieces, stats = refs[:groups], refs[groups : 2 * groups]
    out, held, held_stats, shares = refs[2 * groups :]
    span_len, width = held.shape[1:]
    spans = out.shape[0] // span_len
    gather_groups(pieces, held)
    gather_groups(stats, held_stats)
    shares[...] = jnp.zeros_like(shares)
    for c in range(spans):
        first = held_stats[place[2 * c]][0:1]
        second = held_stats[place[2 * c + 1]][0:1]
        total = first + second
        shares[2 * c : 2 * c + 1, :] = first / total
        shares[2 * c + 1 : 2 * c + 2, :] = second / total
    columns = shares[...].T
    for c in range(spans):
        pair = [held[position[2 * c + i]] for i in range(2)]
        for h in range(width // HD):
            cols = slice(h * HD, (h + 1) * HD)
            part = columns[h * span_len : (h + 1) * span_len]
            total = sum(
                pair[i][:, cols].astype(F32) * part[:, 2 * c + i : 2 * c + i + 1] for i in range(2)
            )
            out[c * span_len : (c + 1) * span_len, cols] = total.astype(BF16)


def combine_context(position, place, pieces, stats, rows):
    groups = len(pieces)
    capacity, span_len, width = pieces[0].shape
    slots, two, lanes = stats[0].shape
    padded = -(-2 * (rows // span_len) // 128) * 128
    return pl.pallas_call(
        functools.partial(combine_context_kernel, groups),
        out_shape=jax.ShapeDtypeStruct((rows, width), BF16),
        in_specs=[smem()] * 2 + [vmem()] * (2 * groups),
        out_specs=vmem(),
        scratch_shapes=[
            pltpu.VMEM((groups * capacity, span_len, width), BF16),
            pltpu.VMEM((groups * slots, two, lanes), F32),
            pltpu.VMEM((padded, lanes), F32),
        ],
        compiler_params=params(24),
        cost_estimate=cost(rows * width * 4, groups * pieces[0].size * 2 + rows * width * 2),
        name="combine_context",
    )(position, place, *pieces, *stats)


def fill_diagonal(dst, block, heads, span_len):
    for h in range(heads):
        side = (h % 2) * HD
        dst[h * span_len : (h + 1) * span_len, side : side + HD] = block[:, h * HD : (h + 1) * HD]


def blocks_of(square, size):
    count = square.shape[0] // size
    return jnp.concatenate(
        [square[i * size : (i + 1) * size, i * size : (i + 1) * size] for i in range(count)], axis=1
    )


def on_diagonal(parts):
    zero = jnp.zeros_like(parts[0])
    return jnp.concatenate(
        [
            jnp.concatenate([part if j == i else zero for j in range(len(parts))], axis=1)
            for i, part in enumerate(parts)
        ],
        axis=0,
    )


def halves(wide, size):
    return [wide[:, i * size : (i + 1) * size] for i in range(wide.shape[1] // size)]


def store_heads(dst, k, both, span_len):
    for h in range(both.shape[0] // span_len):
        rows = slice(h * span_len, (h + 1) * span_len)
        side = (h % 2) * HD
        dst[k, :, h * HD : (h + 1) * HD] = both[rows, side : side + HD].astype(BF16)


def stacked(kv, nbr, first, pairs):
    return kv[nbr, first : first + pairs].reshape(pairs * kv.shape[2], kv.shape[3])


def slot_rows(qg, d, which, span_len):
    return qg[d, pl.ds(pl.multiple_of(which * span_len, span_len), span_len), :]


def safe_inverse(total):
    shrink = jnp.where(total > 2.0**100, 2.0**-64, 1.0)
    scaled = total * shrink
    return shrink, 1.0 / jnp.where(scaled > 0.0, scaled, 1.0)


def arrival(held, d, sems):
    return pltpu.make_async_copy(held.at[d], held.at[d], sems.at[d])


def local_kernel(groups, row_len, span_len, *refs):
    qg_refs, refs = refs[:groups], refs[groups:]
    (kv_ref, stats_ref), refs = refs[:2], refs[2:]
    ctx_refs, (counts, nbrs, partner), refs = refs[:groups], refs[groups : groups + 3], refs[groups + 3 :]
    kv, qg, ctx, heads_up, facts, plain, ksem, isem, hsem, osem = refs[:10]
    diag = refs[10:]
    rows, width = qg_refs[0].shape
    heads = width // HD
    capacity = (rows - HEADER) // (2 * span_len)
    slots = groups * capacity
    pairs = heads // 2
    factor = math.log2(math.e) / math.sqrt(HD)
    head_rows = pl.ds(rows - HEADER, HEADER)
    heads_in = fetch(
        [(ref.at[head_rows, pl.ds(0, 128)], heads_up.at[d]) for d, ref in enumerate(qg_refs)], hsem
    )
    kv_in = fetch([(kv_ref, kv)], ksem)
    fetch([(ref, qg.at[d]) for d, ref in enumerate(qg_refs)], isem)
    ctx_out = [pltpu.make_async_copy(ctx.at[d], ref, osem.at[d]) for d, ref in enumerate(ctx_refs)]
    for copy in heads_in:
        copy.wait()
    facts[...] = heads_up[...].astype(F32).astype(jnp.int32)
    to_scalar = pltpu.make_async_copy(facts, plain, osem.at[groups])
    to_scalar.start()
    for ref in diag:
        ref[...] = jnp.zeros_like(ref)
    to_scalar.wait()

    def unpack(j, carry):
        d, k = j // capacity, j % capacity
        nbrs[j] = plain[d, 0, k]
        partner[j] = plain[d, 1, k] * slots + plain[d, 2, k]
        return carry

    lax.fori_loop(0, slots, unpack, 0)
    for d in range(groups):
        counts[d] = plain[d, 3, 0]
    kv_in[0].wait()

    def one_group(d, carry):
        arrival(qg, d, isem).wait()

        def step(i, carry):
            for u in range(UNROLL):
                k = jnp.minimum(UNROLL * i + u, counts[d] - 1)
                j = d * capacity + k
                q_diag, g_diag = diag[2 * u], diag[2 * u + 1]
                fill_diagonal(q_diag, slot_rows(qg, d, 2 * k, span_len), heads, span_len)
                fill_diagonal(g_diag, slot_rows(qg, d, 2 * k + 1, span_len), heads, span_len)
                values = stacked(kv, nbrs[j], pairs, pairs)
                scores = mm(stacked(kv, nbrs[j], 0, pairs), q_diag[...], NT)
                expo = jnp.exp2(blocks_of(scores, row_len) * factor)
                grad_probs = blocks_of(mm(values, g_diag[...], NT), row_len)
                total = jnp.sum(expo, axis=0, keepdims=True)
                shrink, inverse = safe_inverse(total)
                probs = (expo * shrink) * inverse
                stats_ref[j, 0:1, :] = total
                stats_ref[j, 1:2, :] = jnp.sum(probs * grad_probs, axis=0, keepdims=True)
                turned = on_diagonal([x.T for x in halves(probs.astype(BF16), row_len)])
                store_heads(ctx.at[d], k, mm(turned, values, NN), span_len)
            return carry

        lax.fori_loop(0, (counts[d] + UNROLL - 1) // UNROLL, step, 0)
        for e in range(groups):

            @pl.when(d == e)
            def _():
                ctx_out[e].start()

        return carry

    lax.fori_loop(0, groups, one_group, 0)
    for copy in ctx_out:
        copy.wait()


def attend_local(qg, kv, row_len, span_len):
    groups = len(qg)
    rows, width = qg[0].shape
    capacity = (rows - HEADER) // (2 * span_len)
    slots = groups * capacity
    lanes = span_len * (width // HD)
    outs = pl.pallas_call(
        functools.partial(local_kernel, groups, row_len, span_len),
        out_shape=[jax.ShapeDtypeStruct((slots, 2, lanes), F32)]
        + [jax.ShapeDtypeStruct((capacity, span_len, width), BF16)] * groups
        + [jax.ShapeDtypeStruct((n,), jnp.int32) for n in (groups, slots, slots)],
        in_specs=[anyspace()] * (groups + 1),
        out_specs=[vmem()] + [anyspace()] * groups + [smem()] * 3,
        scratch_shapes=[
            pltpu.VMEM(kv.shape, BF16),
            pltpu.VMEM((groups, rows, width), BF16),
            pltpu.VMEM((groups, capacity, span_len, width), BF16),
            pltpu.VMEM((groups, HEADER, 128), BF16),
            pltpu.VMEM((groups, HEADER, 128), jnp.int32),
            pltpu.SMEM((groups, HEADER, 128), jnp.int32),
            pltpu.SemaphoreType.DMA((1,)),
            pltpu.SemaphoreType.DMA((groups,)),
            pltpu.SemaphoreType.DMA((groups,)),
            pltpu.SemaphoreType.DMA((groups + 1,)),
        ]
        + [pltpu.VMEM((lanes, 2 * HD), BF16)] * (2 * UNROLL),
        compiler_params=params(56),
        cost_estimate=cost(
            slots * 48 * row_len * lanes * HD,
            kv.size * 2 + slots * span_len * width * 6,
            slots * row_len * lanes,
        ),
        name="attend_local",
    )(*qg, kv)
    return outs[0], outs[1 : groups + 1], outs[groups + 1 :]


def grads_kernel(groups, row_len, span_len, counts, nbrs, partner, *refs):
    qg_refs, stat_refs, refs = refs[:groups], refs[groups : 2 * groups], refs[2 * groups :]
    (kv_ref, kw_ref, vw_ref), refs = refs[:3], refs[3:]
    gq_refs, (dkv_ref, part_ref), refs = refs[:groups], refs[groups : groups + 2], refs[groups + 2 :]
    kv, qg, stats, kw, vw, gq, acc, dkv, part, ksem, qsem, ssem, osem, psem = refs[:14]
    diag = refs[14:]
    width = qg_refs[0].shape[1]
    capacity = gq_refs[0].shape[0]
    slots = groups * capacity
    heads = width // HD
    scale = 1.0 / math.sqrt(HD)
    pairs = heads // 2
    factor = math.log2(math.e) * scale
    stats_in = fetch(
        [(ref, stats.at[pl.ds(d * slots, slots)]) for d, ref in enumerate(stat_refs)], ssem
    )
    kv_in, kw_in, vw_in = fetch([(kv_ref, kv), (kw_ref, kw), (vw_ref, vw)], ksem)
    fetch([(ref, qg.at[d]) for d, ref in enumerate(qg_refs)], qsem)
    gq_out = [
        pltpu.make_async_copy(gq.at[d, pl.ds(0, capacity)], ref, osem.at[d])
        for d, ref in enumerate(gq_refs)
    ]
    for ref in diag:
        ref[...] = jnp.zeros_like(ref)
    some = 2 if acc.shape[0] % 2 == 0 else 1
    block = some * row_len
    blocks = acc.shape[0] // some

    def rows_at(i):
        return pl.ds(pl.multiple_of(i * block, block), block)

    def clear(n, carry):
        acc[n] = jnp.zeros(acc.shape[1:], F32)
        return carry

    lax.fori_loop(0, acc.shape[0], clear, 0)
    for copy in [*stats_in, kv_in]:
        copy.wait()

    def one_group(d, carry):
        arrival(qg, d, qsem).wait()

        def step(i, carry):
            for u in range(UNROLL):
                place = UNROLL * i + u
                live = place < counts[d]
                k = jnp.minimum(place, counts[d] - 1)
                j = d * capacity + k
                q_diag, g_diag = diag[2 * u], diag[2 * u + 1]
                fill_diagonal(q_diag, slot_rows(qg, d, 2 * k, span_len), heads, span_len)
                fill_diagonal(g_diag, slot_rows(qg, d, 2 * k + 1, span_len), heads, span_len)
                nbr = nbrs[j]
                kept = jnp.where(live, k, capacity)
                own, other = stats[j], stats[partner[j]]
                total = own[0:1] + other[0:1]
                shrink, inverse = safe_inverse(total)
                shift = ((own[0:1] * shrink) * inverse) * own[1:2]
                shift += ((other[0:1] * shrink) * inverse) * other[1:2]
                inverse = jnp.where(live, inverse, 0.0)
                keys = stacked(kv, nbr, 0, pairs)
                expo = jnp.exp2(blocks_of(mm(keys, q_diag[...], NT), row_len) * factor) * shrink
                grad_probs = blocks_of(mm(stacked(kv, nbr, pairs, pairs), g_diag[...], NT), row_len)
                weights = expo * inverse
                mixed = halves((weights * (grad_probs - shift) * scale).astype(BF16), row_len)
                weights = halves(weights.astype(BF16), row_len)
                turned = on_diagonal([x.T for x in mixed])
                store_heads(gq.at[d], kept, mm(turned, keys, NN), span_len)
                shape = (pairs, row_len, 2 * HD)
                acc[nbr, :pairs] += mm(on_diagonal(mixed), q_diag[...], NN).reshape(shape)
                acc[nbr, pairs:] += mm(on_diagonal(weights), g_diag[...], NN).reshape(shape)
            return carry

        lax.fori_loop(0, (counts[d] + UNROLL - 1) // UNROLL, step, 0)
        for e in range(groups):

            @pl.when(d == e)
            def _():
                gq_out[e].start()

        return carry

    lax.fori_loop(0, groups, one_group, 0)
    kw_in.wait()
    vw_in.wait()

    def results(i):
        b = rows_at(i)
        return (
            pltpu.make_async_copy(part.at[b], part_ref.at[b], psem.at[i, 0]),
            pltpu.make_async_copy(dkv.at[b], dkv_ref.at[b], psem.at[i, 1]),
        )

    def finish(i, carry):
        b = rows_at(i)
        for p in range(2 * pairs):
            part_of = acc[pl.ds(i * some, some), p].reshape(block, 2 * HD)
            dkv[b, p * 2 * HD : (p + 1) * 2 * HD] = part_of.astype(BF16)
        part[b, :] = (mm(dkv[b, :width], kw[...], NT) + mm(dkv[b, width:], vw[...], NT)).astype(BF16)
        for copy in results(i):
            copy.start()
        return carry

    def drain(i, carry):
        for copy in results(i):
            copy.wait()
        return carry

    lax.fori_loop(0, blocks, finish, 0)
    lax.fori_loop(0, blocks, drain, 0)
    for copy in gq_out:
        copy.wait()


def row_blocks(total, size):
    size = size if total % size == 0 else total
    return [pl.ds(i * size, size) for i in range(total // size)]


def attend_grads(lists, qg, stats, kv, key_weight, value_weight, row_len, span_len):
    groups = len(qg)
    width = qg[0].shape[1]
    capacity = (qg[0].shape[0] - HEADER) // (2 * span_len)
    slots = groups * capacity
    lanes = span_len * (width // HD)
    rows = kv.shape[0] * row_len
    feat = key_weight.shape[0]
    outs = pl.pallas_call(
        functools.partial(grads_kernel, groups, row_len, span_len),
        out_shape=[jax.ShapeDtypeStruct((capacity, span_len, width), BF16)] * groups
        + [
            jax.ShapeDtypeStruct((rows, 2 * width), BF16),
            jax.ShapeDtypeStruct((rows, feat), BF16),
        ],
        in_specs=[smem()] * 3 + [anyspace()] * (2 * groups + 3),
        out_specs=[anyspace()] * (groups + 2),
        scratch_shapes=[
            pltpu.VMEM(kv.shape, BF16),
            pltpu.VMEM((groups, *qg[0].shape), BF16),
            pltpu.VMEM((groups * slots, 2, lanes), F32),
            pltpu.VMEM((feat, width), BF16),
            pltpu.VMEM((feat, width), BF16),
            pltpu.VMEM((groups, capacity + 1, span_len, width), BF16),
            pltpu.VMEM(kv.shape, F32),
            pltpu.VMEM((rows, 2 * width), BF16),
            pltpu.VMEM((rows, feat), BF16),
            pltpu.SemaphoreType.DMA((3,)),
            pltpu.SemaphoreType.DMA((groups,)),
            pltpu.SemaphoreType.DMA((groups,)),
            pltpu.SemaphoreType.DMA((groups,)),
            pltpu.SemaphoreType.DMA((kv.shape[0], 2)),
        ]
        + [pltpu.VMEM((lanes, 2 * HD), BF16)] * (2 * UNROLL),
        compiler_params=params(56),
        cost_estimate=cost(
            4 * rows * feat * width + slots * 72 * row_len * lanes * HD,
            rows * feat * 2 + rows * width * 8 + slots * span_len * width * 6,
            slots * row_len * lanes,
        ),
        name="attend_grads",
    )(*lists, *qg, *stats, kv, key_weight, value_weight)
    return outs[:groups], outs[groups], outs[groups + 1]


def weight_kernel(groups, waits, me, table, dkv, *refs):
    piece_refs, total = refs[waits : waits + groups], refs[-1]
    share = total.shape[1]
    for cols in row_blocks(total.shape[2], 256):
        product = mm(table[...], dkv[:, cols], TN).astype(BF16)
        for e in range(groups):
            total[e, :, cols] = product[e * share : (e + 1) * share]
    for d, piece in enumerate(piece_refs):
        piece[...] = total[jnp.bitwise_xor(me[0], d)]


def grad_weights(me, table, grad_kv, groups, waits):
    feat, columns = table.shape[1], grad_kv.shape[1]
    return pl.pallas_call(
        functools.partial(weight_kernel, groups, len(waits)),
        out_shape=[jax.ShapeDtypeStruct((feat // groups, columns), BF16)] * groups,
        in_specs=[smem(), vmem(), vmem()] + [anyspace()] * len(waits),
        out_specs=[vmem()] * groups,
        scratch_shapes=[pltpu.VMEM((groups, feat // groups, columns), BF16)],
        compiler_params=params(56),
        cost_estimate=cost(WEIGHT_FLOPS, table.size * 2 + grad_kv.size * 2),
        name="grad_weights",
    )(me, table, grad_kv, *waits)


def body(
    queries,
    grad_ctx,
    neighbours,
    up_weight,
    down_weight,
    key_weight,
    value_weight,
    group_ids,
    slot_ids,
):
    groups = lax.axis_size("seq")
    if groups & (groups - 1):
        raise ValueError("seq size")
    me = lax.axis_index("seq").reshape(1)
    span_count = group_ids.shape[0]
    capacity = 2 * span_count // groups + 2
    width = queries.shape[1]
    span_len = queries.shape[0] // span_count
    own_count, row_len, feat = neighbours.shape
    table_len = own_count * lax.axis_size("ret")

    encoded_own = encode(neighbours, up_weight, down_weight)
    table = lax.all_gather(encoded_own, "ret", axis=0, tiled=True).reshape(-1, feat)
    outgoing, position, place = dispatch(
        me, group_ids.T, slot_ids.T, queries, grad_ctx, groups, capacity, span_len, [encoded_own]
    )
    arrived = exchange(outgoing, "seq")
    kv = project(table, key_weight, value_weight, row_len)
    own_stats, local_ctx, lists = attend_local(arrived, kv, row_len, span_len)
    stats = exchange([own_stats] * groups, "seq")
    ctx_back = exchange(local_ctx, "seq")
    local_gq, grad_kv, grad_table = attend_grads(
        lists, arrived, stats, kv, key_weight, value_weight, row_len, span_len
    )
    grad_encoded = lax.psum_scatter(
        grad_table.reshape(table_len, row_len, feat), "ret", scatter_dimension=0, tiled=True
    )
    gq_back = exchange(local_gq, "seq")
    pieces = exchange(
        grad_weights(me, table, grad_kv, groups, signs_of(*ctx_back[1:])), "seq"
    )
    grad_weight = sum(piece.astype(F32) for piece in pieces)
    context = combine_context(position, place, ctx_back, stats, queries.shape[0])
    grad_query = combine_grad(position, gq_back, queries.shape[0], [])
    return (context, grad_query, grad_encoded, grad_weight[:, :width], grad_weight[:, width:])


def solution(mesh):
    return jax.shard_map(
        body,
        mesh=mesh,
        in_specs=(
            P("seq", "ret"),
            P("seq", "ret"),
            P(("seq", "ret"), None, None),
            P(),
            P(),
            P(None, "ret"),
            P(None, "ret"),
            P("seq", None),
            P("seq", None),
        ),
        out_specs=(
            P("seq", "ret"),
            P("seq", "ret"),
            P(("seq", "ret"), None, None),
            P("seq", "ret"),
            P("seq", "ret"),
        ),
        check_vma=False,
    )
```

```python
import functools
import math

import jax
import jax.numpy as jnp
from jax import lax
from jax.experimental import pallas as pl
from jax.experimental.pallas import tpu as pltpu
from jax.sharding import PartitionSpec as P

HD = 128
HEADER = 16
UNROLL = 8
TAIL_FLOPS = 32000000000
WEIGHT_FLOPS = 70000000000
NT = (((1,), (1,)), ((), ()))
NN = (((1,), (0,)), ((), ()))
TN = (((0,), (0,)), ((), ()))
BF16 = jnp.bfloat16
F32 = jnp.float32


def params(mib):
    return pltpu.CompilerParams(vmem_limit_bytes=mib * 1024 * 1024)


def vmem():
    return pl.BlockSpec(memory_space=pltpu.VMEM)


def anyspace():
    return pl.BlockSpec(memory_space=pl.ANY)


def smem():
    return pl.BlockSpec(memory_space=pltpu.SMEM)


def cost(flops, nbytes, trans=0):
    return pl.CostEstimate(flops=flops, bytes_accessed=nbytes, transcendentals=trans)


def mm(a, b, dims):
    return lax.dot_general(a, b, dims, preferred_element_type=F32)


def fetch(pairs, sems):
    copies = [pltpu.make_async_copy(src, dst, sems.at[i]) for i, (src, dst) in enumerate(pairs)]
    for copy in copies:
        copy.start()
    return copies


def encode_kernel(x_ref, up_ref, down_ref, out_ref, up, down, normed, acc, usem, dsem):
    steps, _, block = up.shape

    def copies(i):
        cols = pl.ds(pl.multiple_of(i * block, block), block)
        return (
            pltpu.make_async_copy(up_ref.at[:, cols], up.at[i], usem.at[i]),
            pltpu.make_async_copy(down_ref.at[cols, :], down.at[i], dsem.at[i]),
        )

    for i in range(steps):
        for copy in copies(i):
            copy.start()
    x = x_ref[...].astype(F32)
    normed[...] = (x * lax.rsqrt(jnp.mean(x * x, axis=-1, keepdims=True) + 1e-06)).astype(BF16)
    acc[...] = x

    def step(i, carry):
        up_in, down_in = copies(i)
        up_in.wait()
        h = mm(normed[...], up[i], NN)
        inner = math.sqrt(2.0 / math.pi) * (h + 0.044715 * (h * h * h))
        hidden = (0.5 * h * (1.0 + jnp.tanh(inner))).astype(BF16)
        down_in.wait()
        acc[...] += mm(hidden, down[i], NN)
        return carry

    lax.fori_loop(0, steps, step, 0)
    out_ref[...] = acc[...].astype(BF16)


def encode(neighbours, up_weight, down_weight):
    feat, hidden = up_weight.shape
    rows = neighbours.reshape(-1, feat)
    block = 896 if hidden % 896 == 0 else hidden
    steps = hidden // block
    return pl.pallas_call(
        encode_kernel,
        out_shape=jax.ShapeDtypeStruct(rows.shape, BF16),
        in_specs=[vmem(), anyspace(), anyspace()],
        out_specs=vmem(),
        scratch_shapes=[
            pltpu.VMEM((steps, feat, block), BF16),
            pltpu.VMEM((steps, block, feat), BF16),
            pltpu.VMEM(rows.shape, BF16),
            pltpu.VMEM(rows.shape, F32),
            pltpu.SemaphoreType.DMA((steps,)),
            pltpu.SemaphoreType.DMA((steps,)),
        ],
        compiler_params=params(62),
        cost_estimate=cost(4 * rows.shape[0] * feat * hidden, 4 * feat * hidden, rows.shape[0] * hidden),
        name="encode",
    )(rows, up_weight, down_weight).reshape(neighbours.shape)


def project_kernel(row_len, table_ref, kw_ref, vw_ref, kv_ref):
    pairs = kw_ref.shape[1] // (2 * HD)
    for first, weight in ((0, kw_ref), (pairs, vw_ref)):
        product = mm(table_ref[...], weight[...], NN).astype(BF16)
        for n in range(table_ref.shape[0] // row_len):
            for p in range(pairs):
                kv_ref[n, first + p] = product[
                    n * row_len : (n + 1) * row_len, p * 2 * HD : (p + 1) * 2 * HD
                ]


def project(table, key_weight, value_weight, row_len):
    rows, feat = table.shape
    width = key_weight.shape[1]
    block = 512 if rows % 512 == 0 else rows
    blocks = 2 * width // (2 * HD)
    return pl.pallas_call(
        functools.partial(project_kernel, row_len),
        grid=(rows // block,),
        out_shape=jax.ShapeDtypeStruct((rows // row_len, blocks, row_len, 2 * HD), BF16),
        in_specs=[
            pl.BlockSpec((block, feat), lambda i: (i, 0)),
            pl.BlockSpec((feat, width), lambda i: (0, 0)),
            pl.BlockSpec((feat, width), lambda i: (0, 0)),
        ],
        out_specs=pl.BlockSpec((block // row_len, blocks, row_len, 2 * HD), lambda i: (i, 0, 0, 0)),
        compiler_params=params(59),
        cost_estimate=cost(8 * rows * feat * width, rows * (feat + 2 * width) * 2),
        name="project",
    )(table, key_weight, value_weight)


def exchange(pieces, axis):
    size = len(pieces)
    return [pieces[0]] + [
        lax.ppermute(pieces[d], axis, [(s, s ^ d) for s in range(size)]) for d in range(1, size)
    ]


def signs_of(*arrays):
    return [lax.slice(a, (0,) * a.ndim, (1,) * (a.ndim - 1) + (8,)) for a in arrays]


def dispatch_kernel(waits, me, group_ids, slot_ids, q_ref, g_ref, *refs):
    out_refs, refs = refs[waits:-7], refs[-7:]
    position, place, taken, info, header, sems, hsem = refs
    groups, rows = len(out_refs), out_refs[0].shape[0]
    requests = position.shape[0]
    span_len = q_ref.shape[0] // (requests // 2)
    capacity = (rows - HEADER) // (2 * span_len)
    slots = groups * capacity
    for d in range(groups):
        taken[d] = 0
    info[...] = jnp.zeros_like(info)

    def step(i, carry):
        span = i // 2
        offset = jnp.bitwise_xor(group_ids[i % 2, span], me[0])
        rank = taken[offset]
        taken[offset] = rank + 1
        position[i] = offset * capacity + rank
        place[i] = offset * slots + offset * capacity + rank
        source = pl.ds(pl.multiple_of(span * span_len, span_len), span_len)
        for e, out_ref in enumerate(out_refs):

            @pl.when(offset == e)
            def _():
                for half, ref in enumerate((q_ref, g_ref)):
                    first = pl.multiple_of((2 * rank + half) * span_len, span_len)
                    target = out_ref.at[pl.ds(first, span_len)]
                    pltpu.make_async_copy(ref.at[source], target, sems.at[i, half]).start()

        return carry

    lax.fori_loop(0, requests, step, 0)
    kind = lax.broadcasted_iota(jnp.int32, info.shape[1:], 0)
    lane = lax.broadcasted_iota(jnp.int32, info.shape[1:], 1)

    def note(i, carry):
        span, side = i // 2, i % 2
        target, other = group_ids[side, span], group_ids[1 - side, span]
        offset = jnp.bitwise_xor(target, me[0])
        rank = position[i] - offset * capacity
        there = position[2 * span + 1 - side]
        facts = jnp.where(
            kind == 0,
            slot_ids[side, span],
            jnp.where(kind == 1, jnp.bitwise_xor(target, other), jnp.where(kind == 2, there, 0)),
        )
        info[offset] = jnp.where((lane == rank) & (kind < 3), facts, info[offset])
        return carry

    lax.fori_loop(0, requests, note, 0)
    for d in range(groups):
        facts = jnp.where(kind == 3, taken[d], info[d]).astype(F32)
        header[d] = jnp.zeros(header.shape[1:], BF16)
        header[d, :, :128] = facts.astype(BF16)
    head_rows = pl.ds(rows - HEADER, HEADER)
    headers = fetch([(header.at[d], ref.at[head_rows]) for d, ref in enumerate(out_refs)], hsem)

    def drain(i, carry):
        some = pl.ds(0, span_len)
        for half, ref in enumerate((q_ref, g_ref)):
            pltpu.make_async_copy(ref.at[some], out_refs[0].at[some], sems.at[i, half]).wait()
        return carry

    lax.fori_loop(0, requests, drain, 0)
    for copy in headers:
        copy.wait()


def dispatch(me, group_ids, slot_ids, queries, grad_ctx, groups, capacity, span_len, waits):
    width = queries.shape[1]
    requests = group_ids.size
    piece = (capacity * 2 * span_len + HEADER, width)
    outs = pl.pallas_call(
        functools.partial(dispatch_kernel, len(waits)),
        out_shape=[jax.ShapeDtypeStruct(piece, BF16)] * groups
        + [jax.ShapeDtypeStruct((requests,), jnp.int32)] * 2,
        in_specs=[smem()] * 3 + [vmem()] * 2 + [anyspace()] * len(waits),
        out_specs=[anyspace()] * groups + [smem()] * 2,
        scratch_shapes=[
            pltpu.SMEM((groups,), jnp.int32),
            pltpu.VMEM((groups, HEADER, 128), jnp.int32),
            pltpu.VMEM((groups, HEADER, width), BF16),
            pltpu.SemaphoreType.DMA((requests, 2)),
            pltpu.SemaphoreType.DMA((groups,)),
        ],
        compiler_params=params(62),
        cost_estimate=cost(0, groups * capacity * span_len * width * 6),
        name="dispatch",
    )(me, group_ids, slot_ids, queries, grad_ctx, *waits)
    return outs[:groups], outs[groups], outs[groups + 1]


def gather_groups(refs, held):
    size = refs[0].shape[0]
    for d, ref in enumerate(refs):
        held[d * size : (d + 1) * size] = ref[...]


def combine_grad_kernel(groups, position, *refs):
    pieces, (out, held) = refs[:groups], refs[-2:]
    span_len = held.shape[1]
    gather_groups(pieces, held)

    def step(c, carry):
        rows = pl.ds(pl.multiple_of(c * span_len, span_len), span_len)
        first, second = held[position[2 * c]], held[position[2 * c + 1]]
        out[rows, :] = (first.astype(F32) + second.astype(F32)).astype(BF16)
        return carry

    lax.fori_loop(0, out.shape[0] // span_len, step, 0)


def combine_grad(position, pieces, rows, waits):
    groups = len(pieces)
    capacity, span_len, width = pieces[0].shape
    return pl.pallas_call(
        functools.partial(combine_grad_kernel, groups),
        out_shape=jax.ShapeDtypeStruct((rows, width), BF16),
        in_specs=[smem()] + [vmem()] * groups + [anyspace()] * len(waits),
        out_specs=vmem(),
        scratch_shapes=[pltpu.VMEM((groups * capacity, span_len, width), BF16)],
        compiler_params=params(16),
        cost_estimate=cost(TAIL_FLOPS, groups * pieces[0].size * 2 + rows * width * 2),
        name="combine_grad_queries",
    )(position, *pieces, *waits)


def combine_context_kernel(groups, position, place, *refs):
    pieces, stats = refs[:groups], refs[groups : 2 * groups]
    out, held, held_stats, shares = refs[2 * groups :]
    span_len, width = held.shape[1:]
    spans = out.shape[0] // span_len
    gather_groups(pieces, held)
    gather_groups(stats, held_stats)
    shares[...] = jnp.zeros_like(shares)
    for c in range(spans):
        first = held_stats[place[2 * c]][0:1]
        second = held_stats[place[2 * c + 1]][0:1]
        total = first + second
        shares[2 * c : 2 * c + 1, :] = first / total
        shares[2 * c + 1 : 2 * c + 2, :] = second / total
    columns = shares[...].T
    for c in range(spans):
        pair = [held[position[2 * c + i]] for i in range(2)]
        for h in range(width // HD):
            cols = slice(h * HD, (h + 1) * HD)
            part = columns[h * span_len : (h + 1) * span_len]
            total = sum(
                pair[i][:, cols].astype(F32) * part[:, 2 * c + i : 2 * c + i + 1] for i in range(2)
            )
            out[c * span_len : (c + 1) * span_len, cols] = total.astype(BF16)


def combine_context(position, place, pieces, stats, rows):
    groups = len(pieces)
    capacity, span_len, width = pieces[0].shape
    slots, two, lanes = stats[0].shape
    padded = -(-2 * (rows // span_len) // 128) * 128
    return pl.pallas_call(
        functools.partial(combine_context_kernel, groups),
        out_shape=jax.ShapeDtypeStruct((rows, width), BF16),
        in_specs=[smem()] * 2 + [vmem()] * (2 * groups),
        out_specs=vmem(),
        scratch_shapes=[
            pltpu.VMEM((groups * capacity, span_len, width), BF16),
            pltpu.VMEM((groups * slots, two, lanes), F32),
            pltpu.VMEM((padded, lanes), F32),
        ],
        compiler_params=params(24),
        cost_estimate=cost(rows * width * 4, groups * pieces[0].size * 2 + rows * width * 2),
        name="combine_context",
    )(position, place, *pieces, *stats)


def fill_diagonal(dst, block, heads, span_len):
    for h in range(heads):
        side = (h % 2) * HD
        dst[h * span_len : (h + 1) * span_len, side : side + HD] = block[:, h * HD : (h + 1) * HD]


def blocks_of(square, size):
    count = square.shape[0] // size
    return jnp.concatenate(
        [square[i * size : (i + 1) * size, i * size : (i + 1) * size] for i in range(count)], axis=1
    )


def on_diagonal(parts):
    zero = jnp.zeros_like(parts[0])
    return jnp.concatenate(
        [
            jnp.concatenate([part if j == i else zero for j in range(len(parts))], axis=1)
            for i, part in enumerate(parts)
        ],
        axis=0,
    )


def halves(wide, size):
    return [wide[:, i * size : (i + 1) * size] for i in range(wide.shape[1] // size)]


def store_heads(dst, k, both, span_len):
    for h in range(both.shape[0] // span_len):
        rows = slice(h * span_len, (h + 1) * span_len)
        side = (h % 2) * HD
        dst[k, :, h * HD : (h + 1) * HD] = both[rows, side : side + HD].astype(BF16)


def stacked(kv, nbr, first, pairs):
    return kv[nbr, first : first + pairs].reshape(pairs * kv.shape[2], kv.shape[3])


def slot_rows(qg, d, which, span_len):
    return qg[d, pl.ds(pl.multiple_of(which * span_len, span_len), span_len), :]


def safe_inverse(total):
    shrink = jnp.where(total > 2.0**100, 2.0**-64, 1.0)
    scaled = total * shrink
    return shrink, 1.0 / jnp.where(scaled > 0.0, scaled, 1.0)


def arrival(held, d, sems):
    return pltpu.make_async_copy(held.at[d], held.at[d], sems.at[d])


def local_kernel(groups, row_len, span_len, *refs):
    qg_refs, refs = refs[:groups], refs[groups:]
    (kv_ref, stats_ref), refs = refs[:2], refs[2:]
    ctx_refs, (counts, nbrs, partner), refs = refs[:groups], refs[groups : groups + 3], refs[groups + 3 :]
    kv, qg, ctx, heads_up, facts, plain, ksem, isem, hsem, osem = refs[:10]
    diag = refs[10:]
    rows, width = qg_refs[0].shape
    heads = width // HD
    capacity = (rows - HEADER) // (2 * span_len)
    slots = groups * capacity
    pairs = heads // 2
    unroll = min(UNROLL, capacity)
    factor = math.log2(math.e) / math.sqrt(HD)
    head_rows = pl.ds(rows - HEADER, HEADER)
    heads_in = fetch(
        [(ref.at[head_rows, pl.ds(0, 128)], heads_up.at[d]) for d, ref in enumerate(qg_refs)], hsem
    )
    kv_in = fetch([(kv_ref, kv)], ksem)
    fetch([(ref, qg.at[d]) for d, ref in enumerate(qg_refs)], isem)
    ctx_out = [pltpu.make_async_copy(ctx.at[d], ref, osem.at[d]) for d, ref in enumerate(ctx_refs)]
    for copy in heads_in:
        copy.wait()
    facts[...] = heads_up[...].astype(F32).astype(jnp.int32)
    to_scalar = pltpu.make_async_copy(facts, plain, osem.at[groups])
    to_scalar.start()
    for ref in diag:
        ref[...] = jnp.zeros_like(ref)
    to_scalar.wait()

    def unpack(j, carry):
        d, k = j // capacity, j % capacity
        nbrs[j] = plain[d, 0, k]
        partner[j] = plain[d, 1, k] * slots + plain[d, 2, k]
        return carry

    lax.fori_loop(0, slots, unpack, 0)
    for d in range(groups):
        counts[d] = plain[d, 3, 0]
    kv_in[0].wait()

    def one_group(d, carry):
        arrival(qg, d, isem).wait()

        def step(i, carry):
            for u in range(unroll):
                k = jnp.minimum(unroll * i + u, counts[d] - 1)
                j = d * capacity + k
                q_diag, g_diag = diag[2 * u], diag[2 * u + 1]
                fill_diagonal(q_diag, slot_rows(qg, d, 2 * k, span_len), heads, span_len)
                fill_diagonal(g_diag, slot_rows(qg, d, 2 * k + 1, span_len), heads, span_len)
                values = stacked(kv, nbrs[j], pairs, pairs)
                scores = mm(stacked(kv, nbrs[j], 0, pairs), q_diag[...], NT)
                expo = jnp.exp2(blocks_of(scores, row_len) * factor)
                grad_probs = blocks_of(mm(values, g_diag[...], NT), row_len)
                total = jnp.sum(expo, axis=0, keepdims=True)
                shrink, inverse = safe_inverse(total)
                probs = (expo * shrink) * inverse
                stats_ref[j, 0:1, :] = total
                stats_ref[j, 1:2, :] = jnp.sum(probs * grad_probs, axis=0, keepdims=True)
                turned = on_diagonal([x.T for x in halves(probs.astype(BF16), row_len)])
                store_heads(ctx.at[d], k, mm(turned, values, NN), span_len)
            return carry

        lax.fori_loop(0, (counts[d] + unroll - 1) // unroll, step, 0)
        for e in range(groups):

            @pl.when(d == e)
            def _():
                ctx_out[e].start()

        return carry

    lax.fori_loop(0, groups, one_group, 0)
    for copy in ctx_out:
        copy.wait()


def attend_local(qg, kv, row_len, span_len):
    groups = len(qg)
    rows, width = qg[0].shape
    capacity = (rows - HEADER) // (2 * span_len)
    slots = groups * capacity
    lanes = span_len * (width // HD)
    outs = pl.pallas_call(
        functools.partial(local_kernel, groups, row_len, span_len),
        out_shape=[jax.ShapeDtypeStruct((slots, 2, lanes), F32)]
        + [jax.ShapeDtypeStruct((capacity, span_len, width), BF16)] * groups
        + [jax.ShapeDtypeStruct((n,), jnp.int32) for n in (groups, slots, slots)],
        in_specs=[anyspace()] * (groups + 1),
        out_specs=[vmem()] + [anyspace()] * groups + [smem()] * 3,
        scratch_shapes=[
            pltpu.VMEM(kv.shape, BF16),
            pltpu.VMEM((groups, rows, width), BF16),
            pltpu.VMEM((groups, capacity, span_len, width), BF16),
            pltpu.VMEM((groups, HEADER, 128), BF16),
            pltpu.VMEM((groups, HEADER, 128), jnp.int32),
            pltpu.SMEM((groups, HEADER, 128), jnp.int32),
            pltpu.SemaphoreType.DMA((1,)),
            pltpu.SemaphoreType.DMA((groups,)),
            pltpu.SemaphoreType.DMA((groups,)),
            pltpu.SemaphoreType.DMA((groups + 1,)),
        ]
        + [pltpu.VMEM((lanes, 2 * HD), BF16)] * (2 * UNROLL),
        compiler_params=params(62),
        cost_estimate=cost(
            slots * 48 * row_len * lanes * HD,
            kv.size * 2 + slots * span_len * width * 6,
            slots * row_len * lanes,
        ),
        name="attend_local",
    )(*qg, kv)
    return outs[0], outs[1 : groups + 1], outs[groups + 1 :]


def grads_kernel(groups, row_len, span_len, counts, nbrs, partner, *refs):
    qg_refs, stat_refs, refs = refs[:groups], refs[groups : 2 * groups], refs[2 * groups :]
    (kv_ref, kw_ref, vw_ref), refs = refs[:3], refs[3:]
    gq_refs, (dkv_ref, part_ref), refs = refs[:groups], refs[groups : groups + 2], refs[groups + 2 :]
    kv, qg, stats, kw, vw, gq, acc, dkv, part, ksem, qsem, ssem, osem, psem = refs[:14]
    diag = refs[14:]
    width = qg_refs[0].shape[1]
    capacity = gq_refs[0].shape[0]
    slots = groups * capacity
    heads = width // HD
    scale = 1.0 / math.sqrt(HD)
    pairs = heads // 2
    unroll = min(UNROLL, capacity)
    factor = math.log2(math.e) * scale
    stats_in = fetch(
        [(ref, stats.at[pl.ds(d * slots, slots)]) for d, ref in enumerate(stat_refs)], ssem
    )
    (kv_in,) = fetch([(kv_ref, kv)], ksem)
    fetch([(ref, qg.at[d]) for d, ref in enumerate(qg_refs)], qsem)
    kw_in, vw_in = fetch([(kw_ref, kw), (vw_ref, vw)], ksem.at[pl.ds(1, 2)])
    gq_out = [
        pltpu.make_async_copy(gq.at[d, pl.ds(0, capacity)], ref, osem.at[d])
        for d, ref in enumerate(gq_refs)
    ]
    for ref in diag:
        ref[...] = jnp.zeros_like(ref)
    some = 4 if acc.shape[0] % 4 == 0 else 1
    block = some * row_len
    blocks = acc.shape[0] // some

    def rows_at(i):
        return pl.ds(pl.multiple_of(i * block, block), block)

    def clear(n, carry):
        acc[n] = jnp.zeros(acc.shape[1:], F32)
        return carry

    lax.fori_loop(0, acc.shape[0], clear, 0)
    for copy in [*stats_in, kv_in]:
        copy.wait()

    def one_group(d, carry):
        arrival(qg, d, qsem).wait()

        def step(i, carry):
            for u in range(unroll):
                place = unroll * i + u
                live = place < counts[d]
                k = jnp.minimum(place, counts[d] - 1)
                j = d * capacity + k
                q_diag, g_diag = diag[2 * u], diag[2 * u + 1]
                fill_diagonal(q_diag, slot_rows(qg, d, 2 * k, span_len), heads, span_len)
                fill_diagonal(g_diag, slot_rows(qg, d, 2 * k + 1, span_len), heads, span_len)
                nbr = nbrs[j]
                kept = jnp.where(live, k, capacity)
                own, other = stats[j], stats[partner[j]]
                total = own[0:1] + other[0:1]
                shrink, inverse = safe_inverse(total)
                shift = ((own[0:1] * shrink) * inverse) * own[1:2]
                shift += ((other[0:1] * shrink) * inverse) * other[1:2]
                inverse = jnp.where(live, inverse, 0.0)
                keys = stacked(kv, nbr, 0, pairs)
                expo = jnp.exp2(blocks_of(mm(keys, q_diag[...], NT), row_len) * factor) * shrink
                grad_probs = blocks_of(mm(stacked(kv, nbr, pairs, pairs), g_diag[...], NT), row_len)
                weights = expo * inverse
                mixed = halves((weights * (grad_probs - shift) * scale).astype(BF16), row_len)
                weights = halves(weights.astype(BF16), row_len)
                turned = on_diagonal([x.T for x in mixed])
                store_heads(gq.at[d], kept, mm(turned, keys, NN), span_len)
                shape = (pairs, row_len, 2 * HD)
                acc[nbr, :pairs] += mm(on_diagonal(mixed), q_diag[...], NN).reshape(shape)
                acc[nbr, pairs:] += mm(on_diagonal(weights), g_diag[...], NN).reshape(shape)
            return carry

        lax.fori_loop(0, (counts[d] + unroll - 1) // unroll, step, 0)
        for e in range(groups):

            @pl.when(d == e)
            def _():
                gq_out[e].start()

        return carry

    lax.fori_loop(0, groups, one_group, 0)
    kw_in.wait()
    vw_in.wait()

    def results(i):
        b = rows_at(i)
        return (
            pltpu.make_async_copy(part.at[b], part_ref.at[b], psem.at[i, 0]),
            pltpu.make_async_copy(dkv.at[b], dkv_ref.at[b], psem.at[i, 1]),
        )

    def narrow(i, carry):
        b = rows_at(i)
        for p in range(2 * pairs):
            part_of = acc[pl.ds(i * some, some), p].reshape(block, 2 * HD)
            dkv[b, p * 2 * HD : (p + 1) * 2 * HD] = part_of.astype(BF16)
        results(i)[1].start()
        return carry

    def finish(i, carry):
        b = rows_at(i)
        part[b, :] = (mm(dkv[b, :width], kw[...], NT) + mm(dkv[b, width:], vw[...], NT)).astype(BF16)
        results(i)[0].start()
        return carry

    def drain(i, carry):
        for copy in results(i):
            copy.wait()
        return carry

    lax.fori_loop(0, blocks, narrow, 0)
    lax.fori_loop(0, blocks, finish, 0)
    lax.fori_loop(0, blocks, drain, 0)
    for copy in gq_out:
        copy.wait()


def row_blocks(total, size):
    size = size if total % size == 0 else total
    return [pl.ds(i * size, size) for i in range(total // size)]


def attend_grads(lists, qg, stats, kv, key_weight, value_weight, row_len, span_len):
    groups = len(qg)
    width = qg[0].shape[1]
    capacity = (qg[0].shape[0] - HEADER) // (2 * span_len)
    slots = groups * capacity
    lanes = span_len * (width // HD)
    rows = kv.shape[0] * row_len
    feat = key_weight.shape[0]
    outs = pl.pallas_call(
        functools.partial(grads_kernel, groups, row_len, span_len),
        out_shape=[jax.ShapeDtypeStruct((capacity, span_len, width), BF16)] * groups
        + [
            jax.ShapeDtypeStruct((rows, 2 * width), BF16),
            jax.ShapeDtypeStruct((rows, feat), BF16),
        ],
        in_specs=[smem()] * 3 + [anyspace()] * (2 * groups + 3),
        out_specs=[anyspace()] * (groups + 2),
        scratch_shapes=[
            pltpu.VMEM(kv.shape, BF16),
            pltpu.VMEM((groups, *qg[0].shape), BF16),
            pltpu.VMEM((groups * slots, 2, lanes), F32),
            pltpu.VMEM((feat, width), BF16),
            pltpu.VMEM((feat, width), BF16),
            pltpu.VMEM((groups, capacity + 1, span_len, width), BF16),
            pltpu.VMEM(kv.shape, F32),
            pltpu.VMEM((rows, 2 * width), BF16),
            pltpu.VMEM((rows, feat), BF16),
            pltpu.SemaphoreType.DMA((3,)),
            pltpu.SemaphoreType.DMA((groups,)),
            pltpu.SemaphoreType.DMA((groups,)),
            pltpu.SemaphoreType.DMA((groups,)),
            pltpu.SemaphoreType.DMA((kv.shape[0], 2)),
        ]
        + [pltpu.VMEM((lanes, 2 * HD), BF16)] * (2 * UNROLL),
        compiler_params=params(62),
        cost_estimate=cost(
            4 * rows * feat * width + slots * 72 * row_len * lanes * HD,
            rows * feat * 2 + rows * width * 8 + slots * span_len * width * 6,
            slots * row_len * lanes,
        ),
        name="attend_grads",
    )(*lists, *qg, *stats, kv, key_weight, value_weight)
    return outs[:groups], outs[groups], outs[groups + 1]


def weight_kernel(groups, waits, me, table, dkv, *refs):
    piece_refs, total = refs[waits : waits + groups], refs[-1]
    share = total.shape[1]
    for cols in row_blocks(total.shape[2], 256):
        product = mm(table[...], dkv[:, cols], TN).astype(BF16)
        for e in range(groups):
            total[e, :, cols] = product[e * share : (e + 1) * share]
    for d, piece in enumerate(piece_refs):
        piece[...] = total[jnp.bitwise_xor(me[0], d)]


def grad_weights(me, table, grad_kv, groups, waits):
    feat, columns = table.shape[1], grad_kv.shape[1]
    return pl.pallas_call(
        functools.partial(weight_kernel, groups, len(waits)),
        out_shape=[jax.ShapeDtypeStruct((feat // groups, columns), BF16)] * groups,
        in_specs=[smem(), vmem(), vmem()] + [anyspace()] * len(waits),
        out_specs=[vmem()] * groups,
        scratch_shapes=[pltpu.VMEM((groups, feat // groups, columns), BF16)],
        compiler_params=params(62),
        cost_estimate=cost(WEIGHT_FLOPS, table.size * 2 + grad_kv.size * 2),
        name="grad_weights",
    )(me, table, grad_kv, *waits)


def body(
    queries,
    grad_ctx,
    neighbours,
    up_weight,
    down_weight,
    key_weight,
    value_weight,
    group_ids,
    slot_ids,
):
    groups = lax.axis_size("seq")
    if groups & (groups - 1):
        raise ValueError("seq size")
    me = lax.axis_index("seq").reshape(1)
    span_count = group_ids.shape[0]
    capacity = 2 * span_count // groups + 2
    width = queries.shape[1]
    span_len = queries.shape[0] // span_count
    own_count, row_len, feat = neighbours.shape
    table_len = own_count * lax.axis_size("ret")

    encoded_own = encode(neighbours, up_weight, down_weight)
    table = lax.all_gather(encoded_own, "ret", axis=0, tiled=True).reshape(-1, feat)
    outgoing, position, place = dispatch(
        me, group_ids.T, slot_ids.T, queries, grad_ctx, groups, capacity, span_len, [encoded_own]
    )
    arrived = exchange(outgoing, "seq")
    kv = project(table, key_weight, value_weight, row_len)
    own_stats, local_ctx, lists = attend_local(arrived, kv, row_len, span_len)
    stats = exchange([own_stats] * groups, "seq")
    ctx_back = exchange(local_ctx, "seq")
    local_gq, grad_kv, grad_table = attend_grads(
        lists, arrived, stats, kv, key_weight, value_weight, row_len, span_len
    )
    grad_encoded = lax.psum_scatter(
        grad_table.reshape(table_len, row_len, feat), "ret", scatter_dimension=0, tiled=True
    )
    gq_back = exchange(local_gq, "seq")
    pieces = exchange(
        grad_weights(me, table, grad_kv, groups, signs_of(*ctx_back[1:])), "seq"
    )
    grad_weight = sum(piece.astype(F32) for piece in pieces)
    context = combine_context(position, place, ctx_back, stats, queries.shape[0])
    grad_query = combine_grad(position, gq_back, queries.shape[0], [])
    return (context, grad_query, grad_encoded, grad_weight[:, :width], grad_weight[:, width:])


def solution(mesh):
    return jax.shard_map(
        body,
        mesh=mesh,
        in_specs=(
            P("seq", "ret"),
            P("seq", "ret"),
            P(("seq", "ret"), None, None),
            P(),
            P(),
            P(None, "ret"),
            P(None, "ret"),
            P("seq", None),
            P("seq", None),
        ),
        out_specs=(
            P("seq", "ret"),
            P("seq", "ret"),
            P(("seq", "ret"), None, None),
            P("seq", "ret"),
            P("seq", "ret"),
        ),
        check_vma=False,
    )
```

```python
import functools
import math

import jax
import jax.numpy as jnp
from jax import lax
from jax.experimental import pallas as pl
from jax.experimental.pallas import tpu as pltpu
from jax.sharding import PartitionSpec as P

HD = 128
HEADER = 16
UNROLL = 8
KV_COPIES = 4
TAIL_FLOPS = 32000000000
WEIGHT_FLOPS = 70000000000
NT = (((1,), (1,)), ((), ()))
NN = (((1,), (0,)), ((), ()))
TN = (((0,), (0,)), ((), ()))
BF16 = jnp.bfloat16
F32 = jnp.float32


def params(mib):
    return pltpu.CompilerParams(vmem_limit_bytes=mib * 1024 * 1024)


def vmem():
    return pl.BlockSpec(memory_space=pltpu.VMEM)


def anyspace():
    return pl.BlockSpec(memory_space=pl.ANY)


def smem():
    return pl.BlockSpec(memory_space=pltpu.SMEM)


def cost(flops, nbytes, trans=0):
    return pl.CostEstimate(flops=flops, bytes_accessed=nbytes, transcendentals=trans)


def mm(a, b, dims):
    return lax.dot_general(a, b, dims, preferred_element_type=F32)


def fetch(pairs, sems):
    copies = [pltpu.make_async_copy(src, dst, sems.at[i]) for i, (src, dst) in enumerate(pairs)]
    for copy in copies:
        copy.start()
    return copies


def encode_kernel(x_ref, up_ref, down_ref, out_ref, up, down, normed, acc, usem, dsem):
    steps, _, block = up.shape

    def copies(i):
        cols = pl.ds(pl.multiple_of(i * block, block), block)
        return (
            pltpu.make_async_copy(up_ref.at[:, cols], up.at[i], usem.at[i]),
            pltpu.make_async_copy(down_ref.at[cols, :], down.at[i], dsem.at[i]),
        )

    for i in range(steps):
        for copy in copies(i):
            copy.start()
    x = x_ref[...].astype(F32)
    normed[...] = (x * lax.rsqrt(jnp.mean(x * x, axis=-1, keepdims=True) + 1e-06)).astype(BF16)
    acc[...] = x

    def step(i, carry):
        up_in, down_in = copies(i)
        up_in.wait()
        h = mm(normed[...], up[i], NN)
        inner = math.sqrt(2.0 / math.pi) * (h + 0.044715 * (h * h * h))
        hidden = (0.5 * h * (1.0 + jnp.tanh(inner))).astype(BF16)
        down_in.wait()
        acc[...] += mm(hidden, down[i], NN)
        return carry

    lax.fori_loop(0, steps, step, 0)
    out_ref[...] = acc[...].astype(BF16)


def encode(neighbours, up_weight, down_weight):
    feat, hidden = up_weight.shape
    rows = neighbours.reshape(-1, feat)
    block = 896 if hidden % 896 == 0 else hidden
    steps = hidden // block
    return pl.pallas_call(
        encode_kernel,
        out_shape=jax.ShapeDtypeStruct(rows.shape, BF16),
        in_specs=[vmem(), anyspace(), anyspace()],
        out_specs=vmem(),
        scratch_shapes=[
            pltpu.VMEM((steps, feat, block), BF16),
            pltpu.VMEM((steps, block, feat), BF16),
            pltpu.VMEM(rows.shape, BF16),
            pltpu.VMEM(rows.shape, F32),
            pltpu.SemaphoreType.DMA((steps,)),
            pltpu.SemaphoreType.DMA((steps,)),
        ],
        compiler_params=params(62),
        cost_estimate=cost(4 * rows.shape[0] * feat * hidden, 4 * feat * hidden, rows.shape[0] * hidden),
        name="encode",
    )(rows, up_weight, down_weight).reshape(neighbours.shape)


def project_kernel(row_len, table_ref, kw_ref, vw_ref, *refs):
    kv_ref = refs[-1]
    pairs = kw_ref.shape[1] // (2 * HD)
    for first, weight in ((0, kw_ref), (pairs, vw_ref)):
        product = mm(table_ref[...], weight[...], NN).astype(BF16)
        for n in range(table_ref.shape[0] // row_len):
            for p in range(pairs):
                kv_ref[n, first + p] = product[
                    n * row_len : (n + 1) * row_len, p * 2 * HD : (p + 1) * 2 * HD
                ]


def project(table, key_weight, value_weight, row_len, waits):
    rows, feat = table.shape
    width = key_weight.shape[1]
    block = 512 if rows % 512 == 0 else rows
    blocks = 2 * width // (2 * HD)
    return pl.pallas_call(
        functools.partial(project_kernel, row_len),
        grid=(rows // block,),
        out_shape=jax.ShapeDtypeStruct((rows // row_len, blocks, row_len, 2 * HD), BF16),
        in_specs=[
            pl.BlockSpec((block, feat), lambda i: (i, 0)),
            pl.BlockSpec((feat, width), lambda i: (0, 0)),
            pl.BlockSpec((feat, width), lambda i: (0, 0)),
        ]
        + [anyspace()] * len(waits),
        out_specs=pl.BlockSpec((block // row_len, blocks, row_len, 2 * HD), lambda i: (i, 0, 0, 0)),
        compiler_params=params(59),
        cost_estimate=cost(8 * rows * feat * width, rows * (feat + 2 * width) * 2),
        name="project",
    )(table, key_weight, value_weight, *waits)


def exchange(pieces, axis):
    size = len(pieces)
    return [pieces[0]] + [
        lax.ppermute(pieces[d], axis, [(s, s ^ d) for s in range(size)]) for d in range(1, size)
    ]


def signs_of(*arrays):
    return [lax.slice(a, (0,) * a.ndim, (1,) * (a.ndim - 1) + (8,)) for a in arrays]


def dispatch_kernel(waits, me, group_ids, slot_ids, q_ref, g_ref, *refs):
    out_refs, refs = refs[waits:-7], refs[-7:]
    position, place, taken, info, header, sems, hsem = refs
    groups, rows = len(out_refs), out_refs[0].shape[0]
    requests = position.shape[0]
    span_len = q_ref.shape[0] // (requests // 2)
    capacity = (rows - HEADER) // (2 * span_len)
    slots = groups * capacity
    for d in range(groups):
        taken[d] = 0
    info[...] = jnp.zeros_like(info)

    def step(i, carry):
        span = i // 2
        offset = jnp.bitwise_xor(group_ids[i % 2, span], me[0])
        rank = taken[offset]
        taken[offset] = rank + 1
        position[i] = offset * capacity + rank
        place[i] = offset * slots + offset * capacity + rank
        source = pl.ds(pl.multiple_of(span * span_len, span_len), span_len)
        for e, out_ref in enumerate(out_refs):

            @pl.when(offset == e)
            def _():
                for half, ref in enumerate((q_ref, g_ref)):
                    first = pl.multiple_of((2 * rank + half) * span_len, span_len)
                    target = out_ref.at[pl.ds(first, span_len)]
                    pltpu.make_async_copy(ref.at[source], target, sems.at[i, half]).start()

        return carry

    lax.fori_loop(0, requests, step, 0)
    kind = lax.broadcasted_iota(jnp.int32, info.shape[1:], 0)
    lane = lax.broadcasted_iota(jnp.int32, info.shape[1:], 1)

    def note(i, carry):
        span, side = i // 2, i % 2
        target, other = group_ids[side, span], group_ids[1 - side, span]
        offset = jnp.bitwise_xor(target, me[0])
        rank = position[i] - offset * capacity
        there = position[2 * span + 1 - side]
        facts = jnp.where(
            kind == 0,
            slot_ids[side, span],
            jnp.where(kind == 1, jnp.bitwise_xor(target, other), jnp.where(kind == 2, there, 0)),
        )
        info[offset] = jnp.where((lane == rank) & (kind < 3), facts, info[offset])
        return carry

    lax.fori_loop(0, requests, note, 0)
    for d in range(groups):
        facts = jnp.where(kind == 3, taken[d], info[d]).astype(F32)
        header[d] = jnp.zeros(header.shape[1:], BF16)
        header[d, :, :128] = facts.astype(BF16)
    head_rows = pl.ds(rows - HEADER, HEADER)
    headers = fetch([(header.at[d], ref.at[head_rows]) for d, ref in enumerate(out_refs)], hsem)

    def drain(i, carry):
        some = pl.ds(0, span_len)
        for half, ref in enumerate((q_ref, g_ref)):
            pltpu.make_async_copy(ref.at[some], out_refs[0].at[some], sems.at[i, half]).wait()
        return carry

    lax.fori_loop(0, requests, drain, 0)
    for copy in headers:
        copy.wait()


def dispatch(me, group_ids, slot_ids, queries, grad_ctx, groups, capacity, span_len, waits):
    width = queries.shape[1]
    requests = group_ids.size
    piece = (capacity * 2 * span_len + HEADER, width)
    outs = pl.pallas_call(
        functools.partial(dispatch_kernel, len(waits)),
        out_shape=[jax.ShapeDtypeStruct(piece, BF16)] * groups
        + [jax.ShapeDtypeStruct((requests,), jnp.int32)] * 2,
        in_specs=[smem()] * 3 + [vmem()] * 2 + [anyspace()] * len(waits),
        out_specs=[anyspace()] * groups + [smem()] * 2,
        scratch_shapes=[
            pltpu.SMEM((groups,), jnp.int32),
            pltpu.VMEM((groups, HEADER, 128), jnp.int32),
            pltpu.VMEM((groups, HEADER, width), BF16),
            pltpu.SemaphoreType.DMA((requests, 2)),
            pltpu.SemaphoreType.DMA((groups,)),
        ],
        compiler_params=params(62),
        cost_estimate=cost(0, groups * capacity * span_len * width * 6),
        name="dispatch",
    )(me, group_ids, slot_ids, queries, grad_ctx, *waits)
    return outs[:groups], outs[groups], outs[groups + 1]


def gather_groups(refs, held):
    size = refs[0].shape[0]
    for d, ref in enumerate(refs):
        held[d * size : (d + 1) * size] = ref[...]


def combine_grad_kernel(groups, position, *refs):
    pieces, (out, held) = refs[:groups], refs[-2:]
    span_len = held.shape[1]
    gather_groups(pieces, held)

    def step(c, carry):
        rows = pl.ds(pl.multiple_of(c * span_len, span_len), span_len)
        first, second = held[position[2 * c]], held[position[2 * c + 1]]
        out[rows, :] = (first.astype(F32) + second.astype(F32)).astype(BF16)
        return carry

    lax.fori_loop(0, out.shape[0] // span_len, step, 0)


def combine_grad(position, pieces, rows, waits):
    groups = len(pieces)
    capacity, span_len, width = pieces[0].shape
    return pl.pallas_call(
        functools.partial(combine_grad_kernel, groups),
        out_shape=jax.ShapeDtypeStruct((rows, width), BF16),
        in_specs=[smem()] + [vmem()] * groups + [anyspace()] * len(waits),
        out_specs=vmem(),
        scratch_shapes=[pltpu.VMEM((groups * capacity, span_len, width), BF16)],
        compiler_params=params(16),
        cost_estimate=cost(TAIL_FLOPS, groups * pieces[0].size * 2 + rows * width * 2),
        name="combine_grad_queries",
    )(position, *pieces, *waits)


def combine_context_kernel(groups, position, place, *refs):
    pieces, stats = refs[:groups], refs[groups : 2 * groups]
    out, held, held_stats, shares = refs[2 * groups :]
    span_len, width = held.shape[1:]
    spans = out.shape[0] // span_len
    gather_groups(pieces, held)
    gather_groups(stats, held_stats)
    shares[...] = jnp.zeros_like(shares)
    for c in range(spans):
        first = held_stats[place[2 * c]][0:1]
        second = held_stats[place[2 * c + 1]][0:1]
        total = first + second
        shares[2 * c : 2 * c + 1, :] = first / total
        shares[2 * c + 1 : 2 * c + 2, :] = second / total
    columns = shares[...].T
    for c in range(spans):
        pair = [held[position[2 * c + i]] for i in range(2)]
        for h in range(width // HD):
            cols = slice(h * HD, (h + 1) * HD)
            part = columns[h * span_len : (h + 1) * span_len]
            total = sum(
                pair[i][:, cols].astype(F32) * part[:, 2 * c + i : 2 * c + i + 1] for i in range(2)
            )
            out[c * span_len : (c + 1) * span_len, cols] = total.astype(BF16)


def combine_context(position, place, pieces, stats, rows):
    groups = len(pieces)
    capacity, span_len, width = pieces[0].shape
    slots, two, lanes = stats[0].shape
    padded = -(-2 * (rows // span_len) // 128) * 128
    return pl.pallas_call(
        functools.partial(combine_context_kernel, groups),
        out_shape=jax.ShapeDtypeStruct((rows, width), BF16),
        in_specs=[smem()] * 2 + [vmem()] * (2 * groups),
        out_specs=vmem(),
        scratch_shapes=[
            pltpu.VMEM((groups * capacity, span_len, width), BF16),
            pltpu.VMEM((groups * slots, two, lanes), F32),
            pltpu.VMEM((padded, lanes), F32),
        ],
        compiler_params=params(24),
        cost_estimate=cost(rows * width * 4, groups * pieces[0].size * 2 + rows * width * 2),
        name="combine_context",
    )(position, place, *pieces, *stats)


def fill_diagonal(dst, block, heads, span_len):
    for h in range(heads):
        side = (h % 2) * HD
        dst[h * span_len : (h + 1) * span_len, side : side + HD] = block[:, h * HD : (h + 1) * HD]


def blocks_of(square, size):
    count = square.shape[0] // size
    return jnp.concatenate(
        [square[i * size : (i + 1) * size, i * size : (i + 1) * size] for i in range(count)], axis=1
    )


def on_diagonal(parts):
    zero = jnp.zeros_like(parts[0])
    return jnp.concatenate(
        [
            jnp.concatenate([part if j == i else zero for j in range(len(parts))], axis=1)
            for i, part in enumerate(parts)
        ],
        axis=0,
    )


def halves(wide, size):
    return [wide[:, i * size : (i + 1) * size] for i in range(wide.shape[1] // size)]


def store_heads(dst, k, both, span_len):
    for h in range(both.shape[0] // span_len):
        rows = slice(h * span_len, (h + 1) * span_len)
        side = (h % 2) * HD
        dst[k, :, h * HD : (h + 1) * HD] = both[rows, side : side + HD].astype(BF16)


def stacked(kv, nbr, first, pairs):
    return kv[nbr, first : first + pairs].reshape(pairs * kv.shape[2], kv.shape[3])


def slot_rows(qg, d, which, span_len):
    return qg[d, pl.ds(pl.multiple_of(which * span_len, span_len), span_len), :]


def safe_inverse(total):
    shrink = jnp.where(total > 2.0**100, 2.0**-64, 1.0)
    scaled = total * shrink
    return shrink, 1.0 / jnp.where(scaled > 0.0, scaled, 1.0)


def quarters(src, dst):
    size = max(1, src.shape[0] // KV_COPIES)
    return [(src.at[pl.ds(i, size)], dst.at[pl.ds(i, size)]) for i in range(0, src.shape[0], size)]


def arrival(held, d, sems):
    return pltpu.make_async_copy(held.at[d], held.at[d], sems.at[d])


def local_kernel(groups, row_len, span_len, *refs):
    qg_refs, refs = refs[:groups], refs[groups:]
    (kv_ref, stats_ref), refs = refs[:2], refs[2:]
    ctx_refs, (counts, nbrs, partner), refs = refs[:groups], refs[groups : groups + 3], refs[groups + 3 :]
    kv, qg, ctx, heads_up, facts, plain, ksem, isem, hsem, osem = refs[:10]
    diag = refs[10:]
    rows, width = qg_refs[0].shape
    heads = width // HD
    capacity = (rows - HEADER) // (2 * span_len)
    slots = groups * capacity
    pairs = heads // 2
    unroll = min(UNROLL, capacity)
    factor = math.log2(math.e) / math.sqrt(HD)
    head_rows = pl.ds(rows - HEADER, HEADER)
    heads_in = fetch(
        [(ref.at[head_rows, pl.ds(0, 128)], heads_up.at[d]) for d, ref in enumerate(qg_refs)], hsem
    )
    kv_in = fetch(quarters(kv_ref, kv), ksem)
    fetch([(qg_refs[0], qg.at[0])], isem)
    ctx_out = [pltpu.make_async_copy(ctx.at[d], ref, osem.at[d]) for d, ref in enumerate(ctx_refs)]
    for copy in heads_in:
        copy.wait()
    facts[...] = heads_up[...].astype(F32).astype(jnp.int32)
    to_scalar = pltpu.make_async_copy(facts, plain, osem.at[groups])
    to_scalar.start()
    for ref in diag:
        ref[...] = jnp.zeros_like(ref)
    to_scalar.wait()

    def unpack(j, carry):
        d, k = j // capacity, j % capacity
        nbrs[j] = plain[d, 0, k]
        partner[j] = plain[d, 1, k] * slots + plain[d, 2, k]
        return carry

    lax.fori_loop(0, slots, unpack, 0)
    for d in range(groups):
        counts[d] = plain[d, 3, 0]
    for copy in kv_in:
        copy.wait()
    fetch([(ref, qg.at[d + 1]) for d, ref in enumerate(qg_refs[1:])], isem.at[pl.ds(1, groups - 1)])

    def one_group(d, carry):
        arrival(qg, d, isem).wait()

        def step(i, carry):
            for u in range(unroll):
                k = jnp.minimum(unroll * i + u, counts[d] - 1)
                j = d * capacity + k
                q_diag, g_diag = diag[2 * u], diag[2 * u + 1]
                fill_diagonal(q_diag, slot_rows(qg, d, 2 * k, span_len), heads, span_len)
                fill_diagonal(g_diag, slot_rows(qg, d, 2 * k + 1, span_len), heads, span_len)
                values = stacked(kv, nbrs[j], pairs, pairs)
                scores = mm(stacked(kv, nbrs[j], 0, pairs), q_diag[...], NT)
                expo = jnp.exp2(blocks_of(scores, row_len) * factor)
                grad_probs = blocks_of(mm(values, g_diag[...], NT), row_len)
                total = jnp.sum(expo, axis=0, keepdims=True)
                shrink, inverse = safe_inverse(total)
                probs = (expo * shrink) * inverse
                stats_ref[j, 0:1, :] = total
                stats_ref[j, 1:2, :] = jnp.sum(probs * grad_probs, axis=0, keepdims=True)
                turned = on_diagonal([x.T for x in halves(probs.astype(BF16), row_len)])
                store_heads(ctx.at[d], k, mm(turned, values, NN), span_len)
            return carry

        lax.fori_loop(0, (counts[d] + unroll - 1) // unroll, step, 0)
        for e in range(groups):

            @pl.when(d == e)
            def _():
                ctx_out[e].start()

        return carry

    lax.fori_loop(0, groups, one_group, 0)
    for copy in ctx_out:
        copy.wait()


def attend_local(qg, kv, row_len, span_len):
    groups = len(qg)
    rows, width = qg[0].shape
    capacity = (rows - HEADER) // (2 * span_len)
    slots = groups * capacity
    lanes = span_len * (width // HD)
    outs = pl.pallas_call(
        functools.partial(local_kernel, groups, row_len, span_len),
        out_shape=[jax.ShapeDtypeStruct((slots, 2, lanes), F32)]
        + [jax.ShapeDtypeStruct((capacity, span_len, width), BF16)] * groups
        + [jax.ShapeDtypeStruct((n,), jnp.int32) for n in (groups, slots, slots)],
        in_specs=[anyspace()] * (groups + 1),
        out_specs=[vmem()] + [anyspace()] * groups + [smem()] * 3,
        scratch_shapes=[
            pltpu.VMEM(kv.shape, BF16),
            pltpu.VMEM((groups, rows, width), BF16),
            pltpu.VMEM((groups, capacity, span_len, width), BF16),
            pltpu.VMEM((groups, HEADER, 128), BF16),
            pltpu.VMEM((groups, HEADER, 128), jnp.int32),
            pltpu.SMEM((groups, HEADER, 128), jnp.int32),
            pltpu.SemaphoreType.DMA((kv.shape[0],)),
            pltpu.SemaphoreType.DMA((groups,)),
            pltpu.SemaphoreType.DMA((groups,)),
            pltpu.SemaphoreType.DMA((groups + 1,)),
        ]
        + [pltpu.VMEM((lanes, 2 * HD), BF16)] * (2 * UNROLL),
        compiler_params=params(62),
        cost_estimate=cost(
            slots * 48 * row_len * lanes * HD,
            kv.size * 2 + slots * span_len * width * 6,
            slots * row_len * lanes,
        ),
        name="attend_local",
    )(*qg, kv)
    return outs[0], outs[1 : groups + 1], outs[groups + 1 :]


def grads_kernel(groups, row_len, span_len, counts, nbrs, partner, *refs):
    qg_refs, stat_refs, refs = refs[:groups], refs[groups : 2 * groups], refs[2 * groups :]
    (kv_ref, kw_ref, vw_ref), refs = refs[:3], refs[3:]
    gq_refs, (dkv_ref, part_ref), refs = refs[:groups], refs[groups : groups + 2], refs[groups + 2 :]
    kv, qg, stats, kw, vw, gq, acc, dkv, part, ksem, qsem, ssem, osem, psem = refs[:14]
    diag = refs[14:]
    width = qg_refs[0].shape[1]
    capacity = gq_refs[0].shape[0]
    heads = width // HD
    scale = 1.0 / math.sqrt(HD)
    pairs = heads // 2
    unroll = min(UNROLL, capacity)
    factor = math.log2(math.e) * scale
    kv_in = fetch(quarters(kv_ref, kv), ksem)
    fetch([(qg_refs[0], qg.at[0])], qsem)
    gq_out = [
        pltpu.make_async_copy(gq.at[d, pl.ds(0, capacity)], ref, osem.at[d])
        for d, ref in enumerate(gq_refs)
    ]
    for ref in diag:
        ref[...] = jnp.zeros_like(ref)
    some = 4 if acc.shape[0] % 4 == 0 else 1
    block = some * row_len
    blocks = acc.shape[0] // some

    def rows_at(i):
        return pl.ds(pl.multiple_of(i * block, block), block)

    def clear(n, carry):
        acc[n] = jnp.zeros(acc.shape[1:], F32)
        return carry

    lax.fori_loop(0, acc.shape[0], clear, 0)
    gather_groups(stat_refs, stats)
    for copy in kv_in:
        copy.wait()
    fetch([(ref, qg.at[d + 1]) for d, ref in enumerate(qg_refs[1:])], qsem.at[pl.ds(1, groups - 1)])
    weights_in = fetch([(kw_ref, kw), (vw_ref, vw)], ssem)

    def one_group(d, carry):
        arrival(qg, d, qsem).wait()

        def step(i, carry):
            for u in range(unroll):
                place = unroll * i + u
                live = place < counts[d]
                k = jnp.minimum(place, counts[d] - 1)
                j = d * capacity + k
                q_diag, g_diag = diag[2 * u], diag[2 * u + 1]
                fill_diagonal(q_diag, slot_rows(qg, d, 2 * k, span_len), heads, span_len)
                fill_diagonal(g_diag, slot_rows(qg, d, 2 * k + 1, span_len), heads, span_len)
                nbr = nbrs[j]
                kept = jnp.where(live, k, capacity)
                own, other = stats[j], stats[partner[j]]
                total = own[0:1] + other[0:1]
                shrink, inverse = safe_inverse(total)
                shift = ((own[0:1] * shrink) * inverse) * own[1:2]
                shift += ((other[0:1] * shrink) * inverse) * other[1:2]
                inverse = jnp.where(live, inverse, 0.0)
                keys = stacked(kv, nbr, 0, pairs)
                expo = jnp.exp2(blocks_of(mm(keys, q_diag[...], NT), row_len) * factor) * shrink
                grad_probs = blocks_of(mm(stacked(kv, nbr, pairs, pairs), g_diag[...], NT), row_len)
                weights = expo * inverse
                mixed = halves((weights * (grad_probs - shift) * scale).astype(BF16), row_len)
                weights = halves(weights.astype(BF16), row_len)
                turned = on_diagonal([x.T for x in mixed])
                store_heads(gq.at[d], kept, mm(turned, keys, NN), span_len)
                shape = (pairs, row_len, 2 * HD)
                acc[nbr, :pairs] += mm(on_diagonal(mixed), q_diag[...], NN).reshape(shape)
                acc[nbr, pairs:] += mm(on_diagonal(weights), g_diag[...], NN).reshape(shape)
            return carry

        lax.fori_loop(0, (counts[d] + unroll - 1) // unroll, step, 0)
        for e in range(groups):

            @pl.when(d == e)
            def _():
                gq_out[e].start()

        return carry

    lax.fori_loop(0, groups, one_group, 0)
    for copy in weights_in:
        copy.wait()

    def results(i):
        b = rows_at(i)
        return (
            pltpu.make_async_copy(part.at[b], part_ref.at[b], psem.at[i, 0]),
            pltpu.make_async_copy(dkv.at[b], dkv_ref.at[b], psem.at[i, 1]),
        )

    def narrow(i, carry):
        b = rows_at(i)
        for p in range(2 * pairs):
            part_of = acc[pl.ds(i * some, some), p].reshape(block, 2 * HD)
            dkv[b, p * 2 * HD : (p + 1) * 2 * HD] = part_of.astype(BF16)
        results(i)[1].start()
        return carry

    def finish(i, carry):
        b = rows_at(i)
        part[b, :] = (mm(dkv[b, :width], kw[...], NN) + mm(dkv[b, width:], vw[...], NN)).astype(BF16)
        results(i)[0].start()
        return carry

    def drain(i, carry):
        for copy in results(i):
            copy.wait()
        return carry

    lax.fori_loop(0, blocks, narrow, 0)
    lax.fori_loop(0, blocks, finish, 0)
    lax.fori_loop(0, blocks, drain, 0)
    for copy in gq_out:
        copy.wait()


def row_blocks(total, size):
    size = size if total % size == 0 else total
    return [pl.ds(i * size, size) for i in range(total // size)]


def attend_grads(lists, qg, stats, kv, key_weight, value_weight, row_len, span_len):
    groups = len(qg)
    width = qg[0].shape[1]
    capacity = (qg[0].shape[0] - HEADER) // (2 * span_len)
    slots = groups * capacity
    lanes = span_len * (width // HD)
    rows = kv.shape[0] * row_len
    feat = key_weight.shape[1]
    outs = pl.pallas_call(
        functools.partial(grads_kernel, groups, row_len, span_len),
        out_shape=[jax.ShapeDtypeStruct((capacity, span_len, width), BF16)] * groups
        + [
            jax.ShapeDtypeStruct((rows, 2 * width), BF16),
            jax.ShapeDtypeStruct((rows, feat), BF16),
        ],
        in_specs=[smem()] * 3 + [anyspace()] * groups + [vmem()] * groups + [anyspace()] * 3,
        out_specs=[anyspace()] * (groups + 2),
        scratch_shapes=[
            pltpu.VMEM(kv.shape, BF16),
            pltpu.VMEM((groups, *qg[0].shape), BF16),
            pltpu.VMEM((groups * slots, 2, lanes), F32),
            pltpu.VMEM((width, feat), BF16),
            pltpu.VMEM((width, feat), BF16),
            pltpu.VMEM((groups, capacity + 1, span_len, width), BF16),
            pltpu.VMEM(kv.shape, F32),
            pltpu.VMEM((rows, 2 * width), BF16),
            pltpu.VMEM((rows, feat), BF16),
            pltpu.SemaphoreType.DMA((kv.shape[0],)),
            pltpu.SemaphoreType.DMA((groups,)),
            pltpu.SemaphoreType.DMA((2,)),
            pltpu.SemaphoreType.DMA((groups,)),
            pltpu.SemaphoreType.DMA((kv.shape[0], 2)),
        ]
        + [pltpu.VMEM((lanes, 2 * HD), BF16)] * (2 * UNROLL),
        compiler_params=params(62),
        cost_estimate=cost(
            4 * rows * feat * width + slots * 72 * row_len * lanes * HD,
            rows * feat * 2 + rows * width * 8 + slots * span_len * width * 6,
            slots * row_len * lanes,
        ),
        name="attend_grads",
    )(*lists, *qg, *stats, kv, key_weight, value_weight)
    return outs[:groups], outs[groups], outs[groups + 1]


def weight_kernel(groups, waits, me, table, dkv, *refs):
    piece_refs, total = refs[waits : waits + groups], refs[-1]
    share = total.shape[1]
    for cols in row_blocks(total.shape[2], 256):
        product = mm(table[...], dkv[:, cols], TN).astype(BF16)
        for e in range(groups):
            total[e, :, cols] = product[e * share : (e + 1) * share]
    for d, piece in enumerate(piece_refs):
        piece[...] = total[jnp.bitwise_xor(me[0], d)]


def grad_weights(me, table, grad_kv, groups, waits):
    feat, columns = table.shape[1], grad_kv.shape[1]
    return pl.pallas_call(
        functools.partial(weight_kernel, groups, len(waits)),
        out_shape=[jax.ShapeDtypeStruct((feat // groups, columns), BF16)] * groups,
        in_specs=[smem(), vmem(), vmem()] + [anyspace()] * len(waits),
        out_specs=[vmem()] * groups,
        scratch_shapes=[pltpu.VMEM((groups, feat // groups, columns), BF16)],
        compiler_params=params(62),
        cost_estimate=cost(WEIGHT_FLOPS, table.size * 2 + grad_kv.size * 2),
        name="grad_weights",
    )(me, table, grad_kv, *waits)


def body(
    queries,
    grad_ctx,
    neighbours,
    up_weight,
    down_weight,
    key_weight,
    value_weight,
    group_ids,
    slot_ids,
):
    groups = lax.axis_size("seq")
    if groups & (groups - 1):
        raise ValueError("seq size")
    me = lax.axis_index("seq").reshape(1)
    span_count = group_ids.shape[0]
    capacity = 2 * span_count // groups + 2
    width = queries.shape[1]
    span_len = queries.shape[0] // span_count
    own_count, row_len, feat = neighbours.shape
    table_len = own_count * lax.axis_size("ret")

    encoded_own = encode(neighbours, up_weight, down_weight)
    table = lax.all_gather(encoded_own, "ret", axis=0, tiled=True).reshape(-1, feat)
    outgoing, position, place = dispatch(
        me, group_ids.T, slot_ids.T, queries, grad_ctx, groups, capacity, span_len, [encoded_own]
    )
    arrived = exchange(outgoing, "seq")
    turned = [key_weight.T, value_weight.T]
    kv = project(table, key_weight, value_weight, row_len, turned)
    own_stats, local_ctx, lists = attend_local(arrived, kv, row_len, span_len)
    stats = exchange([own_stats] * groups, "seq")
    ctx_back = exchange(local_ctx, "seq")
    local_gq, grad_kv, grad_table = attend_grads(
        lists, arrived, stats, kv, *turned, row_len, span_len
    )
    grad_encoded = lax.psum_scatter(
        grad_table.reshape(table_len, row_len, feat), "ret", scatter_dimension=0, tiled=True
    )
    gq_back = exchange(local_gq, "seq")
    pieces = exchange(
        grad_weights(me, table, grad_kv, groups, signs_of(*ctx_back[1:])), "seq"
    )
    grad_weight = sum(piece.astype(F32) for piece in pieces)
    context = combine_context(position, place, ctx_back, stats, queries.shape[0])
    grad_query = combine_grad(position, gq_back, queries.shape[0], [])
    return (context, grad_query, grad_encoded, grad_weight[:, :width], grad_weight[:, width:])


def solution(mesh):
    return jax.shard_map(
        body,
        mesh=mesh,
        in_specs=(
            P("seq", "ret"),
            P("seq", "ret"),
            P(("seq", "ret"), None, None),
            P(),
            P(),
            P(None, "ret"),
            P(None, "ret"),
            P("seq", None),
            P("seq", None),
        ),
        out_specs=(
            P("seq", "ret"),
            P("seq", "ret"),
            P(("seq", "ret"), None, None),
            P("seq", "ret"),
            P("seq", "ret"),
        ),
        check_vma=False,
    )
```

```python
import functools
import math

import jax
import jax.numpy as jnp
from jax import lax
from jax.experimental import pallas as pl
from jax.experimental.pallas import tpu as pltpu
from jax.sharding import PartitionSpec as P

HD = 128
HEADER = 16
UNROLL = 8
KV_COPIES = 4
TAIL_FLOPS = 32000000000
WEIGHT_FLOPS = 70000000000
NT = (((1,), (1,)), ((), ()))
NN = (((1,), (0,)), ((), ()))
TN = (((0,), (0,)), ((), ()))
BF16 = jnp.bfloat16
F32 = jnp.float32


def params(mib):
    return pltpu.CompilerParams(vmem_limit_bytes=mib * 1024 * 1024)


def vmem():
    return pl.BlockSpec(memory_space=pltpu.VMEM)


def anyspace():
    return pl.BlockSpec(memory_space=pl.ANY)


def smem():
    return pl.BlockSpec(memory_space=pltpu.SMEM)


def cost(flops, nbytes, trans=0):
    return pl.CostEstimate(flops=flops, bytes_accessed=nbytes, transcendentals=trans)


def mm(a, b, dims):
    return lax.dot_general(a, b, dims, preferred_element_type=F32)


def fetch(pairs, sems):
    copies = [pltpu.make_async_copy(src, dst, sems.at[i]) for i, (src, dst) in enumerate(pairs)]
    for copy in copies:
        copy.start()
    return copies


def encode_kernel(x_ref, up_ref, down_ref, out_ref, up, down, normed, acc, usem, dsem):
    steps, _, block = up.shape

    def copies(i):
        cols = pl.ds(pl.multiple_of(i * block, block), block)
        return (
            pltpu.make_async_copy(up_ref.at[:, cols], up.at[i], usem.at[i]),
            pltpu.make_async_copy(down_ref.at[cols, :], down.at[i], dsem.at[i]),
        )

    for i in range(steps):
        for copy in copies(i):
            copy.start()
    x = x_ref[...].astype(F32)
    normed[...] = (x * lax.rsqrt(jnp.mean(x * x, axis=-1, keepdims=True) + 1e-06)).astype(BF16)
    acc[...] = x

    middle = min(512, block)
    parts = [(0, middle), (middle, block)] if middle < block else [(0, block)]

    def step(i, carry):
        up_in, down_in = copies(i)
        up_in.wait()
        sums = [mm(normed[...], up[i, :, first:last], NN) for first, last in parts]
        down_in.wait()
        total = acc[...]
        for h, (first, last) in zip(sums, parts):
            inner = math.sqrt(2.0 / math.pi) * (h + 0.044715 * (h * h * h))
            hidden = (0.5 * h * (1.0 + jnp.tanh(inner))).astype(BF16)
            total += mm(hidden, down[i, first:last, :], NN)
        acc[...] = total
        return carry

    lax.fori_loop(0, steps, step, 0)
    out_ref[...] = acc[...].astype(BF16)


def encode(neighbours, up_weight, down_weight):
    feat, hidden = up_weight.shape
    rows = neighbours.reshape(-1, feat)
    block = 896 if hidden % 896 == 0 else hidden
    steps = hidden // block
    return pl.pallas_call(
        encode_kernel,
        out_shape=jax.ShapeDtypeStruct(rows.shape, BF16),
        in_specs=[vmem(), anyspace(), anyspace()],
        out_specs=vmem(),
        scratch_shapes=[
            pltpu.VMEM((steps, feat, block), BF16),
            pltpu.VMEM((steps, block, feat), BF16),
            pltpu.VMEM(rows.shape, BF16),
            pltpu.VMEM(rows.shape, F32),
            pltpu.SemaphoreType.DMA((steps,)),
            pltpu.SemaphoreType.DMA((steps,)),
        ],
        compiler_params=params(58),
        cost_estimate=cost(4 * rows.shape[0] * feat * hidden, 4 * feat * hidden, rows.shape[0] * hidden),
        name="encode",
    )(rows, up_weight, down_weight).reshape(neighbours.shape)


def project_kernel(row_len, table_ref, kw_ref, vw_ref, *refs):
    kv_ref = refs[-1]
    pairs = kw_ref.shape[1] // (2 * HD)
    for first, weight in ((0, kw_ref), (pairs, vw_ref)):
        product = mm(table_ref[...], weight[...], NN).astype(BF16)
        for n in range(table_ref.shape[0] // row_len):
            for p in range(pairs):
                kv_ref[n, first + p] = product[
                    n * row_len : (n + 1) * row_len, p * 2 * HD : (p + 1) * 2 * HD
                ]


def project(table, key_weight, value_weight, row_len, waits):
    rows, feat = table.shape
    width = key_weight.shape[1]
    block = 512 if rows % 512 == 0 else rows
    blocks = 2 * width // (2 * HD)
    return pl.pallas_call(
        functools.partial(project_kernel, row_len),
        grid=(rows // block,),
        out_shape=jax.ShapeDtypeStruct((rows // row_len, blocks, row_len, 2 * HD), BF16),
        in_specs=[
            pl.BlockSpec((block, feat), lambda i: (i, 0)),
            pl.BlockSpec((feat, width), lambda i: (0, 0)),
            pl.BlockSpec((feat, width), lambda i: (0, 0)),
        ]
        + [anyspace()] * len(waits),
        out_specs=pl.BlockSpec((block // row_len, blocks, row_len, 2 * HD), lambda i: (i, 0, 0, 0)),
        compiler_params=params(59),
        cost_estimate=cost(8 * rows * feat * width, rows * (feat + 2 * width) * 2),
        name="project",
    )(table, key_weight, value_weight, *waits)


def exchange(pieces, axis):
    size = len(pieces)
    return [pieces[0]] + [
        lax.ppermute(pieces[d], axis, [(s, s ^ d) for s in range(size)]) for d in range(1, size)
    ]


def signs_of(*arrays):
    return [lax.slice(a, (0,) * a.ndim, (1,) * (a.ndim - 1) + (8,)) for a in arrays]


def dispatch_kernel(waits, me, group_ids, slot_ids, q_ref, g_ref, *refs):
    out_refs, refs = refs[waits:-7], refs[-7:]
    position, place, taken, info, header, sems, hsem = refs
    groups, rows = len(out_refs), out_refs[0].shape[0]
    requests = position.shape[0]
    span_len = q_ref.shape[0] // (requests // 2)
    capacity = (rows - HEADER) // (2 * span_len)
    slots = groups * capacity
    for d in range(groups):
        taken[d] = 0
    info[...] = jnp.zeros_like(info)

    def step(i, carry):
        span = i // 2
        offset = jnp.bitwise_xor(group_ids[i % 2, span], me[0])
        rank = taken[offset]
        taken[offset] = rank + 1
        position[i] = offset * capacity + rank
        place[i] = offset * slots + offset * capacity + rank
        source = pl.ds(pl.multiple_of(span * span_len, span_len), span_len)
        for e, out_ref in enumerate(out_refs):

            @pl.when(offset == e)
            def _():
                for half, ref in enumerate((q_ref, g_ref)):
                    first = pl.multiple_of((2 * rank + half) * span_len, span_len)
                    target = out_ref.at[pl.ds(first, span_len)]
                    pltpu.make_async_copy(ref.at[source], target, sems.at[i, half]).start()

        return carry

    lax.fori_loop(0, requests, step, 0)
    kind = lax.broadcasted_iota(jnp.int32, info.shape[1:], 0)
    lane = lax.broadcasted_iota(jnp.int32, info.shape[1:], 1)

    def note(i, carry):
        span, side = i // 2, i % 2
        target, other = group_ids[side, span], group_ids[1 - side, span]
        offset = jnp.bitwise_xor(target, me[0])
        rank = position[i] - offset * capacity
        there = position[2 * span + 1 - side]
        facts = jnp.where(
            kind == 0,
            slot_ids[side, span],
            jnp.where(kind == 1, jnp.bitwise_xor(target, other), jnp.where(kind == 2, there, 0)),
        )
        info[offset] = jnp.where((lane == rank) & (kind < 3), facts, info[offset])
        return carry

    lax.fori_loop(0, requests, note, 0)
    for d in range(groups):
        facts = jnp.where(kind == 3, taken[d], info[d]).astype(F32)
        header[d] = jnp.zeros(header.shape[1:], BF16)
        header[d, :, :128] = facts.astype(BF16)
    head_rows = pl.ds(rows - HEADER, HEADER)
    headers = fetch([(header.at[d], ref.at[head_rows]) for d, ref in enumerate(out_refs)], hsem)

    def drain(i, carry):
        some = pl.ds(0, span_len)
        for half, ref in enumerate((q_ref, g_ref)):
            pltpu.make_async_copy(ref.at[some], out_refs[0].at[some], sems.at[i, half]).wait()
        return carry

    lax.fori_loop(0, requests, drain, 0)
    for copy in headers:
        copy.wait()


def dispatch(me, group_ids, slot_ids, queries, grad_ctx, groups, capacity, span_len, waits):
    width = queries.shape[1]
    requests = group_ids.size
    piece = (capacity * 2 * span_len + HEADER, width)
    outs = pl.pallas_call(
        functools.partial(dispatch_kernel, len(waits)),
        out_shape=[jax.ShapeDtypeStruct(piece, BF16)] * groups
        + [jax.ShapeDtypeStruct((requests,), jnp.int32)] * 2,
        in_specs=[smem()] * 3 + [vmem()] * 2 + [anyspace()] * len(waits),
        out_specs=[anyspace()] * groups + [smem()] * 2,
        scratch_shapes=[
            pltpu.SMEM((groups,), jnp.int32),
            pltpu.VMEM((groups, HEADER, 128), jnp.int32),
            pltpu.VMEM((groups, HEADER, width), BF16),
            pltpu.SemaphoreType.DMA((requests, 2)),
            pltpu.SemaphoreType.DMA((groups,)),
        ],
        compiler_params=params(16),
        cost_estimate=cost(0, groups * capacity * span_len * width * 6),
        name="dispatch",
    )(me, group_ids, slot_ids, queries, grad_ctx, *waits)
    return outs[:groups], outs[groups], outs[groups + 1]


def gather_groups(refs, held):
    size = refs[0].shape[0]
    for d, ref in enumerate(refs):
        held[d * size : (d + 1) * size] = ref[...]


def combine_grad_kernel(groups, position, *refs):
    pieces, (out, held) = refs[:groups], refs[-2:]
    span_len = held.shape[1]
    gather_groups(pieces, held)

    def step(c, carry):
        rows = pl.ds(pl.multiple_of(c * span_len, span_len), span_len)
        first, second = held[position[2 * c]], held[position[2 * c + 1]]
        out[rows, :] = (first.astype(F32) + second.astype(F32)).astype(BF16)
        return carry

    lax.fori_loop(0, out.shape[0] // span_len, step, 0)


def combine_grad(position, pieces, rows, waits):
    groups = len(pieces)
    capacity, span_len, width = pieces[0].shape
    return pl.pallas_call(
        functools.partial(combine_grad_kernel, groups),
        out_shape=jax.ShapeDtypeStruct((rows, width), BF16),
        in_specs=[smem()] + [vmem()] * groups + [anyspace()] * len(waits),
        out_specs=vmem(),
        scratch_shapes=[pltpu.VMEM((groups * capacity, span_len, width), BF16)],
        compiler_params=params(16),
        cost_estimate=cost(TAIL_FLOPS, groups * pieces[0].size * 2 + rows * width * 2),
        name="combine_grad_queries",
    )(position, *pieces, *waits)


def combine_context_kernel(groups, position, place, *refs):
    pieces, stats = refs[:groups], refs[groups : 2 * groups]
    out, held, held_stats, shares = refs[2 * groups :]
    span_len, width = held.shape[1:]
    spans = out.shape[0] // span_len
    gather_groups(pieces, held)
    gather_groups(stats, held_stats)
    shares[...] = jnp.zeros_like(shares)
    for c in range(spans):
        first = held_stats[place[2 * c]][0:1]
        second = held_stats[place[2 * c + 1]][0:1]
        total = first + second
        shares[2 * c : 2 * c + 1, :] = first / total
        shares[2 * c + 1 : 2 * c + 2, :] = second / total
    columns = shares[...].T
    for c in range(spans):
        pair = [held[position[2 * c + i]] for i in range(2)]
        for h in range(width // HD):
            cols = slice(h * HD, (h + 1) * HD)
            part = columns[h * span_len : (h + 1) * span_len]
            total = sum(
                pair[i][:, cols].astype(F32) * part[:, 2 * c + i : 2 * c + i + 1] for i in range(2)
            )
            out[c * span_len : (c + 1) * span_len, cols] = total.astype(BF16)


def combine_context(position, place, pieces, stats, rows):
    groups = len(pieces)
    capacity, span_len, width = pieces[0].shape
    slots, two, lanes = stats[0].shape
    padded = -(-2 * (rows // span_len) // 128) * 128
    return pl.pallas_call(
        functools.partial(combine_context_kernel, groups),
        out_shape=jax.ShapeDtypeStruct((rows, width), BF16),
        in_specs=[smem()] * 2 + [vmem()] * (2 * groups),
        out_specs=vmem(),
        scratch_shapes=[
            pltpu.VMEM((groups * capacity, span_len, width), BF16),
            pltpu.VMEM((groups * slots, two, lanes), F32),
            pltpu.VMEM((padded, lanes), F32),
        ],
        compiler_params=params(24),
        cost_estimate=cost(rows * width * 4, groups * pieces[0].size * 2 + rows * width * 2),
        name="combine_context",
    )(position, place, *pieces, *stats)


def fill_diagonal(dst, block, heads, span_len):
    for h in range(heads):
        side = (h % 2) * HD
        dst[h * span_len : (h + 1) * span_len, side : side + HD] = block[:, h * HD : (h + 1) * HD]


def blocks_of(square, size):
    count = square.shape[0] // size
    return jnp.concatenate(
        [square[i * size : (i + 1) * size, i * size : (i + 1) * size] for i in range(count)], axis=1
    )


def on_diagonal(parts):
    zero = jnp.zeros_like(parts[0])
    return jnp.concatenate(
        [
            jnp.concatenate([part if j == i else zero for j in range(len(parts))], axis=1)
            for i, part in enumerate(parts)
        ],
        axis=0,
    )


def halves(wide, size):
    return [wide[:, i * size : (i + 1) * size] for i in range(wide.shape[1] // size)]


def store_heads(dst, k, both, span_len):
    for h in range(both.shape[0] // span_len):
        rows = slice(h * span_len, (h + 1) * span_len)
        side = (h % 2) * HD
        dst[k, :, h * HD : (h + 1) * HD] = both[rows, side : side + HD].astype(BF16)


def stacked(kv, nbr, first, pairs):
    return kv[nbr, first : first + pairs].reshape(pairs * kv.shape[2], kv.shape[3])


def slot_rows(qg, d, which, span_len):
    return qg[d, pl.ds(pl.multiple_of(which * span_len, span_len), span_len), :]


def safe_inverse(total):
    shrink = jnp.where(total > 2.0**100, 2.0**-64, 1.0)
    scaled = total * shrink
    return shrink, 1.0 / jnp.where(scaled > 0.0, scaled, 1.0)


def quarters(src, dst):
    size = max(1, src.shape[0] // KV_COPIES)
    return [(src.at[pl.ds(i, size)], dst.at[pl.ds(i, size)]) for i in range(0, src.shape[0], size)]


def arrival(held, d, sems):
    return pltpu.make_async_copy(held.at[d], held.at[d], sems.at[d])


def local_kernel(groups, row_len, span_len, *refs):
    qg_refs, refs = refs[:groups], refs[groups:]
    (kv_ref, stats_ref), refs = refs[:2], refs[2:]
    ctx_refs, (counts, nbrs, partner), refs = refs[:groups], refs[groups : groups + 3], refs[groups + 3 :]
    kv, qg, ctx, heads_up, facts, plain, ksem, isem, hsem, osem = refs[:10]
    diag = refs[10:]
    rows, width = qg_refs[0].shape
    heads = width // HD
    capacity = (rows - HEADER) // (2 * span_len)
    slots = groups * capacity
    pairs = heads // 2
    unroll = min(UNROLL, capacity)
    factor = math.log2(math.e) / math.sqrt(HD)
    head_rows = pl.ds(rows - HEADER, HEADER)
    heads_in = fetch(
        [(ref.at[head_rows, pl.ds(0, 128)], heads_up.at[d]) for d, ref in enumerate(qg_refs)], hsem
    )
    kv_in = fetch(quarters(kv_ref, kv), ksem)
    fetch([(qg_refs[0], qg.at[0])], isem)
    ctx_out = [pltpu.make_async_copy(ctx.at[d], ref, osem.at[d]) for d, ref in enumerate(ctx_refs)]
    for copy in heads_in:
        copy.wait()
    facts[...] = heads_up[...].astype(F32).astype(jnp.int32)
    to_scalar = pltpu.make_async_copy(facts, plain, osem.at[groups])
    to_scalar.start()
    for ref in diag:
        ref[...] = jnp.zeros_like(ref)
    to_scalar.wait()

    def unpack(j, carry):
        d, k = j // capacity, j % capacity
        nbrs[j] = plain[d, 0, k]
        partner[j] = plain[d, 1, k] * slots + plain[d, 2, k]
        return carry

    lax.fori_loop(0, slots, unpack, 0)
    for d in range(groups):
        counts[d] = plain[d, 3, 0]
    for copy in kv_in:
        copy.wait()
    fetch([(ref, qg.at[d + 1]) for d, ref in enumerate(qg_refs[1:])], isem.at[pl.ds(1, groups - 1)])

    def one_group(d, carry):
        arrival(qg, d, isem).wait()

        def step(i, carry):
            for u in range(unroll):
                k = jnp.minimum(unroll * i + u, counts[d] - 1)
                j = d * capacity + k
                q_diag, g_diag = diag[2 * u], diag[2 * u + 1]
                fill_diagonal(q_diag, slot_rows(qg, d, 2 * k, span_len), heads, span_len)
                fill_diagonal(g_diag, slot_rows(qg, d, 2 * k + 1, span_len), heads, span_len)
                values = stacked(kv, nbrs[j], pairs, pairs)
                scores = mm(stacked(kv, nbrs[j], 0, pairs), q_diag[...], NT)
                expo = jnp.exp2(blocks_of(scores, row_len) * factor)
                grad_probs = blocks_of(mm(values, g_diag[...], NT), row_len)
                total = jnp.sum(expo, axis=0, keepdims=True)
                shrink, inverse = safe_inverse(total)
                probs = (expo * shrink) * inverse
                stats_ref[j, 0:1, :] = total
                stats_ref[j, 1:2, :] = jnp.sum(probs * grad_probs, axis=0, keepdims=True)
                turned = on_diagonal([x.T for x in halves(probs.astype(BF16), row_len)])
                store_heads(ctx.at[d], k, mm(turned, values, NN), span_len)
            return carry

        lax.fori_loop(0, (counts[d] + unroll - 1) // unroll, step, 0)
        for e in range(groups):

            @pl.when(d == e)
            def _():
                ctx_out[e].start()

        return carry

    lax.fori_loop(0, groups, one_group, 0)
    for copy in ctx_out:
        copy.wait()


def attend_local(qg, kv, row_len, span_len):
    groups = len(qg)
    rows, width = qg[0].shape
    capacity = (rows - HEADER) // (2 * span_len)
    slots = groups * capacity
    lanes = span_len * (width // HD)
    outs = pl.pallas_call(
        functools.partial(local_kernel, groups, row_len, span_len),
        out_shape=[jax.ShapeDtypeStruct((slots, 2, lanes), F32)]
        + [jax.ShapeDtypeStruct((capacity, span_len, width), BF16)] * groups
        + [jax.ShapeDtypeStruct((n,), jnp.int32) for n in (groups, slots, slots)],
        in_specs=[anyspace()] * (groups + 1),
        out_specs=[vmem()] + [anyspace()] * groups + [smem()] * 3,
        scratch_shapes=[
            pltpu.VMEM(kv.shape, BF16),
            pltpu.VMEM((groups, rows, width), BF16),
            pltpu.VMEM((groups, capacity, span_len, width), BF16),
            pltpu.VMEM((groups, HEADER, 128), BF16),
            pltpu.VMEM((groups, HEADER, 128), jnp.int32),
            pltpu.SMEM((groups, HEADER, 128), jnp.int32),
            pltpu.SemaphoreType.DMA((kv.shape[0],)),
            pltpu.SemaphoreType.DMA((groups,)),
            pltpu.SemaphoreType.DMA((groups,)),
            pltpu.SemaphoreType.DMA((groups + 1,)),
        ]
        + [pltpu.VMEM((lanes, 2 * HD), BF16)] * (2 * UNROLL),
        compiler_params=params(62),
        cost_estimate=cost(
            slots * 48 * row_len * lanes * HD,
            kv.size * 2 + slots * span_len * width * 6,
            slots * row_len * lanes,
        ),
        name="attend_local",
    )(*qg, kv)
    return outs[0], outs[1 : groups + 1], outs[groups + 1 :]


def grads_kernel(groups, row_len, span_len, counts, nbrs, partner, *refs):
    qg_refs, stat_refs, refs = refs[:groups], refs[groups : 2 * groups], refs[2 * groups :]
    (kv_ref, kw_ref, vw_ref), refs = refs[:3], refs[3:]
    gq_refs, (dkv_ref, part_ref), refs = refs[:groups], refs[groups : groups + 2], refs[groups + 2 :]
    kv, qg, stats, kw, vw, gq, acc, dkv, part, ksem, qsem, ssem, osem, psem = refs[:14]
    diag = refs[14:]
    width = qg_refs[0].shape[1]
    capacity = gq_refs[0].shape[0]
    heads = width // HD
    scale = 1.0 / math.sqrt(HD)
    pairs = heads // 2
    unroll = min(UNROLL, capacity)
    factor = math.log2(math.e) * scale
    kv_in = fetch(quarters(kv_ref, kv), ksem)
    fetch([(qg_refs[0], qg.at[0])], qsem)
    gq_out = [
        pltpu.make_async_copy(gq.at[d, pl.ds(0, capacity)], ref, osem.at[d])
        for d, ref in enumerate(gq_refs)
    ]
    for ref in diag:
        ref[...] = jnp.zeros_like(ref)
    some = 4 if acc.shape[0] % 4 == 0 else 1
    block = some * row_len
    blocks = acc.shape[0] // some

    def rows_at(i):
        return pl.ds(pl.multiple_of(i * block, block), block)

    def clear(n, carry):
        acc[n] = jnp.zeros(acc.shape[1:], F32)
        return carry

    lax.fori_loop(0, acc.shape[0], clear, 0)
    gather_groups(stat_refs, stats)
    for copy in kv_in:
        copy.wait()
    fetch([(ref, qg.at[d + 1]) for d, ref in enumerate(qg_refs[1:])], qsem.at[pl.ds(1, groups - 1)])
    weights_in = fetch([(kw_ref, kw), (vw_ref, vw)], ssem)

    def one_group(d, carry):
        arrival(qg, d, qsem).wait()

        def step(i, carry):
            for u in range(unroll):
                place = unroll * i + u
                live = place < counts[d]
                k = jnp.minimum(place, counts[d] - 1)
                j = d * capacity + k
                q_diag, g_diag = diag[2 * u], diag[2 * u + 1]
                fill_diagonal(q_diag, slot_rows(qg, d, 2 * k, span_len), heads, span_len)
                fill_diagonal(g_diag, slot_rows(qg, d, 2 * k + 1, span_len), heads, span_len)
                nbr = nbrs[j]
                kept = jnp.where(live, k, capacity)
                own, other = stats[j], stats[partner[j]]
                total = own[0:1] + other[0:1]
                shrink, inverse = safe_inverse(total)
                shift = ((own[0:1] * shrink) * inverse) * own[1:2]
                shift += ((other[0:1] * shrink) * inverse) * other[1:2]
                inverse = jnp.where(live, inverse, 0.0)
                keys = stacked(kv, nbr, 0, pairs)
                expo = jnp.exp2(blocks_of(mm(keys, q_diag[...], NT), row_len) * factor) * shrink
                grad_probs = blocks_of(mm(stacked(kv, nbr, pairs, pairs), g_diag[...], NT), row_len)
                weights = expo * inverse
                mixed = halves((weights * (grad_probs - shift) * scale).astype(BF16), row_len)
                weights = halves(weights.astype(BF16), row_len)
                turned = on_diagonal([x.T for x in mixed])
                store_heads(gq.at[d], kept, mm(turned, keys, NN), span_len)
                shape = (pairs, row_len, 2 * HD)
                acc[nbr, :pairs] += mm(on_diagonal(mixed), q_diag[...], NN).reshape(shape)
                acc[nbr, pairs:] += mm(on_diagonal(weights), g_diag[...], NN).reshape(shape)
            return carry

        lax.fori_loop(0, (counts[d] + unroll - 1) // unroll, step, 0)
        for e in range(groups):

            @pl.when(d == e)
            def _():
                gq_out[e].start()

        return carry

    lax.fori_loop(0, groups, one_group, 0)
    for copy in weights_in:
        copy.wait()

    def results(i):
        b = rows_at(i)
        return (
            pltpu.make_async_copy(part.at[b], part_ref.at[b], psem.at[i, 0]),
            pltpu.make_async_copy(dkv.at[b], dkv_ref.at[b], psem.at[i, 1]),
        )

    def narrow(i, carry):
        b = rows_at(i)
        for p in range(2 * pairs):
            part_of = acc[pl.ds(i * some, some), p].reshape(block, 2 * HD)
            dkv[b, p * 2 * HD : (p + 1) * 2 * HD] = part_of.astype(BF16)
        results(i)[1].start()
        return carry

    def finish(i, carry):
        b = rows_at(i)
        part[b, :] = (mm(dkv[b, :width], kw[...], NN) + mm(dkv[b, width:], vw[...], NN)).astype(BF16)
        results(i)[0].start()
        return carry

    def drain(i, carry):
        for copy in results(i):
            copy.wait()
        return carry

    lax.fori_loop(0, blocks, narrow, 0)
    lax.fori_loop(0, blocks, finish, 0)
    lax.fori_loop(0, blocks, drain, 0)
    for copy in gq_out:
        copy.wait()


def row_blocks(total, size):
    size = size if total % size == 0 else total
    return [pl.ds(i * size, size) for i in range(total // size)]


def attend_grads(lists, qg, stats, kv, key_weight, value_weight, row_len, span_len):
    groups = len(qg)
    width = qg[0].shape[1]
    capacity = (qg[0].shape[0] - HEADER) // (2 * span_len)
    slots = groups * capacity
    lanes = span_len * (width // HD)
    rows = kv.shape[0] * row_len
    feat = key_weight.shape[1]
    outs = pl.pallas_call(
        functools.partial(grads_kernel, groups, row_len, span_len),
        out_shape=[jax.ShapeDtypeStruct((capacity, span_len, width), BF16)] * groups
        + [
            jax.ShapeDtypeStruct((rows, 2 * width), BF16),
            jax.ShapeDtypeStruct((rows, feat), BF16),
        ],
        in_specs=[smem()] * 3 + [anyspace()] * groups + [vmem()] * groups + [anyspace()] * 3,
        out_specs=[anyspace()] * (groups + 2),
        scratch_shapes=[
            pltpu.VMEM(kv.shape, BF16),
            pltpu.VMEM((groups, *qg[0].shape), BF16),
            pltpu.VMEM((groups * slots, 2, lanes), F32),
            pltpu.VMEM((width, feat), BF16),
            pltpu.VMEM((width, feat), BF16),
            pltpu.VMEM((groups, capacity + 1, span_len, width), BF16),
            pltpu.VMEM(kv.shape, F32),
            pltpu.VMEM((rows, 2 * width), BF16),
            pltpu.VMEM((rows, feat), BF16),
            pltpu.SemaphoreType.DMA((kv.shape[0],)),
            pltpu.SemaphoreType.DMA((groups,)),
            pltpu.SemaphoreType.DMA((2,)),
            pltpu.SemaphoreType.DMA((groups,)),
            pltpu.SemaphoreType.DMA((kv.shape[0], 2)),
        ]
        + [pltpu.VMEM((lanes, 2 * HD), BF16)] * (2 * UNROLL),
        compiler_params=params(62),
        cost_estimate=cost(
            4 * rows * feat * width + slots * 72 * row_len * lanes * HD,
            rows * feat * 2 + rows * width * 8 + slots * span_len * width * 6,
            slots * row_len * lanes,
        ),
        name="attend_grads",
    )(*lists, *qg, *stats, kv, key_weight, value_weight)
    return outs[:groups], outs[groups], outs[groups + 1]


def weight_kernel(groups, waits, me, table, dkv, *refs):
    piece_refs, total = refs[waits : waits + groups], refs[-1]
    share = total.shape[1]
    for cols in row_blocks(total.shape[2], 256):
        product = mm(table[...], dkv[:, cols], TN).astype(BF16)
        for e in range(groups):
            total[e, :, cols] = product[e * share : (e + 1) * share]
    for d, piece in enumerate(piece_refs):
        piece[...] = total[jnp.bitwise_xor(me[0], d)]


def grad_weights(me, table, grad_kv, groups, waits):
    feat, columns = table.shape[1], grad_kv.shape[1]
    return pl.pallas_call(
        functools.partial(weight_kernel, groups, len(waits)),
        out_shape=[jax.ShapeDtypeStruct((feat // groups, columns), BF16)] * groups,
        in_specs=[smem(), vmem(), vmem()] + [anyspace()] * len(waits),
        out_specs=[vmem()] * groups,
        scratch_shapes=[pltpu.VMEM((groups, feat // groups, columns), BF16)],
        compiler_params=params(62),
        cost_estimate=cost(WEIGHT_FLOPS, table.size * 2 + grad_kv.size * 2),
        name="grad_weights",
    )(me, table, grad_kv, *waits)


def body(
    queries,
    grad_ctx,
    neighbours,
    up_weight,
    down_weight,
    key_weight,
    value_weight,
    group_ids,
    slot_ids,
):
    groups = lax.axis_size("seq")
    if groups & (groups - 1):
        raise ValueError("seq size")
    me = lax.axis_index("seq").reshape(1)
    span_count = group_ids.shape[0]
    capacity = 2 * span_count // groups + 2
    width = queries.shape[1]
    span_len = queries.shape[0] // span_count
    own_count, row_len, feat = neighbours.shape
    table_len = own_count * lax.axis_size("ret")

    encoded_own = encode(neighbours, up_weight, down_weight)
    table = lax.all_gather(encoded_own, "ret", axis=0, tiled=True).reshape(-1, feat)
    outgoing, position, place = dispatch(
        me, group_ids.T, slot_ids.T, queries, grad_ctx, groups, capacity, span_len, [encoded_own]
    )
    arrived = exchange(outgoing, "seq")
    turned = [key_weight.T, value_weight.T]
    kv = project(table, key_weight, value_weight, row_len, turned)
    own_stats, local_ctx, lists = attend_local(arrived, kv, row_len, span_len)
    stats = exchange([own_stats] * groups, "seq")
    ctx_back = exchange(local_ctx, "seq")
    local_gq, grad_kv, grad_table = attend_grads(
        lists, arrived, stats, kv, *turned, row_len, span_len
    )
    grad_encoded = lax.psum_scatter(
        grad_table.reshape(table_len, row_len, feat), "ret", scatter_dimension=0, tiled=True
    )
    gq_back = exchange(local_gq, "seq")
    pieces = exchange(
        grad_weights(me, table, grad_kv, groups, signs_of(*ctx_back[1:])), "seq"
    )
    grad_weight = sum(piece.astype(F32) for piece in pieces)
    context = combine_context(position, place, ctx_back, stats, queries.shape[0])
    grad_query = combine_grad(position, gq_back, queries.shape[0], [])
    return (context, grad_query, grad_encoded, grad_weight[:, :width], grad_weight[:, width:])


def solution(mesh):
    return jax.shard_map(
        body,
        mesh=mesh,
        in_specs=(
            P("seq", "ret"),
            P("seq", "ret"),
            P(("seq", "ret"), None, None),
            P(),
            P(),
            P(None, "ret"),
            P(None, "ret"),
            P("seq", None),
            P("seq", None),
        ),
        out_specs=(
            P("seq", "ret"),
            P("seq", "ret"),
            P(("seq", "ret"), None, None),
            P("seq", "ret"),
            P("seq", "ret"),
        ),
        check_vma=False,
    )
```
